32 devices in a mesh: dp: 8 (over z, y), tensor: 4 (over x, core).
Axes of the slice: x: 2, y: 2, z: 4, core: 2. Of those that a mesh axis runs over, the one named last changes fastest.
Arguments:
- tokens_in: bfloat16 [16384, 768], P(('dp', 'tensor')), may hold values from -6 to 6
- carried_logits: float32 [16384, 12], P(('dp', 'tensor')), may hold values from -3 to 3
- cotangent: bfloat16 [16384, 768], P(('dp', 'tensor')), may hold values from -6 to 6
- segment_ids: int32 [16384], P('dp'), may hold values from 0 to 12, as said below
- parent_ids: int32 [16384], P('dp'), may hold values from 0 to 4, as said below
- routes: int32 [16384, 2], P('dp'), may hold values from 0 to 11, all different within a row; in each aligned block of 2048 rows (0 to 2047, 2048 to 4095, ...) at most 512 rows name the same one
- attention_gain: float32 [768], replicated, may hold values from 0.5 to 1.5
- head_weight: float32 [3, 768, 768], P(None, 'dp', 'tensor'), may hold values from -0.21875 to 0.21875
- output_weight: float32 [768, 768], P('tensor', 'dp'), may hold values from -2.5 to 2.5
- expert_gain: float32 [768], replicated, may hold values from 0.5 to 1.5
- router_weight: float32 [768, 12], replicated, may hold values from -0.15625 to 0.15625
- carry_weight: float32 [12, 12], replicated, may hold values from -1.25 to 1.25
- constant_gate: float32 [768, 4], replicated, may hold values from -0.21875 to 0.21875
- constant_vector: float32 [2, 768], replicated, may hold values from -6 to 6
- expert_first: float32 [8, 2, 768, 2048], P(None, None, 'dp', 'tensor'), may hold values from -0.21875 to 0.21875
- expert_second: float32 [8, 2048, 768], P(None, 'tensor', 'dp'), may hold values from -0.25 to 0.25
Outputs:
- output: bfloat16 [16384, 768], P(('dp', 'tensor'))
- grad_tokens: float32 [16384, 768], P(('dp', 'tensor'))
- grad_carried: float32 [16384, 12], P(('dp', 'tensor'))
- grad_attention_gain: float32 [768], replicated
- grad_head_weight: float32 [3, 768, 768], P(None, 'dp', 'tensor')
- grad_output_weight: float32 [768, 768], P('tensor', 'dp')
- grad_expert_gain: float32 [768], replicated
- grad_router_weight: float32 [768, 12], replicated
- grad_carry_weight: float32 [12, 12], replicated
- grad_constant_gate: float32 [768, 4], replicated
- grad_constant_vector: float32 [2, 768], replicated
- grad_expert_first: float32 [8, 2, 768, 2048], P(None, None, 'dp', 'tensor')
- grad_expert_second: float32 [8, 2048, 768], P(None, 'tensor', 'dp')
The draws below stay inside these ranges and needn't reach their ends.
Inputs may be any that keep to these rules, and one draw needn't show every extreme that they name: `segment_ids`: in each tree (aligned blocks of 2048 tokens) the segments come in order: 0 is the trunk (the first 768 tokens), 1 to 4 are branches, the rest leaves; every segment holds a token. `parent_ids`: the parent of the trunk and of every branch is 0; each branch is the parent of two leaves. `routes`: A token's two experts differ; in each tree no expert is named by more than 512 tokens, a bound that some block reaches.
All inputs are finite; a program needn't handle non-finite values.
Results may differ from the reference program's by a relative error of at most 0.017.
Values may be sent and summed in bfloat16 or wider, within the bound.
A program may use at most 256 MiB of HBM per device.

```python
import math
from functools import partial
import jax
import jax.numpy as jnp
import numpy as np
from jax import lax

D = 768
HEADS = 12
HEAD = 64
FF = 2048
NF = 8
BRANCH = 4
NSEG = 13
NE = 12
TREE = 2048
TRUNK = 768
CAP = 512
TOKENS = 16384


def tree_layout(key):
    tree_count = TOKENS // TREE
    remaining = TREE - TRUNK

    def single_tree(tree_key):
        cut_key, leaf_key = jax.random.split(tree_key)
        cut_points = jnp.sort(jax.random.permutation(cut_key, remaining - 1)[:NSEG - 2] + 1).astype(jnp.int32)
        bounds = jnp.concatenate([jnp.zeros((1,), jnp.int32), cut_points, jnp.full((1,), remaining, jnp.int32)]) + TRUNK
        position_index = jnp.arange(TREE, dtype=jnp.int32)
        segment = jnp.sum((position_index[:, None] >= bounds[None, :-1]).astype(jnp.int32), axis=1).astype(jnp.int32)
        leaves = (1 + jax.random.permutation(leaf_key, 2 * BRANCH) // 2).astype(jnp.int32)
        parent_table = jnp.concatenate([jnp.zeros((BRANCH + 1,), jnp.int32), leaves])
        labels = jnp.arange(NSEG, dtype=jnp.int32)
        parent = jnp.sum((segment[:, None] == labels[None, :]).astype(jnp.int32) * parent_table[None, :], axis=1).astype(jnp.int32)
        return (segment, parent)
    tree_keys = jax.random.split(key, tree_count)
    return jax.vmap(single_tree)(tree_keys)


def draw_segment_ids(key, part):
    segment, parent = tree_layout(key)
    return segment.reshape(-1)


def draw_parent_ids(key, part):
    segment, parent = tree_layout(key)
    return parent.reshape(-1)


def steps_of(rng, shape, cuts, smallest, top_value):
    factor_of = 1.0
    for axis_at, shards_of in cuts:
        draws = jax.random.uniform(jax.random.fold_in(jax.random.fold_in(rng, 6), axis_at), (shards_of,), jnp.float32, smallest / len(cuts), top_value / len(cuts))
        factor_of = factor_of * jnp.repeat(jnp.exp(draws), shape[axis_at] // shards_of).reshape((-1,) + (1,) * (len(shape) - 1 - axis_at))
    return factor_of


def routed_block(rng, own, number, rows, count, top, limit, lean):
    sequence = jax.random.permutation(rng, count)
    heavy_load, common = portions_of(count, rows * top, limit, lean, True), portions_of(count, rows * top, limit, lean, False)
    places = jnp.arange(count)

    def named(sizes, rotation):
        used = int((sizes > 0).sum())
        fixed = max(1, used // 4)
        moved = fixed + (places - fixed + rotation * (used - fixed)) % max(1, count - fixed)
        return jnp.zeros((count,), jnp.int32).at[sequence[jnp.where(places < fixed, places, moved)]].set(jnp.asarray(sizes, jnp.int32))

    sizes = jnp.where(number % 4 == 0, named(heavy_load, number // 4), named(common, number - number // 4 - 1))
    mixed = jax.random.permutation(jax.random.fold_in(own, 3), count)
    source_of, taker = mixed[0:count // 2 * 2:2], mixed[1:count // 2 * 2:2]
    slack = jnp.minimum(sizes[source_of] - 1, limit - sizes[taker]) // 2
    slack = jnp.where((source_of == sequence[0]) | (taker == sequence[0]) | (sizes[taker] == 0), 0, jnp.maximum(slack, 0))
    moved = jax.random.randint(jax.random.fold_in(own, 4), (count // 2,), 0, 1 << 20) % (slack + 1)
    sizes = sizes.at[source_of].add(-moved).at[taker].add(moved)
    items = jnp.searchsorted(jnp.cumsum(sizes), jnp.arange(rows * top), side="right").astype(jnp.int32)
    table = items.reshape(top, rows).T
    table = table[jax.random.permutation(jax.random.fold_in(own, 1), rows)]
    rotation = jax.random.randint(jax.random.fold_in(own, 2), (rows, 1), 0, top)
    return jnp.take_along_axis(table, (jnp.arange(top)[None, :] + rotation) % top, axis=1)


def portions_of(amount, total, limit, slope, full):
    portions = [(1 << 20) // math.isqrt(grade ** slope) + 1 for grade in range(1, amount + 1)]
    largest = limit if full else min(limit, max(-(-total // amount), total * portions[0] // sum(portions)))
    least = 1 if total - largest >= amount - 1 else 0
    holding, spare = [largest] + [least] * (amount - 1), total - largest - least * (amount - 1)
    while spare > 0:
        candidates = [i for i in range(1, amount) if holding[i] < largest] or [i for i in range(1, amount) if holding[i] < limit]
        mass, left = sum([portions[i] for i in candidates]), spare
        for i in candidates:
            addition = min(limit - holding[i], max(1, left * portions[i] // mass), spare)
            holding[i] = holding[i] + addition
            spare = spare - addition
    return np.array(holding)


def gaussian(own_key, shape, scale, limit, shards=(), held_as=jnp.bfloat16):
    level = steps_of(own_key, shape, shards, -0.22, 0.18) if shards else 1.0
    entries = jax.random.normal(own_key, shape, jnp.float32) * scale * level
    return jnp.minimum(jnp.maximum(entries, -limit), limit).astype(held_as)


def setup_inputs(seed: int = 0) -> dict:
    keys = jax.random.split(jax.random.key(seed), 17)
    tokens_in = gaussian(keys[0], (TOKENS, D), 1.0, 6.0, ((0, 32),))
    carried_logits = gaussian(keys[1], (TOKENS, NE), 0.5, 3.0, ((0, 32),), jnp.float32)
    cotangent = gaussian(keys[2], (TOKENS, D), 1.0, 6.0, ((0, 32),))
    segment_ids = draw_segment_ids(jax.random.fold_in(keys[16], 71), 0)
    parent_ids = draw_parent_ids(jax.random.fold_in(keys[16], 71), 0)
    routes_keys = jax.random.split(jax.random.fold_in(keys[5], 1), TOKENS // TREE)
    routes_turns = jax.random.permutation(jax.random.fold_in(keys[5], 3), TOKENS // TREE)
    routes = jax.vmap(lambda own, number: routed_block(jax.random.fold_in(keys[5], 2), own, number, TREE, NE, 2, CAP, 1))(routes_keys, routes_turns).reshape((TOKENS, 2))
    attention_gain = jnp.clip(1.0 + 0.1 * jax.random.normal(keys[6], (D,), jnp.float32), 0.5, 1.5)
    head_weight = gaussian(keys[7], (3, D, HEADS * HEAD), D ** -0.5, 0.21875, ((1, 8), (2, 4)), jnp.float32)
    output_weight = gaussian(keys[8], (HEADS * HEAD, D), (max(1, HEADS * HEAD * 16 // TREE)) ** -0.5, 2.5, ((0, 4), (1, 8)), jnp.float32)
    expert_gain = jnp.clip(1.0 + 0.1 * jax.random.normal(keys[9], (D,), jnp.float32), 0.5, 1.5)
    router_weight = gaussian(keys[10], (D, NE), (2 * D) ** -0.5, 0.15625, (), jnp.float32)
    carry_weight = gaussian(keys[11], (NE, NE), (2 * NE) ** -0.5, 1.25, (), jnp.float32)
    constant_gate = gaussian(keys[12], (D, 4), D ** -0.5, 0.21875, (), jnp.float32)
    constant_vector = gaussian(keys[13], (2, D), 1.0, 6.0, (), jnp.float32)
    expert_first = gaussian(keys[14], (NF, 2, D, FF), D ** -0.5, 0.21875, ((2, 8), (3, 4)), jnp.float32)
    expert_second = gaussian(keys[15], (NF, FF, D), (FF // 4) ** -0.5, 0.25, ((1, 4), (2, 8)), jnp.float32)
    return {"tokens_in": tokens_in, "carried_logits": carried_logits, "cotangent": cotangent, "segment_ids": segment_ids, "parent_ids": parent_ids, "routes": routes, "attention_gain": attention_gain, "head_weight": head_weight, "output_weight": output_weight, "expert_gain": expert_gain, "router_weight": router_weight, "carry_weight": carry_weight, "constant_gate": constant_gate, "constant_vector": constant_vector, "expert_first": expert_first, "expert_second": expert_second}


epsilon = 1e-06
HIGHEST = lax.Precision.HIGHEST

@jax.custom_vjp
def low(v):
    return lax.optimization_barrier(v.astype(jnp.bfloat16)).astype(jnp.float32)

@jax.custom_vjp
def low_back(v):
    return v

def low_keep(v):
    return (low(v), None)

def low_pass(kept, grad):
    return (grad,)

def back_keep(v):
    return (v, None)

def back_low(kept, grad):
    return (low(grad),)
low.defvjp(low_keep, low_pass)
low_back.defvjp(back_keep, back_low)

def normed(values, gain_vector):
    return values * lax.rsqrt(lax.optimization_barrier(jnp.mean(values * values, axis=-1, keepdims=True)) + epsilon) * gain_vector

def tree_positions(segment, parent):
    token_count = segment.shape[0]
    labels = jnp.arange(NSEG, dtype=jnp.int32)
    own_hot = (segment[:, None] == labels[None, :]).astype(jnp.int32)
    parent_hot = (parent[:, None] == labels[None, :]).astype(jnp.int32)
    lengths = lax.optimization_barrier(jnp.sum(own_hot, axis=0)).astype(jnp.int32)
    starts = (jnp.cumsum(lengths) - lengths).astype(jnp.int32)
    own_start = lax.optimization_barrier(jnp.sum(own_hot * starts[None, :], axis=1)).astype(jnp.int32)
    parent_length = lax.optimization_barrier(jnp.sum(parent_hot * lengths[None, :], axis=1)).astype(jnp.int32)
    position_index = jnp.arange(token_count, dtype=jnp.int32)
    shifted = position_index - own_start + jnp.where(segment > 0, lengths[0], 0) + jnp.where(parent > 0, parent_length, 0)
    return shifted.astype(jnp.int32)

def rotary_tables(segment, parent):
    angle_rate = 10000.0 ** (-2.0 * jnp.arange(HEAD // 2, dtype=jnp.float32) / HEAD)
    angles = tree_positions(segment, parent).astype(jnp.float32)[:, None] * angle_rate[None, :]
    return (jnp.cos(angles)[:, None, :], jnp.sin(angles)[:, None, :])

def rotary(values, cosine, sine_part):
    half_size = values.shape[-1] // 2
    first_half = values[..., :half_size]
    second_half = values[..., half_size:]
    return jnp.concatenate([first_half * cosine - second_half * sine_part, second_half * cosine + first_half * sine_part], axis=-1)

def visibility(row_index, row_segment, row_parent, segment):
    columns = jnp.arange(segment.shape[0], dtype=jnp.int32)
    related = (segment[None, :] == row_segment[:, None]) | (segment[None, :] == row_parent[:, None]) | (segment[None, :] == 0)
    return (columns[None, :] <= row_index[:, None]) & related

def router_local(hidden, gain_vector, carried, router_weight, carry_weight, constant_gate, constant_vector, routes):
    normed_two = normed(hidden, gain_vector)
    logits = jnp.dot(normed_two, router_weight, precision=HIGHEST) + jnp.dot(carried, carry_weight, precision=HIGHEST)
    picked = (routes[:, :, None] == jnp.arange(NE, dtype=jnp.int32)[None, None, :]).astype(jnp.float32)
    chosen = jnp.einsum('tkn,tn->tk', picked, logits, precision=HIGHEST)
    gate_values = jax.nn.softmax(chosen, axis=-1)
    mixture = jax.nn.softmax(jnp.dot(normed_two, constant_gate, precision=HIGHEST).reshape(-1, 2, 2), axis=-1)
    copy_weight = lax.optimization_barrier(jnp.sum(gate_values * (routes == NF + 1).astype(jnp.float32), axis=1))
    first_weight = lax.optimization_barrier(jnp.sum(gate_values * (routes == NF + 2).astype(jnp.float32), axis=1))
    second_weight = lax.optimization_barrier(jnp.sum(gate_values * (routes == NF + 3).astype(jnp.float32), axis=1))
    local_sum = copy_weight[:, None] * normed_two
    local_sum = local_sum + first_weight[:, None] * (mixture[:, 0, 0:1] * normed_two + mixture[:, 0, 1:2] * constant_vector[0][None, :])
    local_sum = local_sum + second_weight[:, None] * (mixture[:, 1, 0:1] * normed_two + mixture[:, 1, 1:2] * constant_vector[1][None, :])
    expert_gates = gate_values * (routes < NF).astype(jnp.float32)
    return (normed_two, expert_gates, local_sum)

def dispatch(routes, capacity):
    flat_routes = routes.reshape(-1)
    one_hot = (flat_routes[:, None] == jnp.arange(NE, dtype=jnp.int32)[None, :]).astype(jnp.int32)
    before = jnp.cumsum(one_hot, axis=0) - one_hot
    slot_index = lax.optimization_barrier(jnp.sum(before * one_hot, axis=1)).astype(jnp.int32)
    slot_place = jnp.where(flat_routes < NF, flat_routes * capacity + slot_index, NF * capacity).astype(jnp.int32)
    anchor = jnp.arange(flat_routes.shape[0], dtype=jnp.int32)
    return jnp.full((NF * capacity,), flat_routes.shape[0], jnp.int32).at[slot_place].set(anchor, mode='drop')

def experts_ffn(expert_input, expert_gates, routes, expert_first, expert_second):
    token_count = expert_input.shape[0]
    source = dispatch(routes, CAP)
    filled = source < 2 * token_count
    token_index = jnp.where(filled, source // 2, 0).astype(jnp.int32)
    safe_source = jnp.minimum(source, 2 * token_count - 1).astype(jnp.int32)
    slot_gate = jnp.where(filled, expert_gates.reshape(-1)[safe_source], 0.0)
    expert_rows = expert_input[token_index].reshape(NF, CAP, expert_input.shape[1])
    inner_out = low_back(jnp.einsum('ecd,esdf->escf', expert_rows, expert_first, precision=HIGHEST))
    activated = low(jax.nn.silu(inner_out[:, 0]) * inner_out[:, 1])
    expert_out = low_back(jnp.einsum('ecf,efd->ecd', activated, expert_second, precision=HIGHEST))
    weighted = expert_out.reshape(NF * CAP, -1) * slot_gate[:, None]
    return jnp.zeros(expert_input.shape, jnp.float32).at[token_index].add(weighted)

def attend(queries, keys_all, values_all, segment, parent):
    token_count = queries.shape[0]
    block_rows = min(512, token_count)
    block_count = token_count // block_rows
    score_scale = HEAD ** (-0.5)
    row_index = jnp.arange(token_count, dtype=jnp.int32).reshape(block_count, block_rows)

    def single_block(block_args):
        query_block, index_block, segment_block, parent_block = block_args
        scores = low_back(jnp.einsum('qhe,khe->hqk', query_block, keys_all, precision=HIGHEST) * score_scale)
        visible = visibility(index_block, segment_block, parent_block, segment)
        probs_low = low(jax.nn.softmax(jnp.where(visible[None], scores, -1e+30), axis=-1))
        return jnp.einsum('hqk,khe->qhe', probs_low, values_all, precision=HIGHEST)
    mixed_out = lax.map(jax.checkpoint(single_block), (queries.reshape(block_count, block_rows, HEADS, HEAD), row_index, segment.reshape(block_count, block_rows), parent.reshape(block_count, block_rows)))
    return mixed_out.reshape(token_count, HEADS, HEAD)

def tree_forward(weights, tree_args):
    attention_gain, head_weight, output_weight, expert_gain, router_weight, carry_weight, constant_gate, constant_vector, expert_first, expert_second = weights
    tokens, carried, segment, parent, routes = tree_args
    token_count = tokens.shape[0]
    normed_one = low(normed(tokens, attention_gain))
    projected = low_back(jnp.einsum('td,sdf->stf', normed_one, head_weight, precision=HIGHEST))
    cosine, sine_part = rotary_tables(segment, parent)
    queries = low(rotary(projected[0].reshape(token_count, HEADS, HEAD), cosine, sine_part))
    keys_all = low(rotary(projected[1].reshape(token_count, HEADS, HEAD), cosine, sine_part))
    values_all = low(projected[2].reshape(token_count, HEADS, HEAD))
    attended = attend(queries, keys_all, values_all, segment, parent).reshape(token_count, HEADS * HEAD)
    attended = low(low_back(attended))
    hidden = tokens + low_back(jnp.dot(attended, output_weight, precision=HIGHEST))
    normed_two, expert_gates, local_sum = router_local(hidden, expert_gain, carried, router_weight, carry_weight, constant_gate, constant_vector, routes)
    expert_sum = experts_ffn(low(normed_two), low(expert_gates), routes, expert_first, expert_second)
    return hidden + local_sum + expert_sum

def reference(tokens_in, carried_logits, cotangent, segment_ids, parent_ids, routes, attention_gain, head_weight, output_weight, expert_gain, router_weight, carry_weight, constant_gate, constant_vector, expert_first, expert_second):
    tree_count = segment_ids.shape[0] // TREE

    def forward(tokens, carried, weights):
        rounded = (weights[0], low(weights[1]), low(weights[2]), weights[3], weights[4], weights[5], weights[6], weights[7], low(weights[8]), low(weights[9]))
        tree_args = (tokens.reshape(tree_count, TREE, D), carried.reshape(tree_count, TREE, NE), segment_ids.reshape(tree_count, TREE), parent_ids.reshape(tree_count, TREE), routes.reshape(tree_count, TREE, 2))
        results = lax.map(jax.checkpoint(partial(tree_forward, rounded)), tree_args)
        return results.reshape(tree_count * TREE, D)
    weights = (attention_gain, head_weight, output_weight, expert_gain, router_weight, carry_weight, constant_gate, constant_vector, expert_first, expert_second)
    result, pull_back = jax.vjp(forward, tokens_in.astype(jnp.float32), carried_logits, weights)
    grad_tokens, grad_carried, grad_weights = pull_back(cotangent.astype(jnp.float32))
    return (result.astype(jnp.bfloat16), grad_tokens, grad_carried, grad_weights[0], grad_weights[1], grad_weights[2], grad_weights[3], grad_weights[4], grad_weights[5], grad_weights[6], grad_weights[7], grad_weights[8], grad_weights[9])
```

```python
import functools

import jax
import jax.numpy as jnp
from jax import lax
from jax.experimental import pallas as pl
from jax.experimental.pallas import tpu as pltpu
from jax.sharding import PartitionSpec as P

HEAD = 64
NF = 8
NSEG = 13
NE = 12
PAD = 256
BLOCK = 256
TILE = 256
GROUPS = 4

epsilon = 1e-06
HIGHEST = lax.Precision.HIGHEST
F32 = jnp.float32
BF16 = jnp.bfloat16


def dot_nn(a, b):
    return lax.dot_general(a, b, (((1,), (0,)), ((), ())), preferred_element_type=F32)


def dot_nt(a, b):
    return lax.dot_general(a, b, (((1,), (1,)), ((), ())), preferred_element_type=F32)


def dot_tn(a, b):
    return lax.dot_general(a, b, (((0,), (0,)), ((), ())), preferred_element_type=F32)


def normed(values, gain_vector):
    return (
        values
        * lax.rsqrt(jnp.mean(values * values, axis=-1, keepdims=True) + epsilon)
        * gain_vector
    )


def tree_positions(segment, parent):
    token_count = segment.shape[0]
    labels = jnp.arange(NSEG, dtype=jnp.int32)
    own_hot = (segment[:, None] == labels[None, :]).astype(jnp.int32)
    parent_hot = (parent[:, None] == labels[None, :]).astype(jnp.int32)
    lengths = jnp.sum(own_hot, axis=0)
    starts = jnp.cumsum(lengths) - lengths
    own_start = jnp.sum(own_hot * starts[None, :], axis=1)
    parent_length = jnp.sum(parent_hot * lengths[None, :], axis=1)
    position_index = jnp.arange(token_count, dtype=jnp.int32)
    return (
        position_index
        - own_start
        + jnp.where(segment > 0, lengths[0], 0)
        + jnp.where(parent > 0, parent_length, 0)
    )


def rotary_tables(segment, parent):
    angle_rate = 10000.0 ** (-2.0 * jnp.arange(HEAD // 2, dtype=F32) / HEAD)
    angles = tree_positions(segment, parent).astype(F32)[:, None] * angle_rate[None, :]
    cosine, sine = jnp.cos(angles), jnp.sin(angles)
    copies = PAD // HEAD
    cos_table = jnp.tile(jnp.concatenate([cosine, cosine], axis=1), (1, copies))
    sin_table = jnp.tile(jnp.concatenate([-sine, sine], axis=1), (1, copies))
    return cos_table, sin_table


def router_local(
    hidden, gain_vector, carried, router_weight, carry_weight, constant_gate, constant_vector, routes
):
    normed_two = normed(hidden, gain_vector)
    logits = jnp.dot(normed_two, router_weight, precision=HIGHEST) + jnp.dot(
        carried, carry_weight, precision=HIGHEST
    )
    picked = (routes[:, :, None] == jnp.arange(NE, dtype=jnp.int32)[None, None, :]).astype(F32)
    chosen = jnp.sum(picked * logits[:, None, :], axis=-1)
    gate_values = jax.nn.softmax(chosen, axis=-1)
    by_expert = jnp.sum(picked * gate_values[:, :, None], axis=1)
    mixture = jax.nn.softmax(
        jnp.dot(normed_two, constant_gate, precision=HIGHEST).reshape(-1, 2, 2), axis=-1
    )
    copy_weight = by_expert[:, NF + 1]
    first_weight = by_expert[:, NF + 2]
    second_weight = by_expert[:, NF + 3]
    local_sum = copy_weight[:, None] * normed_two
    local_sum = local_sum + first_weight[:, None] * (
        mixture[:, 0, 0:1] * normed_two + mixture[:, 0, 1:2] * constant_vector[0][None, :]
    )
    local_sum = local_sum + second_weight[:, None] * (
        mixture[:, 1, 0:1] * normed_two + mixture[:, 1, 1:2] * constant_vector[1][None, :]
    )
    return (normed_two, by_expert[:, :NF], local_sum)


def swap(values, axis, bits):
    size = lax.axis_size(axis)
    return lax.ppermute(values, axis, [(i, i ^ bits) for i in range(size)])


def gather_tensor(own):
    index = lax.axis_index("tensor")
    far = swap(own, "tensor", 2)
    near = swap(own, "tensor", 1)
    far_near = swap(far, "tensor", 1)
    core, chip = index % 2 == 0, index // 2 == 0
    here = [jnp.where(core, own, near), jnp.where(core, near, own)]
    there = [jnp.where(core, far, far_near), jnp.where(core, far_near, far)]
    order = [jnp.where(chip, h, t) for h, t in zip(here, there)]
    order += [jnp.where(chip, t, h) for h, t in zip(here, there)]
    return jnp.concatenate(order, axis=0)


def scatter_tensor(parts, rows):
    index = lax.axis_index("tensor")

    def take(which):
        return lax.dynamic_slice_in_dim(parts, which * rows, rows, 0).astype(F32)

    near = swap(
        jnp.concatenate([take(index ^ 1), take(index ^ 3)], axis=0).astype(BF16), "tensor", 1
    ).astype(F32)
    mine = take(index) + near[:rows]
    other = take(index ^ 2) + near[rows:]
    return mine + swap(other.astype(BF16), "tensor", 2).astype(F32)


def pieces_of(own, axis):
    if lax.axis_size("dp") != 8:
        return [lax.all_gather(own, "dp", axis=axis, tiled=True)]
    column = [own, swap(own, "dp", 2), swap(own, "dp", 4), swap(own, "dp", 6)]
    pieces = []
    for shard in column:
        pieces += [shard, swap(shard, "dp", 1)]
    return pieces


def sum_pieces(mine, theirs):
    paired = mine.astype(F32) + swap(theirs, "dp", 1).astype(F32)
    total = paired[0]
    for j in range(1, 4):
        total = total + swap(paired[j].astype(BF16), "dp", 2 * j).astype(F32)
    return total


def sum_all(values):
    if lax.axis_size("dp") != 8:
        return lax.psum(values, ("dp", "tensor"))
    for axis, bits in (("tensor", 1), ("tensor", 2), ("dp", 1), ("dp", 2), ("dp", 4)):
        values = values + swap(values, axis, bits)
    return values


def swap_halves(values):
    lane = lax.broadcasted_iota(jnp.int32, values.shape, 1)
    half = HEAD // 2
    return jnp.where(
        lane % HEAD < half, pltpu.roll(values, PAD - half, 1), pltpu.roll(values, half, 1)
    )


def project_kernel(n_ref, w_ref, c_ref, s_ref, q_ref, k_ref, v_ref, kt_ref, vt_ref):
    rows = n_ref[...]
    cosine, sine = c_ref[...], s_ref[...]
    part = dot_nn(rows, w_ref[:, :PAD])
    q_ref[...] = ((part * cosine + swap_halves(part) * sine) * HEAD**-0.5).astype(BF16)
    part = dot_nn(rows, w_ref[:, PAD : 2 * PAD])
    keys = part * cosine + swap_halves(part) * sine
    k_ref[...] = keys.astype(BF16)
    kt_ref[...] = keys.T.astype(BF16)
    values = dot_nn(rows, w_ref[:, 2 * PAD : 3 * PAD])
    v_ref[...] = values.astype(BF16)
    vt_ref[...] = values.T.astype(BF16)


def project(gathered, weights, cos_table, sin_table):
    rows, width = gathered.shape
    grid = (rows // BLOCK,)
    row_spec = pl.BlockSpec((BLOCK, PAD), lambda i: (i, 0))
    column_spec = pl.BlockSpec((PAD, BLOCK), lambda i: (0, i))
    wide = jax.ShapeDtypeStruct((rows, PAD), BF16)
    tall = jax.ShapeDtypeStruct((PAD, rows), BF16)
    return pl.pallas_call(
        project_kernel,
        grid=grid,
        in_specs=[
            pl.BlockSpec((BLOCK, width), lambda i: (i, 0)),
            pl.BlockSpec(weights.shape, lambda i: (0, 0)),
            row_spec,
            row_spec,
        ],
        out_specs=[row_spec, row_spec, row_spec, column_spec, column_spec],
        out_shape=[wide, wide, wide, tall, tall],
        cost_estimate=pl.CostEstimate(
            flops=2 * rows * width * 3 * PAD, bytes_accessed=8 * rows * width, transcendentals=0
        ),
    )(gathered, weights, cos_table, sin_table)


def head_mask(values, head):
    lane = lax.broadcasted_iota(jnp.int32, values.shape, 1)
    return jnp.where(lane // HEAD == head, values, jnp.zeros_like(values))


def seen(i, j, seg_row, par_row, seg_col):
    key_at = j * BLOCK + lax.broadcasted_iota(jnp.int32, (BLOCK, 1), 0)
    query_at = i * BLOCK + lax.broadcasted_iota(jnp.int32, (1, BLOCK), 1)
    related = (seg_col == seg_row) | (seg_col == par_row) | (seg_col == 0)
    return related & (key_at <= query_at)


def attend_kernel(heads, q_ref, k_ref, vt_ref, rowinfo_ref, colinfo_ref, o_ref, total_ref):
    i = pl.program_id(0)
    queries = q_ref[...]
    by_head = [head_mask(queries, h) for h in range(heads)]
    seg_row, par_row = rowinfo_ref[0:1, :], rowinfo_ref[1:2, :]

    def step(j, carry):
        at = pl.ds(pl.multiple_of(j * BLOCK, BLOCK), BLOCK)
        keys = k_ref[at, :]
        visible = seen(i, j, seg_row, par_row, colinfo_ref[at, 0:1])
        out = []
        for h in range(heads):
            top, total, mixed = carry[h]
            scores = jnp.where(visible, dot_nt(keys, by_head[h]), -1e30)
            new_top = jnp.maximum(top, jnp.max(scores, axis=0, keepdims=True))
            shrink = jnp.exp(top - new_top)
            probs = jnp.exp(scores - new_top)
            total = total * shrink + jnp.sum(probs, axis=0, keepdims=True)
            mixed = mixed * shrink + dot_nn(
                vt_ref[h * HEAD : (h + 1) * HEAD, at], probs.astype(BF16)
            )
            out.append((new_top, total, mixed))
        return tuple(out)

    start = tuple(
        (
            jnp.full((1, BLOCK), -1e30, F32),
            jnp.zeros((1, BLOCK), F32),
            jnp.zeros((HEAD, BLOCK), F32),
        )
        for _ in range(heads)
    )
    done = lax.fori_loop(0, i + 1, step, start)
    mixed = [m / t for _, t, m in done] + [jnp.zeros((PAD - heads * HEAD, BLOCK), F32)]
    o_ref[...] = jnp.concatenate(mixed, axis=0).T.astype(BF16)
    total_ref[...] = jnp.concatenate(
        [m + jnp.log(t) for m, t, _ in done] + [jnp.zeros((8 - heads, BLOCK), F32)], axis=0
    )


def attend(heads, queries, keys, values_t, rowinfo, colinfo):
    rows = queries.shape[0]
    whole = lambda a: pl.BlockSpec(a.shape, lambda i: (0,) * a.ndim)
    return pl.pallas_call(
        functools.partial(attend_kernel, heads),
        grid=(rows // BLOCK,),
        in_specs=[
            pl.BlockSpec((BLOCK, PAD), lambda i: (i, 0)),
            whole(keys),
            whole(values_t),
            pl.BlockSpec((8, BLOCK), lambda i: (0, i)),
            whole(colinfo),
        ],
        out_specs=[
            pl.BlockSpec((BLOCK, PAD), lambda i: (i, 0)),
            pl.BlockSpec((8, BLOCK), lambda i: (0, i)),
        ],
        out_shape=[
            jax.ShapeDtypeStruct((rows, PAD), BF16),
            jax.ShapeDtypeStruct((8, rows), F32),
        ],
        compiler_params=pltpu.CompilerParams(vmem_limit_bytes=32 << 20),
        cost_estimate=pl.CostEstimate(
            flops=heads * rows * rows * 512, bytes_accessed=8 * rows * PAD, transcendentals=0
        ),
    )(queries, keys, values_t, rowinfo, colinfo)


def attend_back_kernel(
    heads,
    q_ref,
    g_ref,
    o_ref,
    k_ref,
    v_ref,
    kt_ref,
    rowinfo_ref,
    colinfo_ref,
    total_ref,
    c_ref,
    s_ref,
    gq_ref,
    gk_ref,
    gv_ref,
    key_sum,
    value_sum,
    query_sum,
):
    i = pl.program_id(0)
    here = pl.ds(pl.multiple_of(i * BLOCK, BLOCK), BLOCK)

    @pl.when(i == 0)
    def _():
        key_sum[...] = jnp.zeros_like(key_sum)
        value_sum[...] = jnp.zeros_like(value_sum)

    query_sum[...] = jnp.zeros_like(query_sum)
    queries, grads = q_ref[...], g_ref[...]
    q_heads = [head_mask(queries, h) for h in range(heads)]
    g_heads = [head_mask(grads, h) for h in range(heads)]
    seg_row, par_row = rowinfo_ref[0:1, :], rowinfo_ref[1:2, :]
    product = grads.astype(F32) * o_ref[...].astype(F32)
    lane = lax.broadcasted_iota(jnp.int32, (8, PAD), 1)
    which = lax.broadcasted_iota(jnp.int32, (8, PAD), 0)
    delta = lax.dot_general(
        (lane // HEAD == which).astype(F32),
        product,
        (((1,), (1,)), ((), ())),
        precision=HIGHEST,
        preferred_element_type=F32,
    )
    totals = total_ref[...]

    def step(j, carry):
        at = pl.ds(pl.multiple_of(j * BLOCK, BLOCK), BLOCK)
        keys, values = k_ref[at, :], v_ref[at, :]
        visible = seen(i, j, seg_row, par_row, colinfo_ref[at, 0:1])
        key_part, value_part = key_sum[at, :], value_sum[at, :]
        for h in range(heads):
            scores = jnp.where(visible, dot_nt(keys, q_heads[h]), -1e30)
            probs = jnp.exp(scores - totals[h : h + 1, :])
            value_part = value_part + dot_nn(probs.astype(BF16), g_heads[h])
            grad_probs = dot_nt(values, g_heads[h])
            grad_scores = (probs * (grad_probs - delta[h : h + 1, :])).astype(BF16)
            key_part = key_part + dot_nn(grad_scores, q_heads[h])
            lanes = slice(h * HEAD, (h + 1) * HEAD)
            query_sum[lanes, :] += dot_nn(kt_ref[lanes, at], grad_scores)
        key_sum[at, :] = key_part
        value_sum[at, :] = value_part
        return carry

    lax.fori_loop(0, i + 1, step, 0)
    grad_q = query_sum[...].T * HEAD**-0.5
    cosine, sine = c_ref[here, :], s_ref[here, :]
    gq_ref[...] = (grad_q * cosine - swap_halves(grad_q) * sine).astype(BF16)

    @pl.when(i == pl.num_programs(0) - 1)
    def _():
        def finish(j, carry):
            at = pl.ds(pl.multiple_of(j * BLOCK, BLOCK), BLOCK)
            grad_k = key_sum[at, :]
            gk_ref[at, :] = (grad_k * c_ref[at, :] - swap_halves(grad_k) * s_ref[at, :]).astype(BF16)
            gv_ref[at, :] = value_sum[at, :].astype(BF16)
            return carry

        lax.fori_loop(0, pl.num_programs(0), finish, 0)


def attend_back(heads, queries, grads, out, keys, values, keys_t, rowinfo, colinfo, totals, cos_table, sin_table):
    rows = queries.shape[0]
    whole = lambda a: pl.BlockSpec(a.shape, lambda i: (0,) * a.ndim)
    row_spec = pl.BlockSpec((BLOCK, PAD), lambda i: (i, 0))
    wide = jax.ShapeDtypeStruct((rows, PAD), BF16)
    return pl.pallas_call(
        functools.partial(attend_back_kernel, heads),
        grid=(rows // BLOCK,),
        in_specs=[
            row_spec,
            row_spec,
            row_spec,
            whole(keys),
            whole(values),
            whole(keys_t),
            pl.BlockSpec((8, BLOCK), lambda i: (0, i)),
            whole(colinfo),
            pl.BlockSpec((8, BLOCK), lambda i: (0, i)),
            whole(cos_table),
            whole(sin_table),
        ],
        out_specs=[
            row_spec,
            pl.BlockSpec((rows, PAD), lambda i: (0, 0)),
            pl.BlockSpec((rows, PAD), lambda i: (0, 0)),
        ],
        out_shape=[wide, wide, wide],
        scratch_shapes=[
            pltpu.VMEM((rows, PAD), F32),
            pltpu.VMEM((rows, PAD), F32),
            pltpu.VMEM((PAD, BLOCK), F32),
        ],
        compiler_params=pltpu.CompilerParams(vmem_limit_bytes=40 << 20),
        cost_estimate=pl.CostEstimate(
            flops=heads * rows * rows * 1280, bytes_accessed=16 * rows * PAD, transcendentals=0
        ),
    )(queries, grads, out, keys, values, keys_t, rowinfo, colinfo, totals, cos_table, sin_table)


def experts_kernel(
    first, n_in, n_out, counts_ref, place_ref, rows_ref, grads_ref, slot_row_ref, gate_row_ref,
    slot_col_ref, gate_col_ref, *refs
):
    in_refs, refs = refs[:n_in], refs[n_in:]
    sum_ref, grad_in_ref, gate_grad_ref = refs[:3]
    out_refs, refs = refs[3 : 3 + n_out], refs[3 + n_out :]
    weight, grad_weight, sum_acc, grad_in_acc = refs
    step = pl.program_id(0)
    expert = first + step
    tokens, width = rows_ref.shape
    hidden = weight.shape[2]
    span = 512

    @pl.when(step == 0)
    def _():
        sum_acc[...] = jnp.zeros_like(sum_acc)
        grad_in_acc[...] = jnp.zeros_like(grad_in_acc)
        gate_grad_ref[...] = jnp.zeros_like(gate_grad_ref)

    grad_weight[...] = jnp.zeros_like(grad_weight)
    if n_in == 1:
        weight[...] = in_refs[0][0]
    else:
        share = width // n_in
        for k in range(n_in):
            at = pl.ds(pl.multiple_of(place_ref[k] * share, share), share)
            weight[:, at, :] = in_refs[k][0]

    lane = lax.broadcasted_iota(jnp.int32, slot_col_ref.shape, 1)
    slot_col = jnp.sum(jnp.where(lane == expert, slot_col_ref[...], 0), axis=1, keepdims=True)
    gate_col = jnp.sum(jnp.where(lane == expert, gate_col_ref[...], 0.0), axis=1, keepdims=True)
    slot_row, gate_row = slot_row_ref[0], gate_row_ref[0]

    def tile(c, carry):
        down = c * TILE + lax.broadcasted_iota(jnp.int32, (TILE, 1), 0)
        across = c * TILE + lax.broadcasted_iota(jnp.int32, (1, TILE), 1)
        picked = slot_row == down
        inputs = dot_nn(jnp.where(picked, 1.0, 0.0).astype(BF16), rows_ref[...]).astype(BF16)
        grad_out = dot_nn(jnp.where(picked, gate_row, 0.0).astype(BF16), grads_ref[...]).astype(BF16)
        gate_part = dot_nn(inputs, weight[0])
        up_part = dot_nn(inputs, weight[1])
        sigmoid = 1.0 / (1.0 + jnp.exp(-gate_part))
        swish = gate_part * sigmoid
        act = (swish * up_part).astype(BF16)
        expert_out = dot_nt(act, weight[2]).astype(BF16)
        grad_act = dot_nn(grad_out, weight[2])
        grad_gate = (grad_act * up_part * sigmoid * (1.0 + gate_part * (1.0 - sigmoid))).astype(BF16)
        grad_up = (grad_act * swish).astype(BF16)
        grad_weight[0] += dot_tn(inputs, grad_gate)
        grad_weight[1] += dot_tn(inputs, grad_up)
        grad_weight[2] += dot_tn(grad_out, act)
        grad_in = (dot_nt(grad_gate, weight[0]) + dot_nt(grad_up, weight[1])).astype(BF16)
        for b in range(tokens // span):
            at = pl.ds(b * span, span)
            back = jnp.where(slot_col[b * span : (b + 1) * span] == across, 1.0, 0.0).astype(BF16)
            part = dot_nn(back, expert_out)
            sum_acc[at, :] += gate_col[b * span : (b + 1) * span] * part
            along = jnp.sum(part * grads_ref[at, :].astype(F32), axis=1, keepdims=True)
            lanes = lax.broadcasted_iota(jnp.int32, (span, gate_grad_ref.shape[1]), 1)
            gate_grad_ref[at, :] += jnp.where(lanes == expert, along, 0.0)
            grad_in_acc[at, :] += dot_nn(back, grad_in)
        return carry

    lax.fori_loop(0, (counts_ref[expert] + TILE - 1) // TILE, tile, 0)

    if n_out == 1:
        out_refs[0][0] = grad_weight[...].astype(BF16)
    else:
        for j in range(n_in // 2):
            for which in range(2):
                at = pl.ds(pl.multiple_of(place_ref[2 * j + which] * share, share), share)
                out_refs[which][j, 0] = grad_weight[:, at, :].astype(BF16)

    @pl.when(step == pl.num_programs(0) - 1)
    def _():
        sum_ref[...] = sum_acc[...].astype(BF16)
        grad_in_ref[...] = grad_in_acc[...].astype(BF16)


def experts(first, pieces, counts, place, rows, grads, slot_rows, gate_rows, slot_cols, gate_cols):
    tokens, width = rows.shape
    group, kinds, share, hidden = pieces[0].shape
    n_in = len(pieces)
    whole = lambda a: pl.BlockSpec(a.shape, lambda e, *_: (0,) * a.ndim, pipeline_mode=pl.Buffered(1))
    by_expert = pl.BlockSpec((1, 1, tokens), lambda e, *_: (first + e, 0, 0))
    piece_spec = pl.BlockSpec((1, kinds, share, hidden), lambda e, *_: (e, 0, 0, 0))
    token_spec = lambda w: pl.BlockSpec((tokens, w), lambda e, *_: (0, 0), pipeline_mode=pl.Buffered(1))
    if n_in == 1:
        grad_specs = [piece_spec]
        grad_shapes = [jax.ShapeDtypeStruct(pieces[0].shape, BF16)]
    else:
        half = n_in // 2
        grad_specs = [pl.BlockSpec((half, 1, kinds, share, hidden), lambda e, *_: (0, e, 0, 0, 0))] * 2
        grad_shapes = [jax.ShapeDtypeStruct((half, group, kinds, share, hidden), BF16)] * 2
    slots = tokens // 4
    return pl.pallas_call(
        functools.partial(experts_kernel, first, n_in, len(grad_specs)),
        grid_spec=pltpu.PrefetchScalarGridSpec(
            num_scalar_prefetch=2,
            grid=(group,),
            in_specs=[whole(rows), whole(grads), by_expert, by_expert, whole(slot_cols), whole(gate_cols)]
            + [piece_spec] * n_in,
            out_specs=[token_spec(width), token_spec(width), token_spec(128)] + grad_specs,
            scratch_shapes=[
                pltpu.VMEM((kinds, width, hidden), BF16),
                pltpu.VMEM((kinds, width, hidden), F32),
                pltpu.VMEM((tokens, width), F32),
                pltpu.VMEM((tokens, width), F32),
            ],
        ),
        out_shape=[
            jax.ShapeDtypeStruct((tokens, width), BF16),
            jax.ShapeDtypeStruct((tokens, width), BF16),
            jax.ShapeDtypeStruct((tokens, 128), F32),
        ]
        + grad_shapes,
        compiler_params=pltpu.CompilerParams(vmem_limit_bytes=60 << 20),
        cost_estimate=pl.CostEstimate(
            flops=group * slots * width * (18 * hidden + 8 * tokens),
            bytes_accessed=16 * tokens * width,
            transcendentals=0,
        ),
    )(counts, place, rows, grads, slot_rows, gate_rows, slot_cols, gate_cols, *pieces)


def per_device(
    tokens_in,
    carried_logits,
    cotangent,
    segment_ids,
    parent_ids,
    routes,
    attention_gain,
    head_weight,
    output_weight,
    expert_gain,
    router_weight,
    carry_weight,
    constant_gate,
    constant_vector,
    expert_first,
    expert_second,
):
    row_count, width = tokens_in.shape
    tree_len = segment_ids.shape[0]
    head_width = head_weight.shape[2]
    heads = head_width // HEAD
    share = head_weight.shape[1]
    group = NF // GROUPS
    me = lax.axis_index("dp")
    place = me ^ jnp.arange(8, dtype=jnp.int32)

    by_section = jnp.concatenate([head_weight, output_weight.T[None]], axis=0).astype(BF16)
    by_section = jnp.pad(by_section, ((0, 0), (0, 0), (0, PAD - head_width)))
    head_pack = by_section.transpose(1, 0, 2).reshape(share, 4 * PAD)
    expert_pack = jnp.concatenate(
        [expert_first.astype(BF16), expert_second.astype(BF16).transpose(0, 2, 1)[:, None]], axis=1
    )

    token_values = tokens_in.astype(F32)
    normed_one = normed(token_values, attention_gain).astype(BF16)
    gathered_one = gather_tensor(normed_one)
    head_pieces = pieces_of(head_pack, 0)
    if len(head_pieces) == 1:
        head_full = head_pieces[0]
    else:
        stacked = jnp.zeros((len(head_pieces), share, 4 * PAD), BF16)
        for k, piece in enumerate(head_pieces):
            stacked = lax.dynamic_update_slice(stacked, piece[None], (place[k], 0, 0))
        head_full = stacked.reshape(width, 4 * PAD)
    expert_pieces = [
        pieces_of(expert_pack[g * group : (g + 1) * group], 2) for g in range(GROUPS)
    ]
    gathered_grads = gather_tensor(cotangent)

    hot = jnp.sum((routes[:, :, None] == jnp.arange(NF, dtype=jnp.int32)).astype(jnp.int32), axis=1)
    rank = jnp.cumsum(hot, axis=0) - hot
    counts = jnp.sum(hot, axis=0)
    slot_cols = jnp.where(hot > 0, rank, -1)
    slot_rows = slot_cols.T[:, None, :]

    cos_table, sin_table = rotary_tables(segment_ids, parent_ids)
    rowinfo = jnp.pad(jnp.stack([segment_ids, parent_ids]), ((0, 6), (0, 0)))
    colinfo = rowinfo.T
    queries, keys, values, keys_t, values_t = project(gathered_one, head_full, cos_table, sin_table)
    attended, totals = attend(heads, queries, keys, values_t, rowinfo, colinfo)
    output_full = head_full[:, 3 * PAD :]
    attention_part = dot_nt(attended, output_full)
    hidden = token_values + scatter_tensor(attention_part, row_count)

    local_routes = lax.dynamic_slice_in_dim(
        routes, lax.axis_index("tensor") * row_count, row_count, 0
    )
    (normed_two, gates, local_sum), pull_router = jax.vjp(
        functools.partial(router_local, routes=local_routes),
        hidden,
        expert_gain,
        carried_logits,
        router_weight,
        carry_weight,
        constant_gate,
        constant_vector,
    )
    gathered_two = gather_tensor(normed_two.astype(BF16))
    gate_cols = gather_tensor(gates.astype(BF16)).astype(F32)
    gate_rows = gate_cols.T[:, None, :]

    sums, grad_ins, gate_grads, own_grads = [], [], [], []
    for g in range(GROUPS):
        part, grad_in, gate_grad, *grad_pieces = experts(
            g * group, expert_pieces[g], counts, place, gathered_two, gathered_grads,
            slot_rows, gate_rows, slot_cols, gate_cols,
        )
        sums.append(part.astype(F32))
        grad_ins.append(grad_in.astype(F32))
        gate_grads.append(gate_grad)
        if len(grad_pieces) == 1:
            own_grads.append(
                lax.psum_scatter(grad_pieces[0].astype(F32), "dp", scatter_dimension=2, tiled=True)
            )
        else:
            own_grads.append(sum_pieces(*grad_pieces))
    grad_normed_two = scatter_tensor(sum(grad_ins), row_count)
    grad_gates = lax.psum_scatter(
        sum(gate_grads)[:, :NF], "tensor", scatter_dimension=0, tiled=True
    )
    expert_total = scatter_tensor(sum(sums), row_count)
    output = (hidden + local_sum + expert_total).astype(BF16)
    own_grads = jnp.concatenate(own_grads, axis=0)
    grad_first = own_grads[:, :2]
    grad_second = own_grads[:, 2].transpose(0, 2, 1)

    grad_values_out = cotangent.astype(F32)
    (
        grad_hidden_local,
        grad_expert_gain,
        grad_carried,
        grad_router,
        grad_carry,
        grad_constant_gate,
        grad_constant_vector,
    ) = pull_router((grad_normed_two, grad_gates, grad_values_out))
    grad_hidden = grad_values_out + grad_hidden_local
    small = [grad_expert_gain, grad_router, grad_carry, grad_constant_gate, grad_constant_vector]
    flat = sum_all(jnp.concatenate([s.reshape(-1) for s in small]))
    small_out, at = [], 0
    for s in small:
        small_out.append(flat[at : at + s.size].reshape(s.shape))
        at += s.size

    grad_branch = gather_tensor(grad_hidden.astype(BF16))
    grad_attended = dot_nn(grad_branch, output_full).astype(BF16)
    grad_output_t = dot_tn(grad_branch, attended)
    grad_projected = jnp.concatenate(
        attend_back(
            heads, queries, grad_attended, attended, keys, values, keys_t, rowinfo, colinfo, totals,
            cos_table, sin_table,
        ),
        axis=1,
    )
    grad_head = dot_tn(gathered_one, grad_projected)
    grad_normed_all = dot_nt(grad_projected, head_full[:, : 3 * PAD])
    grad_normed_one = scatter_tensor(grad_normed_all, row_count)
    grad_pack = jnp.concatenate([grad_head, grad_output_t], axis=1).astype(BF16)
    if len(head_pieces) == 1:
        own_pack = lax.psum_scatter(grad_pack.astype(F32), "dp", scatter_dimension=0, tiled=True)
    else:
        blocks = grad_pack.reshape(8, share, 4 * PAD)
        ordered = [lax.dynamic_index_in_dim(blocks, place[k], 0, keepdims=False) for k in range(8)]
        own_pack = sum_pieces(jnp.stack(ordered[0::2]), jnp.stack(ordered[1::2]))
    own_pack = own_pack.reshape(share, 4, PAD)[:, :, :head_width].transpose(1, 0, 2)
    grad_head_own = own_pack[:3]
    grad_output_own = own_pack[3].T

    norm_values, pull_norm = jax.vjp(normed, token_values, attention_gain)
    grad_token_part, grad_attention_gain = pull_norm(grad_normed_one)
    grad_tokens = grad_hidden + grad_token_part
    grad_attention_gain = sum_all(grad_attention_gain)
    return (
        output,
        grad_tokens,
        grad_carried,
        grad_attention_gain,
        grad_head_own,
        grad_output_own,
        *small_out,
        grad_first,
        grad_second,
    )


def solution(mesh):
    in_specs = (
        P(("dp", "tensor"), None),
        P(("dp", "tensor"), None),
        P(("dp", "tensor"), None),
        P("dp"),
        P("dp"),
        P("dp", None),
        P(),
        P(None, "dp", "tensor"),
        P("tensor", "dp"),
        P(),
        P(),
        P(),
        P(),
        P(),
        P(None, None, "dp", "tensor"),
        P(None, "tensor", "dp"),
    )
    out_specs = (
        P(("dp", "tensor"), None),
        P(("dp", "tensor"), None),
        P(("dp", "tensor"), None),
        P(),
        P(None, "dp", "tensor"),
        P("tensor", "dp"),
        P(),
        P(),
        P(),
        P(),
        P(),
        P(None, None, "dp", "tensor"),
        P(None, "tensor", "dp"),
    )
    return jax.shard_map(
        per_device, mesh=mesh, in_specs=in_specs, out_specs=out_specs, check_vma=False
    )
```

```python
import functools

import jax
import jax.numpy as jnp
from jax import lax
from jax.experimental import pallas as pl
from jax.experimental.pallas import tpu as pltpu
from jax.sharding import PartitionSpec as P

HEAD = 64
NF = 8
NSEG = 13
NE = 12
PAD = 256
BLOCK = 256
TILE = 256
GROUPS = 2

epsilon = 1e-06
HIGHEST = lax.Precision.HIGHEST
F32 = jnp.float32
BF16 = jnp.bfloat16


def dot_nn(a, b):
    return lax.dot_general(a, b, (((1,), (0,)), ((), ())), preferred_element_type=F32)


def dot_nt(a, b):
    return lax.dot_general(a, b, (((1,), (1,)), ((), ())), preferred_element_type=F32)


def dot_tn(a, b):
    return lax.dot_general(a, b, (((0,), (0,)), ((), ())), preferred_element_type=F32)


def normed(values, gain_vector):
    return (
        values
        * lax.rsqrt(jnp.mean(values * values, axis=-1, keepdims=True) + epsilon)
        * gain_vector
    )


def tree_positions(segment, parent):
    token_count = segment.shape[0]
    labels = jnp.arange(NSEG, dtype=jnp.int32)
    own_hot = (segment[:, None] == labels[None, :]).astype(jnp.int32)
    parent_hot = (parent[:, None] == labels[None, :]).astype(jnp.int32)
    lengths = jnp.sum(own_hot, axis=0)
    starts = jnp.cumsum(lengths) - lengths
    own_start = jnp.sum(own_hot * starts[None, :], axis=1)
    parent_length = jnp.sum(parent_hot * lengths[None, :], axis=1)
    position_index = jnp.arange(token_count, dtype=jnp.int32)
    return (
        position_index
        - own_start
        + jnp.where(segment > 0, lengths[0], 0)
        + jnp.where(parent > 0, parent_length, 0)
    )


def rotary_tables(segment, parent):
    angle_rate = 10000.0 ** (-2.0 * jnp.arange(HEAD // 2, dtype=F32) / HEAD)
    angles = tree_positions(segment, parent).astype(F32)[:, None] * angle_rate[None, :]
    cosine, sine = jnp.cos(angles), jnp.sin(angles)
    copies = PAD // HEAD
    cos_table = jnp.tile(jnp.concatenate([cosine, cosine], axis=1), (1, copies))
    sin_table = jnp.tile(jnp.concatenate([-sine, sine], axis=1), (1, copies))
    return cos_table, sin_table


def router_local(
    hidden, gain_vector, carried, router_weight, carry_weight, constant_gate, constant_vector, routes
):
    normed_two = normed(hidden, gain_vector)
    logits = jnp.dot(normed_two, router_weight, precision=HIGHEST) + jnp.dot(
        carried, carry_weight, precision=HIGHEST
    )
    picked = (routes[:, :, None] == jnp.arange(NE, dtype=jnp.int32)[None, None, :]).astype(F32)
    chosen = jnp.sum(picked * logits[:, None, :], axis=-1)
    gate_values = jax.nn.softmax(chosen, axis=-1)
    by_expert = jnp.sum(picked * gate_values[:, :, None], axis=1)
    mixture = jax.nn.softmax(
        jnp.dot(normed_two, constant_gate, precision=HIGHEST).reshape(-1, 2, 2), axis=-1
    )
    copy_weight = by_expert[:, NF + 1]
    first_weight = by_expert[:, NF + 2]
    second_weight = by_expert[:, NF + 3]
    local_sum = copy_weight[:, None] * normed_two
    local_sum = local_sum + first_weight[:, None] * (
        mixture[:, 0, 0:1] * normed_two + mixture[:, 0, 1:2] * constant_vector[0][None, :]
    )
    local_sum = local_sum + second_weight[:, None] * (
        mixture[:, 1, 0:1] * normed_two + mixture[:, 1, 1:2] * constant_vector[1][None, :]
    )
    return (normed_two, by_expert[:, :NF], local_sum)


def swap(values, axis, bits):
    size = lax.axis_size(axis)
    return lax.ppermute(values, axis, [(i, i ^ bits) for i in range(size)])


def gather_tensor(own):
    index = lax.axis_index("tensor")
    far = swap(own, "tensor", 2)
    near = swap(own, "tensor", 1)
    far_near = swap(far, "tensor", 1)
    core, chip = index % 2 == 0, index // 2 == 0
    here = [jnp.where(core, own, near), jnp.where(core, near, own)]
    there = [jnp.where(core, far, far_near), jnp.where(core, far_near, far)]
    order = [jnp.where(chip, h, t) for h, t in zip(here, there)]
    order += [jnp.where(chip, t, h) for h, t in zip(here, there)]
    return jnp.concatenate(order, axis=0)


def scatter_tensor(parts, rows):
    index = lax.axis_index("tensor")

    def take(which):
        return lax.dynamic_slice_in_dim(parts, which * rows, rows, 0).astype(F32)

    near = swap(
        jnp.concatenate([take(index ^ 1), take(index ^ 3)], axis=0).astype(BF16), "tensor", 1
    ).astype(F32)
    mine = take(index) + near[:rows]
    other = take(index ^ 2) + near[rows:]
    return mine + swap(other.astype(BF16), "tensor", 2).astype(F32)


def together(*values):
    return lax.optimization_barrier(values)


def column_groups():
    size = lax.axis_size("dp")
    return [list(range(first, size, 2)) for first in range(2)]


def gather_column(own):
    return lax.all_gather(own, "dp", axis=0, tiled=False, axis_index_groups=column_groups())


def scatter_column(parts):
    return lax.psum_scatter(
        parts, "dp", scatter_dimension=0, tiled=False, axis_index_groups=column_groups()
    )


def by_parity(mine, other):
    even = lax.axis_index("dp") % 2 == 0
    return jnp.stack([jnp.where(even, mine, other), jnp.where(even, other, mine)])


def gather_pair(own):
    half = own.shape[0] // 2
    far, across = swap(own, "tensor", 2), swap(own, "dp", 1)
    corner = jnp.concatenate(
        [swap(across[:half], "tensor", 2), swap(far[half:], "dp", 1)], axis=0
    )
    near = [swap(piece, "tensor", 1) for piece in (own, far, across, corner)]
    return [own, near[0], far, near[1], across, near[2], corner, near[3]]


def scatter_pair(keep, send):
    half = keep.shape[1] // 2
    keep = keep.astype(F32) + swap(send, "tensor", 1).astype(F32)
    mine, far, across, corner = keep[0], keep[1], keep[2], keep[3].astype(BF16)
    from_far = swap(corner[:half], "tensor", 2).astype(F32)
    from_across = swap(corner[half:], "dp", 1).astype(F32)
    far = jnp.concatenate([far[:half], far[half:] + from_across], axis=0).astype(BF16)
    across = jnp.concatenate([across[:half] + from_far, across[half:]], axis=0).astype(BF16)
    return mine + swap(far, "tensor", 2).astype(F32) + swap(across, "dp", 1).astype(F32)


def sum_all(values):
    if lax.axis_size("dp") != 8:
        return lax.psum(values, ("dp", "tensor"))
    for axis, bits in (("tensor", 1), ("tensor", 2), ("dp", 1), ("dp", 2), ("dp", 4)):
        values = values + swap(values, axis, bits)
    return values


def swap_halves(values):
    lane = lax.broadcasted_iota(jnp.int32, values.shape, 1)
    half = HEAD // 2
    return jnp.where(
        lane % HEAD < half, pltpu.roll(values, PAD - half, 1), pltpu.roll(values, half, 1)
    )


def project_kernel(n_ref, w_ref, c_ref, s_ref, q_ref, k_ref, v_ref, kt_ref, vt_ref):
    rows = n_ref[...]
    cosine, sine = c_ref[...], s_ref[...]
    part = dot_nn(rows, w_ref[:, :PAD])
    q_ref[...] = ((part * cosine + swap_halves(part) * sine) * HEAD**-0.5).astype(BF16)
    part = dot_nn(rows, w_ref[:, PAD : 2 * PAD])
    keys = part * cosine + swap_halves(part) * sine
    k_ref[...] = keys.astype(BF16)
    kt_ref[...] = keys.T.astype(BF16)
    values = dot_nn(rows, w_ref[:, 2 * PAD : 3 * PAD])
    v_ref[...] = values.astype(BF16)
    vt_ref[...] = values.T.astype(BF16)


def project(gathered, weights, cos_table, sin_table):
    rows, width = gathered.shape
    grid = (rows // BLOCK,)
    row_spec = pl.BlockSpec((BLOCK, PAD), lambda i: (i, 0))
    column_spec = pl.BlockSpec((PAD, BLOCK), lambda i: (0, i))
    wide = jax.ShapeDtypeStruct((rows, PAD), BF16)
    tall = jax.ShapeDtypeStruct((PAD, rows), BF16)
    return pl.pallas_call(
        project_kernel,
        grid=grid,
        in_specs=[
            pl.BlockSpec((BLOCK, width), lambda i: (i, 0)),
            pl.BlockSpec(weights.shape, lambda i: (0, 0)),
            row_spec,
            row_spec,
        ],
        out_specs=[row_spec, row_spec, row_spec, column_spec, column_spec],
        out_shape=[wide, wide, wide, tall, tall],
        cost_estimate=pl.CostEstimate(
            flops=2 * rows * width * 3 * PAD, bytes_accessed=8 * rows * width, transcendentals=0
        ),
    )(gathered, weights, cos_table, sin_table)


def head_mask(values, head):
    lane = lax.broadcasted_iota(jnp.int32, values.shape, 1)
    return jnp.where(lane // HEAD == head, values, jnp.zeros_like(values))


def seen(i, j, seg_row, par_row, seg_col):
    key_at = j * BLOCK + lax.broadcasted_iota(jnp.int32, (BLOCK, 1), 0)
    query_at = i * BLOCK + lax.broadcasted_iota(jnp.int32, (1, BLOCK), 1)
    related = (seg_col == seg_row) | (seg_col == par_row) | (seg_col == 0)
    return related & (key_at <= query_at)


def attend_kernel(heads, q_ref, k_ref, vt_ref, rowinfo_ref, colinfo_ref, o_ref, total_ref):
    i = pl.program_id(0)
    queries = q_ref[...]
    by_head = [head_mask(queries, h) for h in range(heads)]
    seg_row, par_row = rowinfo_ref[0:1, :], rowinfo_ref[1:2, :]

    def step(j, carry):
        at = pl.ds(pl.multiple_of(j * BLOCK, BLOCK), BLOCK)
        keys = k_ref[at, :]
        visible = seen(i, j, seg_row, par_row, colinfo_ref[at, 0:1])
        out = []
        for h in range(heads):
            top, total, mixed = carry[h]
            scores = jnp.where(visible, dot_nt(keys, by_head[h]), -1e30)
            new_top = jnp.maximum(top, jnp.max(scores, axis=0, keepdims=True))
            shrink = jnp.exp(top - new_top)
            probs = jnp.exp(scores - new_top)
            total = total * shrink + jnp.sum(probs, axis=0, keepdims=True)
            mixed = mixed * shrink + dot_nn(
                vt_ref[h * HEAD : (h + 1) * HEAD, at], probs.astype(BF16)
            )
            out.append((new_top, total, mixed))
        return tuple(out)

    start = tuple(
        (
            jnp.full((1, BLOCK), -1e30, F32),
            jnp.zeros((1, BLOCK), F32),
            jnp.zeros((HEAD, BLOCK), F32),
        )
        for _ in range(heads)
    )
    done = lax.fori_loop(0, i + 1, step, start)
    mixed = [m / t for _, t, m in done] + [jnp.zeros((PAD - heads * HEAD, BLOCK), F32)]
    o_ref[...] = jnp.concatenate(mixed, axis=0).T.astype(BF16)
    total_ref[...] = jnp.concatenate(
        [m + jnp.log(t) for m, t, _ in done] + [jnp.zeros((8 - heads, BLOCK), F32)], axis=0
    )


def attend(heads, queries, keys, values_t, rowinfo, colinfo):
    rows = queries.shape[0]
    whole = lambda a: pl.BlockSpec(a.shape, lambda i: (0,) * a.ndim)
    return pl.pallas_call(
        functools.partial(attend_kernel, heads),
        grid=(rows // BLOCK,),
        in_specs=[
            pl.BlockSpec((BLOCK, PAD), lambda i: (i, 0)),
            whole(keys),
            whole(values_t),
            pl.BlockSpec((8, BLOCK), lambda i: (0, i)),
            whole(colinfo),
        ],
        out_specs=[
            pl.BlockSpec((BLOCK, PAD), lambda i: (i, 0)),
            pl.BlockSpec((8, BLOCK), lambda i: (0, i)),
        ],
        out_shape=[
            jax.ShapeDtypeStruct((rows, PAD), BF16),
            jax.ShapeDtypeStruct((8, rows), F32),
        ],
        compiler_params=pltpu.CompilerParams(vmem_limit_bytes=32 << 20),
        cost_estimate=pl.CostEstimate(
            flops=heads * rows * rows * 512, bytes_accessed=8 * rows * PAD, transcendentals=0
        ),
    )(queries, keys, values_t, rowinfo, colinfo)


def attend_back_kernel(
    heads,
    q_ref,
    g_ref,
    o_ref,
    k_ref,
    v_ref,
    kt_ref,
    rowinfo_ref,
    colinfo_ref,
    total_ref,
    c_ref,
    s_ref,
    gq_ref,
    gk_ref,
    gv_ref,
    key_sum,
    value_sum,
    query_sum,
):
    i = pl.program_id(0)
    here = pl.ds(pl.multiple_of(i * BLOCK, BLOCK), BLOCK)

    @pl.when(i == 0)
    def _():
        key_sum[...] = jnp.zeros_like(key_sum)
        value_sum[...] = jnp.zeros_like(value_sum)

    query_sum[...] = jnp.zeros_like(query_sum)
    queries, grads = q_ref[...], g_ref[...]
    q_heads = [head_mask(queries, h) for h in range(heads)]
    g_heads = [head_mask(grads, h) for h in range(heads)]
    seg_row, par_row = rowinfo_ref[0:1, :], rowinfo_ref[1:2, :]
    product = grads.astype(F32) * o_ref[...].astype(F32)
    lane = lax.broadcasted_iota(jnp.int32, (8, PAD), 1)
    which = lax.broadcasted_iota(jnp.int32, (8, PAD), 0)
    delta = lax.dot_general(
        (lane // HEAD == which).astype(F32),
        product,
        (((1,), (1,)), ((), ())),
        precision=HIGHEST,
        preferred_element_type=F32,
    )
    totals = total_ref[...]

    def step(j, carry):
        at = pl.ds(pl.multiple_of(j * BLOCK, BLOCK), BLOCK)
        keys, values = k_ref[at, :], v_ref[at, :]
        visible = seen(i, j, seg_row, par_row, colinfo_ref[at, 0:1])
        key_part, value_part = key_sum[at, :], value_sum[at, :]
        for h in range(heads):
            scores = jnp.where(visible, dot_nt(keys, q_heads[h]), -1e30)
            probs = jnp.exp(scores - totals[h : h + 1, :])
            value_part = value_part + dot_nn(probs.astype(BF16), g_heads[h])
            grad_probs = dot_nt(values, g_heads[h])
            grad_scores = (probs * (grad_probs - delta[h : h + 1, :])).astype(BF16)
            key_part = key_part + dot_nn(grad_scores, q_heads[h])
            lanes = slice(h * HEAD, (h + 1) * HEAD)
            query_sum[lanes, :] += dot_nn(kt_ref[lanes, at], grad_scores)
        key_sum[at, :] = key_part
        value_sum[at, :] = value_part
        return carry

    lax.fori_loop(0, i + 1, step, 0)
    grad_q = query_sum[...].T * HEAD**-0.5
    cosine, sine = c_ref[here, :], s_ref[here, :]
    gq_ref[...] = (grad_q * cosine - swap_halves(grad_q) * sine).astype(BF16)

    @pl.when(i == pl.num_programs(0) - 1)
    def _():
        def finish(j, carry):
            at = pl.ds(pl.multiple_of(j * BLOCK, BLOCK), BLOCK)
            grad_k = key_sum[at, :]
            gk_ref[at, :] = (grad_k * c_ref[at, :] - swap_halves(grad_k) * s_ref[at, :]).astype(BF16)
            gv_ref[at, :] = value_sum[at, :].astype(BF16)
            return carry

        lax.fori_loop(0, pl.num_programs(0), finish, 0)


def attend_back(heads, queries, grads, out, keys, values, keys_t, rowinfo, colinfo, totals, cos_table, sin_table):
    rows = queries.shape[0]
    whole = lambda a: pl.BlockSpec(a.shape, lambda i: (0,) * a.ndim)
    row_spec = pl.BlockSpec((BLOCK, PAD), lambda i: (i, 0))
    wide = jax.ShapeDtypeStruct((rows, PAD), BF16)
    return pl.pallas_call(
        functools.partial(attend_back_kernel, heads),
        grid=(rows // BLOCK,),
        in_specs=[
            row_spec,
            row_spec,
            row_spec,
            whole(keys),
            whole(values),
            whole(keys_t),
            pl.BlockSpec((8, BLOCK), lambda i: (0, i)),
            whole(colinfo),
            pl.BlockSpec((8, BLOCK), lambda i: (0, i)),
            whole(cos_table),
            whole(sin_table),
        ],
        out_specs=[
            row_spec,
            pl.BlockSpec((rows, PAD), lambda i: (0, 0)),
            pl.BlockSpec((rows, PAD), lambda i: (0, 0)),
        ],
        out_shape=[wide, wide, wide],
        scratch_shapes=[
            pltpu.VMEM((rows, PAD), F32),
            pltpu.VMEM((rows, PAD), F32),
            pltpu.VMEM((PAD, BLOCK), F32),
        ],
        compiler_params=pltpu.CompilerParams(vmem_limit_bytes=40 << 20),
        cost_estimate=pl.CostEstimate(
            flops=heads * rows * rows * 1280, bytes_accessed=16 * rows * PAD, transcendentals=0
        ),
    )(queries, grads, out, keys, values, keys_t, rowinfo, colinfo, totals, cos_table, sin_table)


def experts_kernel(whole_weights, base_ref, counts_ref, slot_rows_ref, slot_cols_ref, weights_ref, *refs):
    rows_refs, grads_refs, refs = refs[:8], refs[8:16], refs[16:]
    sum_refs, grad_in_refs, out_ref, weight, grad_weight, gates = (
        refs[0:2], refs[2:4], refs[4], refs[5], refs[6], refs[7],
    )
    step = pl.program_id(0)
    expert = base_ref[0] + step
    rows, width = grads_refs[0].shape

    @pl.when(step == 0)
    def _():
        for ref in (*sum_refs, *grad_in_refs):
            ref[...] = jnp.zeros_like(ref)
        for k in range(8):
            at = pl.ds((k % 4) * rows, rows)
            gates[k // 4, :, at] = rows_refs[k][:, width:].astype(F32).T

    grad_weight[...] = jnp.zeros_like(grad_weight)
    if whole_weights:
        weight[...] = weights_ref[0]
    else:
        depth, _, _, _, share, _ = weights_ref.shape
        for z in range(depth):
            for y in range(2):
                weight[:, pl.ds((2 * z + y) * share, share), :] = weights_ref[z, y, 0]

    def tree(a):
        slot_row = slot_rows_ref[a, pl.ds(expert, 1), :]
        gate_row = gates[a, pl.ds(expert, 1), :]

        def tile(c, carry):
            down = c * TILE + lax.broadcasted_iota(jnp.int32, (TILE, 1), 0)
            across = c * TILE + lax.broadcasted_iota(jnp.int32, (1, TILE), 1)
            inputs = jnp.zeros((TILE, width), F32)
            grad_out = jnp.zeros((TILE, width), F32)
            for b in range(4):
                picked = slot_row[:, b * rows : (b + 1) * rows] == down
                gate = gate_row[:, b * rows : (b + 1) * rows]
                inputs = inputs + dot_nn(
                    jnp.where(picked, 1.0, 0.0).astype(BF16), rows_refs[4 * a + b][:, :width]
                )
                grad_out = grad_out + dot_nn(
                    jnp.where(picked, gate, 0.0).astype(BF16), grads_refs[4 * a + b][...]
                )
            inputs, grad_out = inputs.astype(BF16), grad_out.astype(BF16)
            gate_part = dot_nn(inputs, weight[0])
            up_part = dot_nn(inputs, weight[1])
            sigmoid = 1.0 / (1.0 + jnp.exp(-gate_part))
            swish = gate_part * sigmoid
            act = (swish * up_part).astype(BF16)
            expert_out = dot_nt(act, weight[2]).astype(BF16)
            grad_act = dot_nn(grad_out, weight[2])
            grad_gate = (
                grad_act * up_part * sigmoid * (1.0 + gate_part * (1.0 - sigmoid))
            ).astype(BF16)
            grad_up = (grad_act * swish).astype(BF16)
            grad_weight[0] += dot_tn(inputs, grad_gate)
            grad_weight[1] += dot_tn(inputs, grad_up)
            grad_weight[2] += dot_tn(grad_out, act)
            grad_in = (dot_nt(grad_gate, weight[0]) + dot_nt(grad_up, weight[1])).astype(BF16)
            for b in range(4):
                k = 4 * a + b
                lane = lax.broadcasted_iota(jnp.int32, (rows, 8), 1)
                slot_col = jnp.sum(
                    jnp.where(lane == expert, slot_cols_ref[pl.ds(k * rows, rows), :], 0),
                    axis=1,
                    keepdims=True,
                )
                lane = lax.broadcasted_iota(jnp.int32, (rows, 128), 1)
                gate_col = jnp.sum(
                    jnp.where(lane == expert, rows_refs[k][:, width:].astype(F32), 0.0),
                    axis=1,
                    keepdims=True,
                )
                back = jnp.where(slot_col == across, 1.0, 0.0).astype(BF16)
                part = dot_nn(back, expert_out)
                sum_ref, grad_in_ref = sum_refs[b % 2], grad_in_refs[b % 2]
                at = 2 * a + b // 2
                sum_ref[at] = (sum_ref[at].astype(F32) + gate_col * part).astype(BF16)
                along = jnp.sum(part * grads_refs[k][...].astype(F32), axis=1, keepdims=True)
                grad_in_ref[at, :, :width] = (
                    grad_in_ref[at, :, :width].astype(F32) + dot_nn(back, grad_in)
                ).astype(BF16)
                grad_in_ref[at, :, width:] = (
                    grad_in_ref[at, :, width:].astype(F32) + jnp.where(lane == expert, along, 0.0)
                ).astype(BF16)
            return carry

        lax.fori_loop(0, (counts_ref[a, expert] + TILE - 1) // TILE, tile, 0)

    tree(0)
    tree(1)
    if whole_weights:
        out_ref[0] = grad_weight[...].astype(BF16)
    else:
        for z in range(depth):
            for y in range(2):
                at = pl.ds((2 * z + y) * share, share)
                out_ref[z, y, 0] = grad_weight[:, at, :].astype(BF16)


def experts(base, weights, counts, rows, grads, slot_rows, slot_cols):
    count, width = grads[0].shape
    wide = rows[0].shape[1]
    whole_weights = weights.ndim == 4
    kinds, share, hidden = weights.shape[-3:]
    group = weights.shape[0] if whole_weights else weights.shape[2]
    depth = width if whole_weights else 2 * weights.shape[0] * share
    whole = lambda a: pl.BlockSpec(a.shape, lambda e, *_: (0,) * a.ndim, pipeline_mode=pl.Buffered(1))
    if whole_weights:
        weight_spec = pl.BlockSpec((1, kinds, share, hidden), lambda e, *_: (e, 0, 0, 0))
    else:
        weight_spec = pl.BlockSpec(
            (weights.shape[0], 2, 1, kinds, share, hidden), lambda e, *_: (0, 0, e, 0, 0, 0)
        )
    sums = jax.ShapeDtypeStruct((4, count, width), BF16)
    grad_ins = jax.ShapeDtypeStruct((4, count, wide), BF16)
    slots = count * 2
    return pl.pallas_call(
        functools.partial(experts_kernel, whole_weights),
        grid_spec=pltpu.PrefetchScalarGridSpec(
            num_scalar_prefetch=2,
            grid=(group,),
            in_specs=[whole(slot_rows), whole(slot_cols), weight_spec]
            + [whole(a) for a in rows]
            + [whole(a) for a in grads],
            out_specs=[whole(sums), whole(sums), whole(grad_ins), whole(grad_ins), weight_spec],
            scratch_shapes=[
                pltpu.VMEM((kinds, depth, hidden), BF16),
                pltpu.VMEM((kinds, depth, hidden), F32),
                pltpu.VMEM((2, wide - width, 4 * count), F32),
            ],
        ),
        out_shape=[sums, sums, grad_ins, grad_ins, jax.ShapeDtypeStruct(weights.shape, BF16)],
        compiler_params=pltpu.CompilerParams(vmem_limit_bytes=60 << 20),
        cost_estimate=pl.CostEstimate(
            flops=group * slots * width * (18 * hidden + 32 * count),
            bytes_accessed=64 * count * width,
            transcendentals=0,
        ),
    )(base, counts, slot_rows, slot_cols, weights, *rows, *grads)


def per_device(
    tokens_in,
    carried_logits,
    cotangent,
    segment_ids,
    parent_ids,
    routes,
    attention_gain,
    head_weight,
    output_weight,
    expert_gain,
    router_weight,
    carry_weight,
    constant_gate,
    constant_vector,
    expert_first,
    expert_second,
):
    row_count, width = tokens_in.shape
    tree_len = segment_ids.shape[0]
    head_width = head_weight.shape[2]
    heads = head_width // HEAD
    share = head_weight.shape[1]
    parity = lax.axis_index("dp") % 2
    index = lax.axis_index("tensor")
    own_experts = NF // 2
    group = own_experts // GROUPS
    layered = share % 16 == 0

    by_section = jnp.concatenate([head_weight, output_weight.T[None]], axis=0).astype(BF16)
    by_section = jnp.pad(by_section, ((0, 0), (0, 0), (0, PAD - head_width)))
    head_pack = by_section.transpose(1, 0, 2).reshape(share, 4 * PAD)
    expert_pack = jnp.concatenate(
        [expert_first.astype(BF16), expert_second.astype(BF16).transpose(0, 2, 1)[:, None]], axis=1
    )

    token_values = tokens_in.astype(F32)
    normed_one = normed(token_values, attention_gain).astype(BF16)
    gathered_one = gather_tensor(normed_one)
    column = gather_column(head_pack)
    head_full = jnp.moveaxis(by_parity(column, swap(column, "dp", 1)), 0, 1).reshape(width, 4 * PAD)
    expert_weights = []
    kept = lax.dynamic_slice_in_dim(expert_pack, parity * own_experts, own_experts, 0)
    given = lax.dynamic_slice_in_dim(expert_pack, (1 - parity) * own_experts, own_experts, 0)
    for g in range(GROUPS):
        at = slice(g * group, (g + 1) * group)
        shards = gather_column(by_parity(kept[at], swap(given[at], "dp", 1)))
        if not layered:
            shards = shards.transpose(2, 3, 0, 1, 4, 5).reshape(group, 3, width, -1)
        expert_weights.append(shards)
    grad_rows = gather_pair(cotangent)

    labels = jnp.arange(NF, dtype=jnp.int32)
    slot_cols, counts = [], []
    for tree_routes in (routes, swap(routes, "dp", 1)):
        hot = jnp.sum((tree_routes[:, :, None] == labels).astype(jnp.int32), axis=1)
        rank = jnp.cumsum(hot, axis=0) - hot
        counts.append(jnp.sum(hot, axis=0))
        quarters = jnp.where(hot > 0, rank, -1).reshape(4, row_count, NF)
        for b in range(4):
            slot_cols.append(lax.dynamic_index_in_dim(quarters, index ^ b, 0, keepdims=False))
    counts = jnp.stack(counts)
    slot_cols = jnp.concatenate(slot_cols, axis=0)
    slot_rows = slot_cols.reshape(2, tree_len, NF).transpose(0, 2, 1)

    cos_table, sin_table = rotary_tables(segment_ids, parent_ids)
    rowinfo = jnp.pad(jnp.stack([segment_ids, parent_ids]), ((0, 6), (0, 0)))
    colinfo = rowinfo.T
    queries, keys, values, keys_t, values_t = project(gathered_one, head_full, cos_table, sin_table)
    attended, totals = attend(heads, queries, keys, values_t, rowinfo, colinfo)
    output_full = head_full[:, 3 * PAD :]
    attention_part = dot_nt(attended, output_full)
    hidden = token_values + scatter_tensor(attention_part, row_count)

    local_routes = lax.dynamic_slice_in_dim(
        routes, lax.axis_index("tensor") * row_count, row_count, 0
    )
    (normed_two, gates, local_sum), pull_router = jax.vjp(
        functools.partial(router_local, routes=local_routes),
        hidden,
        expert_gain,
        carried_logits,
        router_weight,
        carry_weight,
        constant_gate,
        constant_vector,
    )
    expert_rows = gather_pair(
        jnp.concatenate([normed_two, jnp.pad(gates, ((0, 0), (0, 128 - NF)))], axis=1).astype(BF16)
    )

    parts, own_grads = [], []
    for g in range(GROUPS):
        base = (parity * own_experts + g * group).astype(jnp.int32).reshape(1)
        *part, weight_grads = experts(
            base, expert_weights[g], counts, expert_rows, grad_rows, slot_rows, slot_cols
        )
        parts.append(part)
        if not layered:
            weight_grads = weight_grads.reshape(group, 3, -1, 2, share, weight_grads.shape[-1])
            weight_grads = weight_grads.transpose(2, 3, 0, 1, 4, 5)
        own_grads.append(scatter_column(weight_grads))
    keep, send, grad_keep, grad_send = [
        sum(p.astype(F32) for p in same).astype(BF16) for same in zip(*parts)
    ]
    both = scatter_pair(grad_keep, grad_send)
    grad_normed_two, grad_gates = both[:, :width], both[:, width : width + NF]
    output = (hidden + local_sum + scatter_pair(keep, send)).astype(BF16)
    grad_values_out = cotangent.astype(F32)
    (
        grad_hidden_local,
        grad_expert_gain,
        grad_carried,
        grad_router,
        grad_carry,
        grad_constant_gate,
        grad_constant_vector,
    ) = pull_router((grad_normed_two, grad_gates, grad_values_out))
    grad_hidden = grad_values_out + grad_hidden_local
    grad_hidden, own_grads[0] = together(grad_hidden, own_grads[0])
    small = [grad_expert_gain, grad_router, grad_carry, grad_constant_gate, grad_constant_vector]
    flat = sum_all(jnp.concatenate([s.reshape(-1) for s in small]))
    small_out, at = [], 0
    for s in small:
        small_out.append(flat[at : at + s.size].reshape(s.shape))
        at += s.size

    grad_branch = gather_tensor(grad_hidden.astype(BF16))
    grad_attended = dot_nn(grad_branch, output_full).astype(BF16)
    grad_output_t = dot_tn(grad_branch, attended)
    grad_projected = jnp.concatenate(
        attend_back(
            heads, queries, grad_attended, attended, keys, values, keys_t, rowinfo, colinfo, totals,
            cos_table, sin_table,
        ),
        axis=1,
    )
    grad_projected, own_grads[1] = together(grad_projected, own_grads[1])
    own_grads = jnp.concatenate(own_grads, axis=1)
    kept = lax.dynamic_index_in_dim(own_grads, parity, 0, keepdims=False)
    given = lax.dynamic_index_in_dim(own_grads, 1 - parity, 0, keepdims=False)
    own_grads = by_parity(kept, swap(given, "dp", 1)).reshape(NF, 3, share, -1).astype(F32)
    grad_first = own_grads[:, :2]
    grad_second = own_grads[:, 2].transpose(0, 2, 1)
    grad_head = dot_tn(gathered_one, grad_projected)
    grad_normed_all = dot_nt(grad_projected, head_full[:, : 3 * PAD])
    grad_normed_one = scatter_tensor(grad_normed_all, row_count)
    grad_pack = jnp.concatenate([grad_head, grad_output_t], axis=1).astype(BF16)
    blocks = grad_pack.reshape(-1, 2, share, 4 * PAD)
    kept = lax.dynamic_index_in_dim(blocks, parity, 1, keepdims=False)
    given = lax.dynamic_index_in_dim(blocks, 1 - parity, 1, keepdims=False)
    paired = kept.astype(F32) + swap(given, "dp", 1).astype(F32)
    own_pack = scatter_column(paired.astype(BF16)).astype(F32)
    own_pack = own_pack.reshape(share, 4, PAD)[:, :, :head_width].transpose(1, 0, 2)
    grad_head_own = own_pack[:3]
    grad_output_own = own_pack[3].T

    grad_attention_gain = sum_all(
        jnp.sum(grad_head * head_full[:, : 3 * PAD].astype(F32), axis=1) / attention_gain
    )
    _, pull_norm = jax.vjp(lambda v: normed(v, attention_gain), token_values)
    grad_tokens = grad_hidden + pull_norm(grad_normed_one)[0]
    return (
        output,
        grad_tokens,
        grad_carried,
        grad_attention_gain,
        grad_head_own,
        grad_output_own,
        *small_out,
        grad_first,
        grad_second,
    )


def solution(mesh):
    in_specs = (
        P(("dp", "tensor"), None),
        P(("dp", "tensor"), None),
        P(("dp", "tensor"), None),
        P("dp"),
        P("dp"),
        P("dp", None),
        P(),
        P(None, "dp", "tensor"),
        P("tensor", "dp"),
        P(),
        P(),
        P(),
        P(),
        P(),
        P(None, None, "dp", "tensor"),
        P(None, "tensor", "dp"),
    )
    out_specs = (
        P(("dp", "tensor"), None),
        P(("dp", "tensor"), None),
        P(("dp", "tensor"), None),
        P(),
        P(None, "dp", "tensor"),
        P("tensor", "dp"),
        P(),
        P(),
        P(),
        P(),
        P(),
        P(None, None, "dp", "tensor"),
        P(None, "tensor", "dp"),
    )
    return jax.shard_map(
        per_device, mesh=mesh, in_specs=in_specs, out_specs=out_specs, check_vma=False
    )
```

```python
import functools

import jax
import jax.numpy as jnp
from jax import lax
from jax.experimental import pallas as pl
from jax.experimental.pallas import tpu as pltpu
from jax.sharding import PartitionSpec as P

HEAD = 64
NF = 8
NSEG = 13
NE = 12
PAD = 256
BLOCK = 256
SLICES = 4
MIX = 12
TILE = 256
GROUPS = 2

epsilon = 1e-06
HIGHEST = lax.Precision.HIGHEST
F32 = jnp.float32
BF16 = jnp.bfloat16
MESH = pl.DeviceIdType.MESH


def dot_nn(a, b):
    return lax.dot_general(a, b, (((1,), (0,)), ((), ())), preferred_element_type=F32)


def dot_nt(a, b):
    return lax.dot_general(a, b, (((1,), (1,)), ((), ())), preferred_element_type=F32)


def dot_tn(a, b):
    return lax.dot_general(a, b, (((0,), (0,)), ((), ())), preferred_element_type=F32)


def normed(values, gain_vector):
    return (
        values
        * lax.rsqrt(jnp.mean(values * values, axis=-1, keepdims=True) + epsilon)
        * gain_vector
    )


def tree_positions(segment, parent):
    token_count = segment.shape[0]
    labels = jnp.arange(NSEG, dtype=jnp.int32)
    own_hot = (segment[:, None] == labels[None, :]).astype(jnp.int32)
    parent_hot = (parent[:, None] == labels[None, :]).astype(jnp.int32)
    lengths = jnp.sum(own_hot, axis=0)
    starts = jnp.cumsum(lengths) - lengths
    own_start = jnp.sum(own_hot * starts[None, :], axis=1)
    parent_length = jnp.sum(parent_hot * lengths[None, :], axis=1)
    position_index = jnp.arange(token_count, dtype=jnp.int32)
    return (
        position_index
        - own_start
        + jnp.where(segment > 0, lengths[0], 0)
        + jnp.where(parent > 0, parent_length, 0)
    )


def rotary_angles(segment, parent):
    angle_rate = 10000.0 ** (-2.0 * jnp.arange(HEAD // 2, dtype=F32) / HEAD)
    angles = tree_positions(segment, parent).astype(F32)[:, None] * angle_rate[None, :]
    return jnp.concatenate([jnp.cos(angles), jnp.sin(angles)], axis=1)


def swap(values, axis, bits):
    size = lax.axis_size(axis)
    return lax.ppermute(values, axis, [(i, i ^ bits) for i in range(size)])


def gather_tensor(own):
    index = lax.axis_index("tensor")
    far = swap(own, "tensor", 2)
    near = swap(own, "tensor", 1)
    far_near = swap(far, "tensor", 1)
    core, chip = index % 2 == 0, index // 2 == 0
    here = [jnp.where(core, own, near), jnp.where(core, near, own)]
    there = [jnp.where(core, far, far_near), jnp.where(core, far_near, far)]
    order = [jnp.where(chip, h, t) for h, t in zip(here, there)]
    order += [jnp.where(chip, t, h) for h, t in zip(here, there)]
    return jnp.concatenate(order, axis=0)


def scatter_tensor(parts, rows):
    index = lax.axis_index("tensor")

    def take(which):
        return lax.dynamic_slice_in_dim(parts, which * rows, rows, 0).astype(F32)

    near = swap(
        jnp.concatenate([take(index ^ 1), take(index ^ 3)], axis=0).astype(BF16), "tensor", 1
    ).astype(F32)
    mine = take(index) + near[:rows]
    other = take(index ^ 2) + near[rows:]
    return mine + swap(other.astype(BF16), "tensor", 2).astype(F32)


def together(*values):
    return lax.optimization_barrier(values)


def column_groups():
    size = lax.axis_size("dp")
    return [list(range(first, size, 2)) for first in range(2)]


def gather_column(own):
    return lax.all_gather(own, "dp", axis=0, tiled=False, axis_index_groups=column_groups())


def scatter_column(parts):
    return lax.psum_scatter(
        parts, "dp", scatter_dimension=0, tiled=False, axis_index_groups=column_groups()
    )


def by_parity(mine, other):
    even = lax.axis_index("dp") % 2 == 0
    return jnp.stack([jnp.where(even, mine, other), jnp.where(even, other, mine)])


def gather_pair(own):
    half = own.shape[0] // 2
    far, across = swap(own, "tensor", 2), swap(own, "dp", 1)
    corner = jnp.concatenate(
        [swap(across[:half], "tensor", 2), swap(far[half:], "dp", 1)], axis=0
    )
    near = [swap(piece, "tensor", 1) for piece in (own, far, across, corner)]
    return [own, near[0], far, near[1], across, near[2], corner, near[3]]


def scatter_pair(keep, send):
    half = keep.shape[1] // 2
    keep = keep.astype(F32) + swap(send, "tensor", 1).astype(F32)
    mine, far, across, corner = keep[0], keep[1], keep[2], keep[3].astype(BF16)
    from_far = swap(corner[:half], "tensor", 2).astype(F32)
    from_across = swap(corner[half:], "dp", 1).astype(F32)
    far = jnp.concatenate([far[:half], far[half:] + from_across], axis=0).astype(BF16)
    across = jnp.concatenate([across[:half] + from_far, across[half:]], axis=0).astype(BF16)
    return mine + swap(far, "tensor", 2).astype(F32) + swap(across, "dp", 1).astype(F32)


def sum_all(values):
    if lax.axis_size("dp") != 8:
        return lax.psum(values, ("dp", "tensor"))
    for axis, bits in (("tensor", 1), ("tensor", 2), ("dp", 1), ("dp", 2), ("dp", 4)):
        values = values + swap(values, axis, bits)
    return values


def swap_halves(values):
    lane = lax.broadcasted_iota(jnp.int32, values.shape, 1)
    half = HEAD // 2
    return jnp.where(
        lane % HEAD < half, pltpu.roll(values, PAD - half, 1), pltpu.roll(values, half, 1)
    )


def rotation(angles):
    half = HEAD // 2
    source = lax.broadcasted_iota(jnp.int32, (2 * half, PAD), 0)
    lane = lax.broadcasted_iota(jnp.int32, (2 * half, PAD), 1)
    to_cos = (source == lane % half).astype(F32)
    to_sin = jnp.where(
        source == half + lane % half, jnp.where(lane % HEAD < half, -1.0, 1.0), 0.0
    )
    return [
        lax.dot_general(
            angles, where, (((1,), (0,)), ((), ())), precision=HIGHEST, preferred_element_type=F32
        )
        for where in (to_cos, to_sin)
    ]


def project_kernel(columns, tok_ref, gain_ref, angle_ref, pack_ref, *refs):
    q_ref, k_ref, v_ref, kt_ref, vt_ref, one_ref = refs[:6]
    if columns:
        head_ref, gathered, shards, send_sems, recv_sems = refs[6:]
    else:
        head_ref, (gathered, send_sems, recv_sems) = pack_ref, refs[6:]
    near, far, across, *column = enter(columns)
    copies = Copies(send_sems, recv_sems)
    dp, tensor = lax.axis_index("dp"), lax.axis_index("tensor")
    rows, width = tok_ref.shape
    share = pack_ref.shape[0]
    heads, last = [], []
    if columns:
        heads = [copies.start(pack_ref, shards.at[dp], device) for device in column]
        last.append(copies.start(pack_ref, shards.at[dp], across))
        shards[dp] = pack_ref[...]
    size = rows // SLICES
    slices = [pl.ds(c * size, size) for c in range(SLICES)]
    far_moves, near_moves = [], []
    for at in slices:
        values = tok_ref[at, :].astype(F32)
        scale = lax.rsqrt(jnp.mean(values * values, axis=1, keepdims=True) + epsilon)
        gathered[0, at, :] = (values * scale * gain_ref[...]).astype(BF16)
        far_moves.append(copies.start(gathered.at[0, at], gathered.at[2, at], far))
        near_moves.append(copies.start(gathered.at[0, at], gathered.at[1, at], near))
    corner_moves = []
    for c, at in enumerate(slices):
        far_moves[c].wait_recv()
        corner_moves.append(copies.start(gathered.at[2, at], gathered.at[3, at], near))
        if c < len(heads):
            heads[c].wait_recv()
            origin = lax.rem(dp + 8 - 2 * (c + 1), 8)
            last.append(copies.start(shards.at[origin], shards.at[origin], across))
    for move in last + near_moves + corner_moves:
        move.wait_recv()
    if columns:
        for d in range(8):
            at = pl.ds(d * share, share)
            piece = shards[d]
            for section in range(4):
                head_ref[at, section * PAD : section * PAD + 128] = piece[
                    :, section * 128 : (section + 1) * 128
                ]
                start = 512 + 128 * (section // 2)
                rest = piece[:, start : start + 128].astype(F32)
                if section % 2:
                    rest = pltpu.roll(rest, 64, 1)
                lane = lax.broadcasted_iota(jnp.int32, rest.shape, 1)
                head_ref[at, section * PAD + 128 : (section + 1) * PAD] = jnp.where(
                    lane < 64, rest, 0.0
                ).astype(BF16)
    for bits in range(4):
        start = pl.multiple_of(other(tensor, bits) * rows, rows)
        at = pl.ds(start, rows)
        values = gathered[bits]
        one_ref[at, :] = values
        cosine, sine = rotation(angle_ref[at, :])
        part = dot_nn(values, head_ref[:, :PAD])
        q_ref[at, :] = ((part * cosine + swap_halves(part) * sine) * HEAD**-0.5).astype(BF16)
        part = dot_nn(values, head_ref[:, PAD : 2 * PAD])
        part = part * cosine + swap_halves(part) * sine
        k_ref[at, :] = part.astype(BF16)
        kt_ref[:, at] = part.T.astype(BF16)
        part = dot_nn(values, head_ref[:, 2 * PAD : 3 * PAD])
        v_ref[at, :] = part.astype(BF16)
        vt_ref[:, at] = part.T.astype(BF16)
    copies.finish()


def project(columns, tokens, gain, angles, pack):
    rows, width = tokens.shape
    total = angles.shape[0]
    vmem = pl.BlockSpec(memory_space=pltpu.VMEM)
    copies = 3 * SLICES + 7
    wide = jax.ShapeDtypeStruct((total, PAD), BF16)
    tall = jax.ShapeDtypeStruct((PAD, total), BF16)
    shapes = [wide, wide, wide, tall, tall, jax.ShapeDtypeStruct((total, width), BF16)]
    scratch = [pltpu.VMEM((4, rows, width), BF16)]
    if columns:
        shapes.append(jax.ShapeDtypeStruct((width, 4 * PAD), BF16))
        scratch.append(pltpu.VMEM((8, *pack.shape), BF16))
    out = pl.pallas_call(
        functools.partial(project_kernel, columns),
        in_specs=[vmem] * 4,
        out_specs=[vmem] * len(shapes),
        out_shape=shapes,
        scratch_shapes=scratch
        + [pltpu.SemaphoreType.DMA((copies,)), pltpu.SemaphoreType.DMA((copies,))],
        compiler_params=pltpu.CompilerParams(
            collective_id=3, has_side_effects=True, vmem_limit_bytes=56 << 20
        ),
        cost_estimate=pl.CostEstimate(
            flops=6 * total * width * PAD, bytes_accessed=16 * total * width, transcendentals=0
        ),
    )(tokens, gain[None], angles, pack)
    return out if columns else [*out, pack]


def head_mask(values, head):
    lane = lax.broadcasted_iota(jnp.int32, values.shape, 1)
    return jnp.where(lane // HEAD == head, values, jnp.zeros_like(values))


def seen(i, j, seg_row, par_row, seg_col):
    key_at = j * BLOCK + lax.broadcasted_iota(jnp.int32, (BLOCK, 1), 0)
    query_at = i * BLOCK + lax.broadcasted_iota(jnp.int32, (1, BLOCK), 1)
    related = (seg_col == seg_row) | (seg_col == par_row) | (seg_col == 0)
    return related & (key_at <= query_at)


def attend_kernel(heads, q_ref, k_ref, vt_ref, rowinfo_ref, colinfo_ref, o_ref, total_ref):
    i = pl.program_id(0)
    queries = q_ref[...]
    by_head = [head_mask(queries, h) for h in range(heads)]
    seg_row, par_row = rowinfo_ref[0:1, :], rowinfo_ref[1:2, :]

    def step(j, carry):
        at = pl.ds(pl.multiple_of(j * BLOCK, BLOCK), BLOCK)
        keys = k_ref[at, :]
        visible = seen(i, j, seg_row, par_row, colinfo_ref[at, 0:1])
        out = []
        for h in range(heads):
            top, total, mixed = carry[h]
            scores = jnp.where(visible, dot_nt(keys, by_head[h]), -1e30)
            new_top = jnp.maximum(top, jnp.max(scores, axis=0, keepdims=True))
            shrink = jnp.exp(top - new_top)
            probs = jnp.exp(scores - new_top)
            total = total * shrink + jnp.sum(probs, axis=0, keepdims=True)
            mixed = mixed * shrink + dot_nn(
                vt_ref[h * HEAD : (h + 1) * HEAD, at], probs.astype(BF16)
            )
            out.append((new_top, total, mixed))
        return tuple(out)

    start = tuple(
        (
            jnp.full((1, BLOCK), -1e30, F32),
            jnp.zeros((1, BLOCK), F32),
            jnp.zeros((HEAD, BLOCK), F32),
        )
        for _ in range(heads)
    )
    done = lax.fori_loop(0, i + 1, step, start)
    mixed = [m / t for _, t, m in done] + [jnp.zeros((PAD - heads * HEAD, BLOCK), F32)]
    o_ref[...] = jnp.concatenate(mixed, axis=0).T.astype(BF16)
    total_ref[...] = jnp.concatenate(
        [m + jnp.log(t) for m, t, _ in done] + [jnp.zeros((8 - heads, BLOCK), F32)], axis=0
    )


def attend(heads, queries, keys, values_t, rowinfo, colinfo):
    rows = queries.shape[0]
    whole = lambda a: pl.BlockSpec(a.shape, lambda i: (0,) * a.ndim)
    return pl.pallas_call(
        functools.partial(attend_kernel, heads),
        grid=(rows // BLOCK,),
        in_specs=[
            pl.BlockSpec((BLOCK, PAD), lambda i: (i, 0)),
            whole(keys),
            whole(values_t),
            pl.BlockSpec((8, BLOCK), lambda i: (0, i)),
            whole(colinfo),
        ],
        out_specs=[
            pl.BlockSpec((BLOCK, PAD), lambda i: (i, 0)),
            pl.BlockSpec((8, BLOCK), lambda i: (0, i)),
        ],
        out_shape=[
            jax.ShapeDtypeStruct((rows, PAD), BF16),
            jax.ShapeDtypeStruct((8, rows), F32),
        ],
        compiler_params=pltpu.CompilerParams(vmem_limit_bytes=32 << 20),
        cost_estimate=pl.CostEstimate(
            flops=heads * rows * rows * 512, bytes_accessed=8 * rows * PAD, transcendentals=0
        ),
    )(queries, keys, values_t, rowinfo, colinfo)


def attend_back_kernel(
    heads,
    q_ref,
    g_ref,
    o_ref,
    k_ref,
    v_ref,
    kt_ref,
    rowinfo_ref,
    colinfo_ref,
    total_ref,
    angle_ref,
    grad_ref,
    key_sum,
    value_sum,
    query_sum,
):
    i = pl.program_id(0)
    here = pl.ds(pl.multiple_of(i * BLOCK, BLOCK), BLOCK)

    @pl.when(i == 0)
    def _():
        key_sum[...] = jnp.zeros_like(key_sum)
        value_sum[...] = jnp.zeros_like(value_sum)

    query_sum[...] = jnp.zeros_like(query_sum)
    queries, grads = q_ref[...], g_ref[...]
    q_heads = [head_mask(queries, h) for h in range(heads)]
    g_heads = [head_mask(grads, h) for h in range(heads)]
    seg_row, par_row = rowinfo_ref[0:1, :], rowinfo_ref[1:2, :]
    product = grads.astype(F32) * o_ref[...].astype(F32)
    lane = lax.broadcasted_iota(jnp.int32, (8, PAD), 1)
    which = lax.broadcasted_iota(jnp.int32, (8, PAD), 0)
    delta = lax.dot_general(
        (lane // HEAD == which).astype(F32),
        product,
        (((1,), (1,)), ((), ())),
        precision=HIGHEST,
        preferred_element_type=F32,
    )
    totals = total_ref[...]

    def step(j, carry):
        at = pl.ds(pl.multiple_of(j * BLOCK, BLOCK), BLOCK)
        keys, values = k_ref[at, :], v_ref[at, :]
        visible = seen(i, j, seg_row, par_row, colinfo_ref[at, 0:1])
        key_part, value_part = key_sum[at, :], value_sum[at, :]
        for h in range(heads):
            scores = jnp.where(visible, dot_nt(keys, q_heads[h]), -1e30)
            probs = jnp.exp(scores - totals[h : h + 1, :])
            value_part = value_part + dot_nn(probs.astype(BF16), g_heads[h])
            grad_probs = dot_nt(values, g_heads[h])
            grad_scores = (probs * (grad_probs - delta[h : h + 1, :])).astype(BF16)
            key_part = key_part + dot_nn(grad_scores, q_heads[h])
            lanes = slice(h * HEAD, (h + 1) * HEAD)
            query_sum[lanes, :] += dot_nn(kt_ref[lanes, at], grad_scores)
        key_sum[at, :] = key_part
        value_sum[at, :] = value_part
        return carry

    lax.fori_loop(0, i + 1, step, 0)
    def turned_back(values, at):
        cosine, sine = rotation(angle_ref[at, :])
        return (values * cosine - swap_halves(values) * sine).astype(BF16)

    grad_ref[here, :PAD] = turned_back(query_sum[...].T * HEAD**-0.5, here)

    @pl.when(i == pl.num_programs(0) - 1)
    def _():
        def finish(j, carry):
            at = pl.ds(pl.multiple_of(j * BLOCK, BLOCK), BLOCK)
            grad_ref[at, PAD : 2 * PAD] = turned_back(key_sum[at, :], at)
            grad_ref[at, 2 * PAD :] = value_sum[at, :].astype(BF16)
            return carry

        lax.fori_loop(0, pl.num_programs(0), finish, 0)


def attend_back(heads, queries, grads, out, keys, values, keys_t, rowinfo, colinfo, totals, angles):
    rows = queries.shape[0]
    whole = lambda a: pl.BlockSpec(a.shape, lambda i: (0,) * a.ndim)
    row_spec = pl.BlockSpec((BLOCK, PAD), lambda i: (i, 0))
    return pl.pallas_call(
        functools.partial(attend_back_kernel, heads),
        grid=(rows // BLOCK,),
        in_specs=[
            row_spec,
            row_spec,
            row_spec,
            whole(keys),
            whole(values),
            whole(keys_t),
            pl.BlockSpec((8, BLOCK), lambda i: (0, i)),
            whole(colinfo),
            pl.BlockSpec((8, BLOCK), lambda i: (0, i)),
            whole(angles),
        ],
        out_specs=pl.BlockSpec((rows, 3 * PAD), lambda i: (0, 0)),
        out_shape=jax.ShapeDtypeStruct((rows, 3 * PAD), BF16),
        scratch_shapes=[
            pltpu.VMEM((rows, PAD), F32),
            pltpu.VMEM((rows, PAD), F32),
            pltpu.VMEM((PAD, BLOCK), F32),
        ],
        compiler_params=pltpu.CompilerParams(vmem_limit_bytes=60 << 20),
        cost_estimate=pl.CostEstimate(
            flops=heads * rows * rows * 1280, bytes_accessed=16 * rows * PAD, transcendentals=0
        ),
    )(queries, grads, out, keys, values, keys_t, rowinfo, colinfo, totals, angles)


def other(place, bits):
    if bits & 2:
        place = place + 2 - 4 * lax.rem(lax.div(place, 2), 2)
    if bits & 1:
        place = place + 1 - 2 * lax.rem(place, 2)
    return place


def enter(columns=False):
    dp, tensor = lax.axis_index("dp"), lax.axis_index("tensor")
    others = [(dp, other(tensor, 1)), (dp, other(tensor, 2)), (other(dp, 1), tensor)]
    if columns:
        others += [(lax.rem(dp + 2 * j, 8), tensor) for j in (1, 2, 3)]
    barrier = pltpu.get_barrier_semaphore()
    for device in others:
        pl.semaphore_signal(barrier, inc=1, device_id=device, device_id_type=MESH)
    pl.semaphore_wait(barrier, len(others))
    return others


class Copies:
    def __init__(self, send_sems, recv_sems):
        self.send_sems, self.recv_sems, self.made = send_sems, recv_sems, []

    def start(self, source, target, device):
        k = len(self.made)
        copy = pltpu.make_async_remote_copy(
            src_ref=source,
            dst_ref=target,
            send_sem=self.send_sems.at[k],
            recv_sem=self.recv_sems.at[k],
            device_id=device,
            device_id_type=MESH,
        )
        copy.start()
        self.made.append(copy)
        return copy

    def finish(self):
        for copy in self.made:
            copy.wait_send()


def quarter(ref, bits, rows):
    place = other(lax.axis_index("tensor"), bits)
    return ref.at[pl.ds(pl.multiple_of(place * rows, rows), rows)]


def sum_of_quarters(part, copies, near, far, near_send, near_recv, far_send, far_recv):
    rows = far_send.shape[0]
    near_send[0] = part(3).astype(BF16)
    first = copies.start(near_send.at[0], near_recv.at[0], near)
    near_send[1] = part(1).astype(BF16)
    second = copies.start(near_send.at[1], near_recv.at[1], near)
    mine = part(2)
    first.wait_recv()
    far_send[...] = (mine + near_recv[0].astype(F32)).astype(BF16)
    moves = []
    for c in range(SLICES):
        at = pl.ds(c * rows // SLICES, rows // SLICES)
        moves.append(copies.start(far_send.at[at], far_recv.at[at], far))
    mine = part(0)
    second.wait_recv()
    return mine + near_recv[1].astype(F32), moves


def branch_kernel(
    att_ref, out_ref, tok_ref, gain_ref, carried_ref, mix_ref, picked_ref,
    hidden_ref, aux_ref, rows_ref,
    near_send, near_recv, far_send, far_recv, own, send_sems, recv_sems, local_sems,
):
    near, far, across = enter()
    copies = Copies(send_sems, recv_sems)
    rows, width = tok_ref.shape
    weights = out_ref[...]

    def part(bits):
        return dot_nt(quarter(att_ref, bits, rows)[...], weights)

    mine, moves = sum_of_quarters(
        part, copies, near, far, near_send, near_recv, far_send, far_recv
    )
    hidden_ref[...] = tok_ref[...].astype(F32) + mine
    size = rows // SLICES
    slices = [pl.ds(c * size, size) for c in range(SLICES)]
    from_far, from_across, ends, locals_ = [], [], [], []
    for c, at in enumerate(slices):
        moves[c].wait_recv()
        hidden = hidden_ref[at, :] + far_recv[at, :].astype(F32)
        hidden_ref[at, :] = hidden
        scale = lax.rsqrt(jnp.mean(hidden * hidden, axis=1, keepdims=True) + epsilon)
        normed_two = hidden * scale * gain_ref[...]
        logits = carried_ref[at, :] + lax.dot_general(
            normed_two,
            mix_ref[...],
            (((1,), (0,)), ((), ())),
            precision=HIGHEST,
            preferred_element_type=F32,
        )
        picked = picked_ref[at, :] > 0
        top = jnp.max(jnp.where(picked, logits, -1e30), axis=1, keepdims=True)
        weight = jnp.where(picked, jnp.exp(jnp.where(picked, logits - top, 0.0)), 0.0)
        gate = weight / jnp.sum(weight, axis=1, keepdims=True)
        lane = lax.broadcasted_iota(jnp.int32, logits.shape, 1)
        turned = jnp.where(
            lane % 2 == 0, pltpu.roll(logits, 127, 1), pltpu.roll(logits, 1, 1)
        )
        top = jnp.maximum(logits, turned)
        mixture = jnp.exp(logits - top) / (jnp.exp(logits - top) + jnp.exp(turned - top))
        aux_ref[at, :] = jnp.where(lane < MIX, gate, jnp.where(lane < MIX + 4, mixture, 0.0))
        own[at, :width] = normed_two.astype(BF16)
        own[at, width:] = jnp.where(lane < NF, gate, 0.0).astype(BF16)
        from_far.append(copies.start(own.at[at], rows_ref.at[2, at], far))
        from_across.append(copies.start(own.at[at], rows_ref.at[4, at], across))
        ends.append(copies.start(own.at[at], rows_ref.at[1, at], near))
        local = pltpu.make_async_copy(own.at[at], rows_ref.at[0, at], local_sems.at[c])
        local.start()
        locals_.append(local)
    corner = []
    for c, at in enumerate(slices):
        from_far[c].wait_recv()
        if c >= SLICES // 2:
            corner.append(copies.start(rows_ref.at[2, at], rows_ref.at[6, at], across))
        ends.append(copies.start(rows_ref.at[2, at], rows_ref.at[3, at], near))
        from_across[c].wait_recv()
        if c < SLICES // 2:
            corner.append(copies.start(rows_ref.at[4, at], rows_ref.at[6, at], far))
        ends.append(copies.start(rows_ref.at[4, at], rows_ref.at[5, at], near))
    for c, at in enumerate(slices):
        corner[c].wait_recv()
        ends.append(copies.start(rows_ref.at[6, at], rows_ref.at[7, at], near))
    for copy in ends:
        copy.wait_recv()
    for local in locals_:
        local.wait()
    copies.finish()


def branch(attended, head_full, tokens, gain, carried, mix, picked):
    rows, width = tokens.shape
    vmem = pl.BlockSpec(memory_space=pltpu.VMEM)
    copies = 2 + 8 * SLICES
    return pl.pallas_call(
        branch_kernel,
        in_specs=[vmem] * 7,
        out_specs=[vmem, vmem, pl.BlockSpec(memory_space=pl.ANY)],
        out_shape=[
            jax.ShapeDtypeStruct((rows, width), F32),
            jax.ShapeDtypeStruct((rows, 128), F32),
            jax.ShapeDtypeStruct((8, rows, width + 128), BF16),
        ],
        scratch_shapes=[
            pltpu.VMEM((2, rows, width), BF16),
            pltpu.VMEM((2, rows, width), BF16),
            pltpu.VMEM((rows, width), BF16),
            pltpu.VMEM((rows, width), BF16),
            pltpu.VMEM((rows, width + 128), BF16),
            pltpu.SemaphoreType.DMA((copies,)),
            pltpu.SemaphoreType.DMA((copies,)),
            pltpu.SemaphoreType.DMA((SLICES,)),
        ],
        compiler_params=pltpu.CompilerParams(
            collective_id=1, has_side_effects=True, vmem_limit_bytes=40 << 20
        ),
        cost_estimate=pl.CostEstimate(
            flops=16 * rows * width * PAD, bytes_accessed=64 * rows * width, transcendentals=0
        ),
    )(attended, head_full[:, 3 * PAD :], tokens, gain[None], carried, mix, picked)


def branch_back_kernel(
    hidden_ref, aux_ref, cot_ref, gain_ref, mix_ref, vector_ref, carried_ref, att_ref, out_ref,
    keep_ref, send_ref,
    grad_hidden_ref, grad_logits_ref, grad_att_ref, grad_out_ref, small_ref,
    kept, near_recv, corner_send, corner_recv, far_send, far_recv, across_send, across_recv,
    total, normed_two, base, gathered, send_sems, recv_sems, local_sems,
):
    near, far, across = enter()
    copies = Copies(send_sems, recv_sems)
    rows, width = hidden_ref.shape
    half = rows // 2
    halves = [pl.ds(0, half), pl.ds(half, half)]
    order = (3, 1, 2, 0)
    arrivals, locals_ = {}, {}
    for b in order:
        arrivals[b] = copies.start(send_ref.at[b], near_recv.at[b], near)
        locals_[b] = pltpu.make_async_copy(keep_ref.at[b], kept.at[b], local_sems.at[b])
        locals_[b].start()

    gain = gain_ref[...]
    lane = lax.broadcasted_iota(jnp.int32, (half, 128), 1)

    def column(values, at):
        return jnp.sum(jnp.where(lane == at, values, 0.0), axis=1, keepdims=True)

    known = []
    for at in halves:
        hidden, aux, grads = hidden_ref[at, :], aux_ref[at, :], cot_ref[at, :].astype(F32)
        scale = lax.rsqrt(jnp.mean(hidden * hidden, axis=1, keepdims=True) + epsilon)
        normed = hidden * scale * gain
        normed_two[at, :] = normed
        gates = [column(aux, NF + 1 + k) for k in range(3)]
        mixes = [column(aux, MIX + k) for k in range(4)]
        along = jnp.sum(grads * normed, axis=1, keepdims=True)
        vectors = [
            jnp.sum(grads * vector_ref[c : c + 1, :], axis=1, keepdims=True) for c in range(2)
        ]
        base[at, :] = grads * (gates[0] + gates[1] * mixes[0] + gates[2] * mixes[2])
        sums = []
        for c in range(2):
            sums.append(
                jnp.sum(grads * (gates[1 + c] * mixes[2 * c + 1]), axis=0, keepdims=True)
            )
        by_gate = jnp.where(lane == NF + 1, along, 0.0)
        by_mix = jnp.zeros((half, 128), F32)
        for c in range(2):
            first, second = mixes[2 * c], mixes[2 * c + 1]
            by_gate = by_gate + jnp.where(
                lane == NF + 2 + c, first * along + second * vectors[c], 0.0
            )
            d_first, d_second = gates[1 + c] * along, gates[1 + c] * vectors[c]
            inner = first * d_first + second * d_second
            by_mix = by_mix + jnp.where(lane == MIX + 2 * c, first * (d_first - inner), 0.0)
            by_mix = by_mix + jnp.where(lane == MIX + 2 * c + 1, second * (d_second - inner), 0.0)
        known.append((scale, by_gate, by_mix, sums))

    def joined(b, at):
        return kept[b, at, :].astype(F32) + near_recv[b, at, :].astype(F32)

    def arrived(b):
        arrivals[b].wait_recv()
        locals_[b].wait()

    arrived(3)
    corner_send[...] = (kept[3].astype(F32) + near_recv[3].astype(F32)).astype(BF16)
    corner_far = copies.start(corner_send.at[halves[0]], corner_recv.at[0], far)
    corner_across = copies.start(corner_send.at[halves[1]], corner_recv.at[1], across)
    from_far, from_across = {}, {}
    arrived(1)
    far_send[halves[0], :] = joined(1, halves[0]).astype(BF16)
    from_far[0] = copies.start(far_send.at[halves[0]], far_recv.at[halves[0]], far)
    arrived(2)
    across_send[halves[1], :] = joined(2, halves[1]).astype(BF16)
    from_across[1] = copies.start(across_send.at[halves[1]], across_recv.at[halves[1]], across)
    corner_far.wait_recv()
    across_send[halves[0], :] = (
        joined(2, halves[0]) + corner_recv[0].astype(F32)
    ).astype(BF16)
    from_across[0] = copies.start(across_send.at[halves[0]], across_recv.at[halves[0]], across)
    corner_across.wait_recv()
    far_send[halves[1], :] = (joined(1, halves[1]) + corner_recv[1].astype(F32)).astype(BF16)
    from_far[1] = copies.start(far_send.at[halves[1]], far_recv.at[halves[1]], far)
    arrived(0)
    total[...] = kept[0].astype(F32) + near_recv[0].astype(F32)

    gain_sum = jnp.zeros((1, width), F32)
    far_moves, near_moves = [], []
    for h, at in enumerate(halves):
        from_far[h].wait_recv()
        from_across[h].wait_recv()
        scale, by_gate, by_mix, _ = known[h]
        incoming = total[at, :] + far_recv[at, :].astype(F32) + across_recv[at, :].astype(F32)
        by_gate = by_gate + jnp.where(lane < NF, incoming[:, width:], 0.0)
        gates = jnp.where(lane < MIX, aux_ref[at, :], 0.0)
        grad_logits = by_mix + gates * (
            by_gate - jnp.sum(gates * by_gate, axis=1, keepdims=True)
        )
        grad_logits_ref[at, :] = grad_logits
        grad_normed = incoming[:, :width] + base[at, :] + lax.dot_general(
            grad_logits,
            mix_ref[...],
            (((1,), (1,)), ((), ())),
            precision=HIGHEST,
            preferred_element_type=F32,
        )
        hidden = hidden_ref[at, :]
        gain_sum = gain_sum + jnp.sum(hidden * scale * grad_normed, axis=0, keepdims=True)
        weighted = gain * grad_normed
        inner = jnp.mean(hidden * weighted, axis=1, keepdims=True)
        grad_hidden = (
            cot_ref[at, :].astype(F32) + scale * weighted - hidden * (scale * scale * scale * inner)
        )
        grad_hidden_ref[at, :] = grad_hidden
        gathered[0, at, :] = grad_hidden.astype(BF16)
        far_moves.append(copies.start(gathered.at[0, at], gathered.at[2, at], far))
        near_moves.append(copies.start(gathered.at[0, at], gathered.at[1, at], near))
    def over_tokens(a, b):
        return lax.dot_general(
            a, b, (((0,), (0,)), ((), ())), precision=HIGHEST, preferred_element_type=F32
        )

    small_ref[...] = jnp.zeros_like(small_ref)
    small_ref[:16, :width] = over_tokens(grad_logits_ref[...], normed_two[...])[:16]
    small_ref[16:, :width] = jnp.concatenate(
        [gain_sum] + [known[0][3][c] + known[1][3][c] for c in range(2)]
        + [jnp.zeros((5, width), F32)],
        axis=0,
    )
    small_ref[:16, width:] = over_tokens(carried_ref[...], grad_logits_ref[...])[:16]

    def project_back(bits, first):
        values = gathered[bits]
        quarter(grad_att_ref, bits, rows)[...] = dot_nn(values, out_ref[...]).astype(BF16)
        product = dot_tn(values, quarter(att_ref, bits, rows)[...])
        grad_out_ref[...] = product if first else grad_out_ref[...] + product

    project_back(0, True)
    for move in near_moves:
        move.wait_recv()
    project_back(1, False)
    last = []
    for h, at in enumerate(halves):
        far_moves[h].wait_recv()
        last.append(copies.start(gathered.at[2, at], gathered.at[3, at], near))
    project_back(2, False)
    for move in last:
        move.wait_recv()
    project_back(3, False)
    copies.finish()


def branch_back(hidden, aux, cotangent, gain, mix, vectors, carried, attended, head_full, keep, send):
    rows, width = hidden.shape
    wide = keep.shape[2]
    vmem, anywhere = pl.BlockSpec(memory_space=pltpu.VMEM), pl.BlockSpec(memory_space=pl.ANY)
    copies = 16
    return pl.pallas_call(
        branch_back_kernel,
        in_specs=[vmem] * 9 + [anywhere] * 2,
        out_specs=[vmem] * 5,
        out_shape=[
            jax.ShapeDtypeStruct((rows, width), F32),
            jax.ShapeDtypeStruct((rows, 128), F32),
            jax.ShapeDtypeStruct(attended.shape, BF16),
            jax.ShapeDtypeStruct((width, PAD), F32),
            jax.ShapeDtypeStruct((24, width + 128), F32),
        ],
        scratch_shapes=[
            pltpu.VMEM((4, rows, wide), BF16),
            pltpu.VMEM((4, rows, wide), BF16),
            pltpu.VMEM((rows, wide), BF16),
            pltpu.VMEM((2, rows // 2, wide), BF16),
            pltpu.VMEM((rows, wide), BF16),
            pltpu.VMEM((rows, wide), BF16),
            pltpu.VMEM((rows, wide), BF16),
            pltpu.VMEM((rows, wide), BF16),
            pltpu.VMEM((rows, wide), F32),
            pltpu.VMEM((rows, width), F32),
            pltpu.VMEM((rows, width), F32),
            pltpu.VMEM((4, rows, width), BF16),
            pltpu.SemaphoreType.DMA((copies,)),
            pltpu.SemaphoreType.DMA((copies,)),
            pltpu.SemaphoreType.DMA((4,)),
        ],
        compiler_params=pltpu.CompilerParams(
            collective_id=2, has_side_effects=True, vmem_limit_bytes=60 << 20
        ),
        cost_estimate=pl.CostEstimate(
            flops=32 * rows * width * PAD, bytes_accessed=64 * rows * width, transcendentals=0
        ),
    )(
        hidden, aux, cotangent, gain[None], mix, vectors, carried, attended, head_full[:, 3 * PAD :],
        keep, send,
    )


def finish_kernel(
    columns, grad_ref, one_ref, head_ref, grad_out_ref, small_ref, grad_hidden_ref, tok_ref, gain_ref,
    *refs
):
    grad_tok_ref, pack_ref, sum_ref, refs = refs[0], refs[1], refs[2], refs[3:]
    near_send, near_recv, far_send, far_recv, send_sems, recv_sems = refs[:6]
    near, far, across, *column = enter(columns)
    copies = Copies(send_sems, recv_sems)
    dp = lax.axis_index("dp")
    rows, width = tok_ref.shape
    share = width // 8

    def part(bits):
        return dot_nt(quarter(grad_ref, bits, rows)[...], head_ref[:, : 3 * PAD])

    mine, moves = sum_of_quarters(
        part, copies, near, far, near_send, near_recv, far_send, far_recv
    )
    grad_tok_ref[...] = mine

    packed = refs[6] if columns else pack_ref
    along = jnp.zeros((8, width), F32)
    rest = None
    for section in range(4):
        at = slice(section * PAD, (section + 1) * PAD)
        if section < 3:
            grad = dot_tn(one_ref[...], grad_ref[:, at])
            along = along + lax.dot_general(
                jnp.ones((8, PAD), F32),
                grad * head_ref[:, at].astype(F32),
                (((1,), (1,)), ((), ())),
                precision=HIGHEST,
                preferred_element_type=F32,
            )
        else:
            grad = grad_out_ref[...]
        if not columns:
            packed[:, at] = grad.astype(BF16)
            continue
        low, high = grad[:, :128].astype(BF16), grad[:, 128:]
        if section % 2 == 0:
            rest = high
        else:
            lane = lax.broadcasted_iota(jnp.int32, high.shape, 1)
            rest = jnp.where(lane < 64, rest, pltpu.roll(high, 64, 1)).astype(BF16)
        for d in range(8):
            cut = slice(d * share, (d + 1) * share)
            packed[d, :, section * 128 : (section + 1) * 128] = low[cut]
            if section % 2:
                start = 512 + 128 * (section // 2)
                packed[d, :, start : start + 128] = rest[cut]
    small = small_ref[...]
    row = lax.broadcasted_iota(jnp.int32, (24, width), 0)
    small = jnp.concatenate(
        [
            jnp.where(row == 19, along[:1] / gain_ref[...], small[:, :width]),
            small[:, width:],
        ],
        axis=1,
    )
    if columns:
        _, pair_recv, column_send, column_recv, sums, sum_recv = refs[6:]
        pair_moves = []
        for j in range(4):
            there = lax.rem(other(dp, 1) + 2 * j, 8)
            pair_moves.append(copies.start(packed.at[there], pair_recv.at[j], across))
        sums[0] = small
        steps = [near, far, across, (other(dp, 2), lax.axis_index("tensor")), column[1]]
        sum_moves = [copies.start(sums.at[0], sum_recv.at[0], steps[0])]

        def add_up():
            k = len(sum_moves)
            sum_moves[-1].wait_recv()
            if k < 5:
                sums[k] = sums[k - 1] + sum_recv[k - 1]
                sum_moves.append(copies.start(sums.at[k], sum_recv.at[k], steps[k]))
            else:
                sum_ref[...] = sums[4] + sum_recv[4]

        add_up()
        add_up()
        column_moves = []
        for j in (1, 2, 3, 0):
            pair_moves[j].wait_recv()
            paired = packed[lax.rem(dp + 2 * j, 8)].astype(F32) + pair_recv[j].astype(F32)
            if j:
                column_send[j - 1] = paired.astype(BF16)
                column_moves.append(
                    copies.start(column_send.at[j - 1], column_recv.at[j - 1], column[j - 1])
                )
            else:
                pack_ref[...] = paired
        add_up()
    else:
        sum_ref[...] = small

    size = rows // SLICES
    for c in range(SLICES):
        at = pl.ds(c * size, size)
        moves[c].wait_recv()
        grad_normed = grad_tok_ref[at, :] + far_recv[at, :].astype(F32)
        values = tok_ref[at, :].astype(F32)
        scale = lax.rsqrt(jnp.mean(values * values, axis=1, keepdims=True) + epsilon)
        weighted = gain_ref[...] * grad_normed
        inner = jnp.mean(values * weighted, axis=1, keepdims=True)
        grad_tok_ref[at, :] = (
            grad_hidden_ref[at, :] + scale * weighted - values * (scale * scale * scale * inner)
        )
    if columns:
        add_up()
        for j in range(3):
            column_moves[j].wait_recv()
            pack_ref[...] = pack_ref[...] + column_recv[j].astype(F32)
        add_up()
    copies.finish()


def finish(columns, grads, ones, head_full, grad_out, small, grad_hidden, tokens, gain):
    rows, width = tokens.shape
    share = width // 8
    vmem = pl.BlockSpec(memory_space=pltpu.VMEM)
    copies = 2 + SLICES + 12
    pack = (
        jax.ShapeDtypeStruct((share, width), F32)
        if columns
        else jax.ShapeDtypeStruct(head_full.shape, BF16)
    )
    scratch = [
        pltpu.VMEM((2, rows, width), BF16),
        pltpu.VMEM((2, rows, width), BF16),
        pltpu.VMEM((rows, width), BF16),
        pltpu.VMEM((rows, width), BF16),
        pltpu.SemaphoreType.DMA((copies,)),
        pltpu.SemaphoreType.DMA((copies,)),
    ]
    if columns:
        scratch += [
            pltpu.VMEM((8, share, width), BF16),
            pltpu.VMEM((4, share, width), BF16),
            pltpu.VMEM((3, share, width), BF16),
            pltpu.VMEM((3, share, width), BF16),
            pltpu.VMEM((5, *small.shape), F32),
            pltpu.VMEM((5, *small.shape), F32),
        ]
    return pl.pallas_call(
        functools.partial(finish_kernel, columns),
        in_specs=[vmem] * 8,
        out_specs=[vmem] * 3,
        out_shape=[
            jax.ShapeDtypeStruct((rows, width), F32),
            pack,
            jax.ShapeDtypeStruct(small.shape, F32),
        ],
        scratch_shapes=scratch,
        compiler_params=pltpu.CompilerParams(
            collective_id=4, has_side_effects=True, vmem_limit_bytes=56 << 20
        ),
        cost_estimate=pl.CostEstimate(
            flops=32 * rows * width * PAD, bytes_accessed=64 * rows * width, transcendentals=0
        ),
    )(grads, ones, head_full, grad_out, small, grad_hidden, tokens, gain[None])


def experts_kernel(
    whole_weights, n_before, base_ref, counts_ref, slot_rows_ref, slot_cols_ref, weights_ref, rows_ref,
    *refs
):
    grads_refs, before_refs, refs = refs[:8], refs[8 : 8 + n_before], refs[8 + n_before :]
    sum_refs, grad_in_refs, out_ref, weight, grad_weight, gates, sems = (
        refs[0:2], refs[2:4], refs[4], refs[5], refs[6], refs[7], refs[8],
    )
    step = pl.program_id(0)
    expert = base_ref[0] + step
    rows, width = grads_refs[0].shape
    copies = [
        pltpu.make_async_copy(source, ref, sems.at[k])
        for k, (source, ref) in enumerate(zip(before_refs, (*sum_refs, *grad_in_refs)))
    ]

    @pl.when(step == 0)
    def _():
        if n_before:
            for copy in copies:
                copy.start()
        else:
            for ref in (*sum_refs, *grad_in_refs):
                ref[...] = jnp.zeros_like(ref)
        for k in range(8):
            at = pl.ds((k % 4) * rows, rows)
            gates[k // 4, :, at] = rows_ref[k, :, width:].astype(F32).T

    grad_weight[...] = jnp.zeros_like(grad_weight)
    if whole_weights:
        weight[...] = weights_ref[0]
    else:
        depth, _, _, _, share, _ = weights_ref.shape
        for z in range(depth):
            for y in range(2):
                weight[:, pl.ds((2 * z + y) * share, share), :] = weights_ref[z, y, 0]

    if n_before:

        @pl.when(step == 0)
        def _():
            for copy in copies:
                copy.wait()

    def tree(a):
        slot_row = slot_rows_ref[a, pl.ds(expert, 1), :]
        gate_row = gates[a, pl.ds(expert, 1), :]

        def tile(c, carry):
            down = c * TILE + lax.broadcasted_iota(jnp.int32, (TILE, 1), 0)
            across = c * TILE + lax.broadcasted_iota(jnp.int32, (1, TILE), 1)
            inputs = jnp.zeros((TILE, width), F32)
            grad_out = jnp.zeros((TILE, width), F32)
            for b in range(4):
                picked = slot_row[:, b * rows : (b + 1) * rows] == down
                gate = gate_row[:, b * rows : (b + 1) * rows]
                inputs = inputs + dot_nn(
                    jnp.where(picked, 1.0, 0.0).astype(BF16), rows_ref[4 * a + b, :, :width]
                )
                grad_out = grad_out + dot_nn(
                    jnp.where(picked, gate, 0.0).astype(BF16), grads_refs[4 * a + b][...]
                )
            inputs, grad_out = inputs.astype(BF16), grad_out.astype(BF16)
            gate_part = dot_nn(inputs, weight[0])
            up_part = dot_nn(inputs, weight[1])
            sigmoid = 1.0 / (1.0 + jnp.exp(-gate_part))
            swish = gate_part * sigmoid
            act = (swish * up_part).astype(BF16)
            expert_out = dot_nt(act, weight[2]).astype(BF16)
            grad_act = dot_nn(grad_out, weight[2])
            grad_gate = (
                grad_act * up_part * sigmoid * (1.0 + gate_part * (1.0 - sigmoid))
            ).astype(BF16)
            grad_up = (grad_act * swish).astype(BF16)
            grad_weight[0] += dot_tn(inputs, grad_gate)
            grad_weight[1] += dot_tn(inputs, grad_up)
            grad_weight[2] += dot_tn(grad_out, act)
            grad_in = (dot_nt(grad_gate, weight[0]) + dot_nt(grad_up, weight[1])).astype(BF16)
            for b in range(4):
                k = 4 * a + b
                lane = lax.broadcasted_iota(jnp.int32, (rows, 8), 1)
                slot_col = jnp.sum(
                    jnp.where(lane == expert, slot_cols_ref[pl.ds(k * rows, rows), :], 0),
                    axis=1,
                    keepdims=True,
                )
                lane = lax.broadcasted_iota(jnp.int32, (rows, 128), 1)
                gate_col = jnp.sum(
                    jnp.where(lane == expert, rows_ref[k, :, width:].astype(F32), 0.0),
                    axis=1,
                    keepdims=True,
                )
                back = jnp.where(slot_col == across, 1.0, 0.0).astype(BF16)
                part = dot_nn(back, expert_out)
                sum_ref, grad_in_ref = sum_refs[b % 2], grad_in_refs[b % 2]
                at = 2 * a + b // 2
                sum_ref[at] = (sum_ref[at].astype(F32) + gate_col * part).astype(BF16)
                along = jnp.sum(part * grads_refs[k][...].astype(F32), axis=1, keepdims=True)
                grad_in_ref[at, :, :width] = (
                    grad_in_ref[at, :, :width].astype(F32) + dot_nn(back, grad_in)
                ).astype(BF16)
                grad_in_ref[at, :, width:] = (
                    grad_in_ref[at, :, width:].astype(F32) + jnp.where(lane == expert, along, 0.0)
                ).astype(BF16)
            return carry

        lax.fori_loop(0, (counts_ref[a, expert] + TILE - 1) // TILE, tile, 0)

    tree(0)
    tree(1)
    if whole_weights:
        out_ref[0] = grad_weight[...].astype(BF16)
    else:
        for z in range(depth):
            for y in range(2):
                at = pl.ds((2 * z + y) * share, share)
                out_ref[z, y, 0] = grad_weight[:, at, :].astype(BF16)


def experts(base, weights, counts, rows, grads, slot_rows, slot_cols, before):
    count, width = grads[0].shape
    wide = rows.shape[2]
    whole_weights = weights.ndim == 4
    kinds, share, hidden = weights.shape[-3:]
    group = weights.shape[0] if whole_weights else weights.shape[2]
    depth = width if whole_weights else 2 * weights.shape[0] * share
    whole = lambda a: pl.BlockSpec(a.shape, lambda e, *_: (0,) * a.ndim, pipeline_mode=pl.Buffered(1))
    if whole_weights:
        weight_spec = pl.BlockSpec((1, kinds, share, hidden), lambda e, *_: (e, 0, 0, 0))
    else:
        weight_spec = pl.BlockSpec(
            (weights.shape[0], 2, 1, kinds, share, hidden), lambda e, *_: (0, 0, e, 0, 0, 0)
        )
    sums = jax.ShapeDtypeStruct((4, count, width), BF16)
    grad_ins = jax.ShapeDtypeStruct((4, count, wide), BF16)
    slots = count * 2
    return pl.pallas_call(
        functools.partial(experts_kernel, whole_weights, len(before)),
        grid_spec=pltpu.PrefetchScalarGridSpec(
            num_scalar_prefetch=2,
            grid=(group,),
            in_specs=[whole(slot_rows), whole(slot_cols), weight_spec, whole(rows)]
            + [whole(a) for a in grads]
            + [pl.BlockSpec(memory_space=pl.ANY) for _ in before],
            out_specs=[whole(sums), whole(sums), whole(grad_ins), whole(grad_ins), weight_spec],
            scratch_shapes=[
                pltpu.VMEM((kinds, depth, hidden), BF16),
                pltpu.VMEM((kinds, depth, hidden), F32),
                pltpu.VMEM((2, wide - width, 4 * count), F32),
                pltpu.SemaphoreType.DMA((4,)),
            ],
        ),
        out_shape=[sums, sums, grad_ins, grad_ins, jax.ShapeDtypeStruct(weights.shape, BF16)],
        compiler_params=pltpu.CompilerParams(vmem_limit_bytes=60 << 20),
        cost_estimate=pl.CostEstimate(
            flops=group * slots * width * (18 * hidden + 32 * count),
            bytes_accessed=64 * count * width,
            transcendentals=0,
        ),
    )(base, counts, slot_rows, slot_cols, weights, rows, *grads, *before)


def per_device(
    tokens_in,
    carried_logits,
    cotangent,
    segment_ids,
    parent_ids,
    routes,
    attention_gain,
    head_weight,
    output_weight,
    expert_gain,
    router_weight,
    carry_weight,
    constant_gate,
    constant_vector,
    expert_first,
    expert_second,
):
    row_count, width = tokens_in.shape
    tree_len = segment_ids.shape[0]
    head_width = head_weight.shape[2]
    heads = head_width // HEAD
    share = head_weight.shape[1]
    parity = lax.axis_index("dp") % 2
    index = lax.axis_index("tensor")
    own_experts = NF // 2
    group = own_experts // GROUPS
    layered = share % 16 == 0

    columns = lax.axis_size("dp") == 8

    sections = jnp.concatenate([head_weight, output_weight.T[None]], axis=0).astype(BF16)
    spread = lambda a, to: jnp.pad(a, ((0, 0), (0, to - a.shape[1])))
    if columns:
        pack = jnp.concatenate(
            [sections[k, :, :128] for k in range(4)] + [sections[k, :, 128:] for k in range(4)], axis=1
        )
    else:
        pack = jnp.concatenate([spread(sections[k], PAD) for k in range(4)], axis=1)
        pack = gather_column(pack)
        pack = jnp.moveaxis(by_parity(pack, swap(pack, "dp", 1)), 0, 1).reshape(width, 4 * PAD)
    expert_pack = jnp.concatenate(
        [expert_first.astype(BF16), expert_second.astype(BF16).transpose(0, 2, 1)[:, None]], axis=1
    )
    expert_weights = []
    kept = lax.dynamic_slice_in_dim(expert_pack, parity * own_experts, own_experts, 0)
    given = lax.dynamic_slice_in_dim(expert_pack, (1 - parity) * own_experts, own_experts, 0)
    shards = []
    for g in range(GROUPS):
        at = slice(g * group, (g + 1) * group)
        shards.append(by_parity(kept[at], swap(given[at], "dp", 1)))
    pack, shards[0] = together(pack, shards[0])
    for g in range(GROUPS):
        gathered = gather_column(shards[g])
        if not layered:
            gathered = gathered.transpose(2, 3, 0, 1, 4, 5).reshape(group, 3, width, -1)
        expert_weights.append(gathered)

    labels = jnp.arange(NF, dtype=jnp.int32)
    slot_cols, counts = [], []
    for tree_routes in (routes, swap(routes, "dp", 1)):
        hot = jnp.sum((tree_routes[:, :, None] == labels).astype(jnp.int32), axis=1)
        rank = jnp.cumsum(hot, axis=0) - hot
        counts.append(jnp.sum(hot, axis=0))
        quarters = jnp.where(hot > 0, rank, -1).reshape(4, row_count, NF)
        for b in range(4):
            slot_cols.append(lax.dynamic_index_in_dim(quarters, index ^ b, 0, keepdims=False))
    counts = jnp.stack(counts)
    slot_cols = jnp.concatenate(slot_cols, axis=0)
    slot_rows = slot_cols.reshape(2, tree_len, NF).transpose(0, 2, 1)

    angles = rotary_angles(segment_ids, parent_ids)
    rowinfo = jnp.pad(jnp.stack([segment_ids, parent_ids]), ((0, 6), (0, 0)))
    colinfo = rowinfo.T
    queries, keys, values, keys_t, values_t, gathered_one, head_full = project(
        columns, tokens_in, attention_gain, angles, pack
    )
    queries, late_cotangent = together(queries, cotangent)
    grad_rows = gather_pair(late_cotangent)
    attended, totals = attend(heads, queries, keys, values_t, rowinfo, colinfo)
    attended, *grad_rows = together(attended, *grad_rows)
    local_routes = lax.dynamic_slice_in_dim(routes, index * row_count, row_count, 0)
    picked = jnp.sum(
        (local_routes[:, :, None] == jnp.arange(128, dtype=jnp.int32)).astype(F32), axis=1
    )
    carried_part = spread(jnp.dot(carried_logits, carry_weight, precision=HIGHEST), 128)
    mix_weight = spread(jnp.concatenate([spread(router_weight, MIX), constant_gate], axis=1), 128)
    hidden, aux, expert_rows = branch(
        attended, head_full, tokens_in, expert_gain, carried_part, mix_weight, picked
    )

    parts, own_grads = [], []
    for g in range(GROUPS):
        base = (parity * own_experts + g * group).astype(jnp.int32).reshape(1)
        *parts, weight_grads = experts(
            base, expert_weights[g], counts, expert_rows, grad_rows, slot_rows, slot_cols, parts
        )
        if not layered:
            weight_grads = weight_grads.reshape(group, 3, -1, 2, share, weight_grads.shape[-1])
            weight_grads = weight_grads.transpose(2, 3, 0, 1, 4, 5)
        own_grads.append(scatter_column(weight_grads))
    keep, send, grad_keep, grad_send = parts

    vectors = jnp.pad(constant_vector, ((0, 6), (0, 0)))
    grad_hidden, grad_logits, grad_attended, grad_output_t, small = branch_back(
        hidden, aux, cotangent, expert_gain, mix_weight, vectors, spread(carried_logits, 128),
        attended, head_full, grad_keep, grad_send,
    )
    grad_carried = lax.dot_general(
        grad_logits[:, :NE], carry_weight, (((1,), (1,)), ((), ())), precision=HIGHEST
    )
    grad_attended, own_grads[0], keep, send = together(grad_attended, own_grads[0], keep, send)

    scale = lax.rsqrt(jnp.mean(hidden * hidden, axis=-1, keepdims=True) + epsilon)
    gate = lambda k: aux[:, NF + 1 + k : NF + 2 + k]
    mixture = lambda k: aux[:, MIX + k : MIX + k + 1]
    along = gate(0) + gate(1) * mixture(0) + gate(2) * mixture(2)
    local_sum = along * (hidden * scale * expert_gain)
    for c in range(2):
        local_sum = local_sum + gate(1 + c) * mixture(2 * c + 1) * constant_vector[c][None, :]
    output = (hidden + local_sum + scatter_pair(keep, send)).astype(BF16)

    grad_projected = attend_back(
        heads, queries, grad_attended, attended, keys, values, keys_t, rowinfo, colinfo, totals, angles
    )
    grad_projected, own_grads[1], output = together(grad_projected, own_grads[1], output)
    grad_tokens, own_pack, small = finish(
        columns, grad_projected, gathered_one, head_full, grad_output_t, small, grad_hidden, tokens_in,
        attention_gain,
    )
    if columns:
        own_sections = [
            jnp.concatenate(
                [own_pack[:, 128 * k : 128 * (k + 1)], own_pack[:, 512 + 64 * k : 576 + 64 * k]], axis=1
            )
            for k in range(4)
        ]
    else:
        blocks = own_pack.reshape(-1, 2, share, 4 * PAD)
        kept = lax.dynamic_index_in_dim(blocks, parity, 1, keepdims=False)
        given = lax.dynamic_index_in_dim(blocks, 1 - parity, 1, keepdims=False)
        paired = kept.astype(F32) + swap(given, "dp", 1).astype(F32)
        own_pack = scatter_column(paired.astype(BF16)).astype(F32)
        own_sections = [own_pack[:, k * PAD : k * PAD + head_width] for k in range(4)]
        small = lax.psum(small, ("dp", "tensor"))
    own_grads = jnp.concatenate(own_grads, axis=1)
    kept = lax.dynamic_index_in_dim(own_grads, parity, 0, keepdims=False)
    given = lax.dynamic_index_in_dim(own_grads, 1 - parity, 0, keepdims=False)
    own_grads = by_parity(kept, swap(given, "dp", 1)).reshape(NF, 3, share, -1).astype(F32)
    grad_first = own_grads[:, :2]
    grad_second = own_grads[:, 2].transpose(0, 2, 1)
    return (
        output,
        grad_tokens,
        grad_carried,
        small[19, :width],
        jnp.stack(own_sections[:3]),
        own_sections[3].T,
        small[16, :width],
        small[:NE, :width].T,
        small[:NE, width : width + NE],
        small[MIX : MIX + 4, :width].T,
        small[17:19, :width],
        grad_first,
        grad_second,
    )


def solution(mesh):
    in_specs = (
        P(("dp", "tensor"), None),
        P(("dp", "tensor"), None),
        P(("dp", "tensor"), None),
        P("dp"),
        P("dp"),
        P("dp", None),
        P(),
        P(None, "dp", "tensor"),
        P("tensor", "dp"),
        P(),
        P(),
        P(),
        P(),
        P(),
        P(None, None, "dp", "tensor"),
        P(None, "tensor", "dp"),
    )
    out_specs = (
        P(("dp", "tensor"), None),
        P(("dp", "tensor"), None),
        P(("dp", "tensor"), None),
        P(),
        P(None, "dp", "tensor"),
        P("tensor", "dp"),
        P(),
        P(),
        P(),
        P(),
        P(),
        P(None, None, "dp", "tensor"),
        P(None, "tensor", "dp"),
    )
    return jax.shard_map(
        per_device, mesh=mesh, in_specs=in_specs, out_specs=out_specs, check_vma=False
    )
```

```python
import functools

import jax
import jax.numpy as jnp
from jax import lax
from jax.experimental import pallas as pl
from jax.experimental.pallas import tpu as pltpu
from jax.sharding import PartitionSpec as P

HEAD = 64
NF = 8
NSEG = 13
NE = 12
PAD = 256
BLOCK = 256
SLICES = 4
MIX = 12
WINDOW = 1280
TILE = 256
GROUPS = 2

epsilon = 1e-06
HIGHEST = lax.Precision.HIGHEST
F32 = jnp.float32
BF16 = jnp.bfloat16
MESH = pl.DeviceIdType.MESH


def dot_nn(a, b):
    return lax.dot_general(a, b, (((1,), (0,)), ((), ())), preferred_element_type=F32)


def dot_nt(a, b):
    return lax.dot_general(a, b, (((1,), (1,)), ((), ())), preferred_element_type=F32)


def dot_tn(a, b):
    return lax.dot_general(a, b, (((0,), (0,)), ((), ())), preferred_element_type=F32)


def normed(values, gain_vector):
    return (
        values
        * lax.rsqrt(jnp.mean(values * values, axis=-1, keepdims=True) + epsilon)
        * gain_vector
    )


def tree_positions(segment, parent):
    token_count = segment.shape[0]
    labels = jnp.arange(NSEG, dtype=jnp.int32)
    own_hot = (segment[:, None] == labels[None, :]).astype(jnp.int32)
    parent_hot = (parent[:, None] == labels[None, :]).astype(jnp.int32)
    lengths = jnp.sum(own_hot, axis=0)
    starts = jnp.cumsum(lengths) - lengths
    own_start = jnp.sum(own_hot * starts[None, :], axis=1)
    parent_length = jnp.sum(parent_hot * lengths[None, :], axis=1)
    position_index = jnp.arange(token_count, dtype=jnp.int32)
    return (
        position_index
        - own_start
        + jnp.where(segment > 0, lengths[0], 0)
        + jnp.where(parent > 0, parent_length, 0)
    )


def rotary_angles(segment, parent):
    angle_rate = 10000.0 ** (-2.0 * jnp.arange(HEAD // 2, dtype=F32) / HEAD)
    angles = tree_positions(segment, parent).astype(F32)[:, None] * angle_rate[None, :]
    return jnp.concatenate([jnp.cos(angles), jnp.sin(angles)], axis=1)


def swap(values, axis, bits):
    size = lax.axis_size(axis)
    return lax.ppermute(values, axis, [(i, i ^ bits) for i in range(size)])


def together(*values):
    return lax.optimization_barrier(values)


def column_groups():
    size = lax.axis_size("dp")
    return [list(range(first, size, 2)) for first in range(2)]


def gather_column(own):
    return lax.all_gather(own, "dp", axis=0, tiled=False, axis_index_groups=column_groups())


def scatter_column(parts):
    return lax.psum_scatter(
        parts, "dp", scatter_dimension=0, tiled=False, axis_index_groups=column_groups()
    )


def by_parity(mine, other):
    even = lax.axis_index("dp") % 2 == 0
    return jnp.stack([jnp.where(even, mine, other), jnp.where(even, other, mine)])


def swap_halves(values):
    lane = lax.broadcasted_iota(jnp.int32, values.shape, 1)
    half = HEAD // 2
    return jnp.where(
        lane % HEAD < half, pltpu.roll(values, PAD - half, 1), pltpu.roll(values, half, 1)
    )


def rotation(angles):
    half = HEAD // 2
    source = lax.broadcasted_iota(jnp.int32, (2 * half, PAD), 0)
    lane = lax.broadcasted_iota(jnp.int32, (2 * half, PAD), 1)
    to_cos = (source == lane % half).astype(F32)
    to_sin = jnp.where(
        source == half + lane % half, jnp.where(lane % HEAD < half, -1.0, 1.0), 0.0
    )
    return [
        lax.dot_general(
            angles, where, (((1,), (0,)), ((), ())), precision=HIGHEST, preferred_element_type=F32
        )
        for where in (to_cos, to_sin)
    ]


def project_kernel(columns, tok_ref, gain_ref, angle_ref, pack_ref, *refs):
    q_ref, k_ref, v_ref, kt_ref, vt_ref, one_ref = refs[:6]
    if columns:
        head_ref, gathered, shards, send_sems, recv_sems = refs[6:]
    else:
        head_ref, (gathered, send_sems, recv_sems) = pack_ref, refs[6:]
    near, far, across, *column = enter(columns)
    copies = Copies(send_sems, recv_sems)
    dp, tensor = lax.axis_index("dp"), lax.axis_index("tensor")
    rows, width = tok_ref.shape
    share = pack_ref.shape[0]
    heads, last = [], []
    if columns:
        heads = [copies.start(pack_ref, shards.at[dp], device) for device in column]
        last.append(copies.start(pack_ref, shards.at[dp], across))
        shards[dp] = pack_ref[...]
    size = rows // SLICES
    slices = [pl.ds(c * size, size) for c in range(SLICES)]
    far_moves, near_moves = [], []
    for at in slices:
        values = tok_ref[at, :].astype(F32)
        scale = lax.rsqrt(jnp.mean(values * values, axis=1, keepdims=True) + epsilon)
        gathered[0, at, :] = (values * scale * gain_ref[...]).astype(BF16)
        far_moves.append(copies.start(gathered.at[0, at], gathered.at[2, at], far))
        near_moves.append(copies.start(gathered.at[0, at], gathered.at[1, at], near))
    corner_moves = []
    for c, at in enumerate(slices):
        far_moves[c].wait_recv()
        corner_moves.append(copies.start(gathered.at[2, at], gathered.at[3, at], near))
        if c < len(heads):
            heads[c].wait_recv()
            origin = lax.rem(dp + 8 - 2 * (c + 1), 8)
            last.append(copies.start(shards.at[origin], shards.at[origin], across))
    for move in last + near_moves + corner_moves:
        move.wait_recv()
    if columns:
        for d in range(8):
            at = pl.ds(d * share, share)
            piece = shards[d]
            for section in range(4):
                head_ref[at, section * PAD : section * PAD + 128] = piece[
                    :, section * 128 : (section + 1) * 128
                ]
                start = 512 + 128 * (section // 2)
                rest = piece[:, start : start + 128].astype(F32)
                if section % 2:
                    rest = pltpu.roll(rest, 64, 1)
                lane = lax.broadcasted_iota(jnp.int32, rest.shape, 1)
                head_ref[at, section * PAD + 128 : (section + 1) * PAD] = jnp.where(
                    lane < 64, rest, 0.0
                ).astype(BF16)
    for bits in range(4):
        start = pl.multiple_of(other(tensor, bits) * rows, rows)
        at = pl.ds(start, rows)
        values = gathered[bits]
        one_ref[at, :] = values
        cosine, sine = rotation(angle_ref[at, :])
        part = dot_nn(values, head_ref[:, :PAD])
        q_ref[at, :] = ((part * cosine + swap_halves(part) * sine) * HEAD**-0.5).astype(BF16)
        part = dot_nn(values, head_ref[:, PAD : 2 * PAD])
        part = part * cosine + swap_halves(part) * sine
        k_ref[at, :] = part.astype(BF16)
        kt_ref[:, at] = part.T.astype(BF16)
        part = dot_nn(values, head_ref[:, 2 * PAD : 3 * PAD])
        v_ref[at, :] = part.astype(BF16)
        vt_ref[:, at] = part.T.astype(BF16)
    copies.finish()


def project(columns, tokens, gain, angles, pack):
    rows, width = tokens.shape
    total = angles.shape[0]
    vmem = pl.BlockSpec(memory_space=pltpu.VMEM)
    copies = 3 * SLICES + 7
    wide = jax.ShapeDtypeStruct((total, PAD), BF16)
    tall = jax.ShapeDtypeStruct((PAD, total), BF16)
    shapes = [wide, wide, wide, tall, tall, jax.ShapeDtypeStruct((total, width), BF16)]
    scratch = [pltpu.VMEM((4, rows, width), BF16)]
    if columns:
        shapes.append(jax.ShapeDtypeStruct((width, 4 * PAD), BF16))
        scratch.append(pltpu.VMEM((8, *pack.shape), BF16))
    out = pl.pallas_call(
        functools.partial(project_kernel, columns),
        in_specs=[vmem] * 4,
        out_specs=[vmem] * len(shapes),
        out_shape=shapes,
        scratch_shapes=scratch
        + [pltpu.SemaphoreType.DMA((copies,)), pltpu.SemaphoreType.DMA((copies,))],
        compiler_params=pltpu.CompilerParams(
            collective_id=3, has_side_effects=True, vmem_limit_bytes=56 << 20
        ),
        cost_estimate=pl.CostEstimate(
            flops=6 * total * width * PAD, bytes_accessed=16 * total * width, transcendentals=0
        ),
    )(tokens, gain[None], angles, pack)
    return out if columns else [*out, pack]


def head_mask(values, head):
    lane = lax.broadcasted_iota(jnp.int32, values.shape, 1)
    return jnp.where(lane // HEAD == head, values, jnp.zeros_like(values))


def seen(i, j, seg_row, par_row, seg_col):
    key_at = j * BLOCK + lax.broadcasted_iota(jnp.int32, (BLOCK, 1), 0)
    query_at = i * BLOCK + lax.broadcasted_iota(jnp.int32, (1, BLOCK), 1)
    related = (seg_col == seg_row) | (seg_col == par_row) | (seg_col == 0)
    return related & (key_at <= query_at)


def attend_block(heads, i, q_ref, k_ref, vt_ref, rowinfo_ref, colinfo_ref, o_ref, total_ref):
    here = pl.ds(pl.multiple_of(i * BLOCK, BLOCK), BLOCK)
    queries = q_ref[here, :]
    by_head = [head_mask(queries, h) for h in range(heads)]
    seg_row, par_row = rowinfo_ref[0:1, here], rowinfo_ref[1:2, here]

    def step(j, carry):
        at = pl.ds(pl.multiple_of(j * BLOCK, BLOCK), BLOCK)
        keys = k_ref[at, :]
        visible = seen(i, j, seg_row, par_row, colinfo_ref[at, 0:1])
        out = []
        for h in range(heads):
            top, total, mixed = carry[h]
            scores = jnp.where(visible, dot_nt(keys, by_head[h]), -1e30)
            new_top = jnp.maximum(top, jnp.max(scores, axis=0, keepdims=True))
            shrink = jnp.exp(top - new_top)
            probs = jnp.exp(scores - new_top)
            total = total * shrink + jnp.sum(probs, axis=0, keepdims=True)
            mixed = mixed * shrink + dot_nn(
                vt_ref[h * HEAD : (h + 1) * HEAD, at], probs.astype(BF16)
            )
            out.append((new_top, total, mixed))
        return tuple(out)

    start = tuple(
        (
            jnp.full((1, BLOCK), -1e30, F32),
            jnp.zeros((1, BLOCK), F32),
            jnp.zeros((HEAD, BLOCK), F32),
        )
        for _ in range(heads)
    )
    done = lax.fori_loop(0, i + 1, step, start)
    mixed = [m / t for _, t, m in done] + [jnp.zeros((PAD - heads * HEAD, BLOCK), F32)]
    o_ref[here, :] = jnp.concatenate(mixed, axis=0).T.astype(BF16)
    total_ref[:, here] = jnp.concatenate(
        [m + jnp.log(t) for m, t, _ in done] + [jnp.zeros((8 - heads, BLOCK), F32)], axis=0
    )


def other(place, bits):
    if bits & 2:
        place = place + 2 - 4 * lax.rem(lax.div(place, 2), 2)
    if bits & 1:
        place = place + 1 - 2 * lax.rem(place, 2)
    return place


def enter(columns=False):
    dp, tensor = lax.axis_index("dp"), lax.axis_index("tensor")
    others = [(dp, other(tensor, 1)), (dp, other(tensor, 2)), (other(dp, 1), tensor)]
    if columns:
        others += [(lax.rem(dp + 2 * j, 8), tensor) for j in (1, 2, 3)]
    barrier = pltpu.get_barrier_semaphore()
    for device in others:
        pl.semaphore_signal(barrier, inc=1, device_id=device, device_id_type=MESH)
    pl.semaphore_wait(barrier, len(others))
    return others


class Copies:
    def __init__(self, send_sems, recv_sems):
        self.send_sems, self.recv_sems, self.made = send_sems, recv_sems, []

    def start(self, source, target, device):
        k = len(self.made)
        copy = pltpu.make_async_remote_copy(
            src_ref=source,
            dst_ref=target,
            send_sem=self.send_sems.at[k],
            recv_sem=self.recv_sems.at[k],
            device_id=device,
            device_id_type=MESH,
        )
        copy.start()
        self.made.append(copy)
        return copy

    def finish(self):
        for copy in self.made:
            copy.wait_send()


def quarter(ref, bits, rows):
    place = other(lax.axis_index("tensor"), bits)
    return ref.at[pl.ds(pl.multiple_of(place * rows, rows), rows)]


def sum_of_quarters(part, copies, near, far, near_send, near_recv, far_send, far_recv):
    rows = far_send.shape[0]
    near_send[0] = part(3).astype(BF16)
    first = copies.start(near_send.at[0], near_recv.at[0], near)
    near_send[1] = part(1).astype(BF16)
    second = copies.start(near_send.at[1], near_recv.at[1], near)
    mine = part(2)
    first.wait_recv()
    far_send[...] = (mine + near_recv[0].astype(F32)).astype(BF16)
    moves = []
    for c in range(SLICES):
        at = pl.ds(c * rows // SLICES, rows // SLICES)
        moves.append(copies.start(far_send.at[at], far_recv.at[at], far))
    mine = part(0)
    second.wait_recv()
    return mine + near_recv[1].astype(F32), moves


class Spread:
    def __init__(self, copies, devices, target, rows):
        self.copies, (self.near, self.far, self.across) = copies, devices
        self.rows, self.own, self.beside = rows, quarter(target.at[0], 0, rows), quarter(target.at[1], 0, rows)
        self.over, self.corner = quarter(target.at[0], 2, rows), quarter(target.at[1], 2, rows)
        self.from_far, self.from_across, self.from_corner, self.ends = {}, {}, {}, []

    def send(self, source, at, c):
        copies = self.copies
        self.from_far[c] = copies.start(source.at[at], self.own.at[at], self.far)
        self.from_across[c] = copies.start(source.at[at], self.beside.at[at], self.across)
        self.ends.append(copies.start(source.at[at], self.own.at[at], self.near))

    def pass_on(self, c, at):
        copies = self.copies
        self.from_far[c].wait_recv()
        if c >= SLICES // 2:
            self.from_corner[c] = copies.start(self.over.at[at], self.corner.at[at], self.across)
        self.ends.append(copies.start(self.over.at[at], self.over.at[at], self.near))
        self.from_across[c].wait_recv()
        if c < SLICES // 2:
            self.from_corner[c] = copies.start(self.beside.at[at], self.beside.at[at], self.far)
        self.ends.append(copies.start(self.beside.at[at], self.beside.at[at], self.near))

    def pass_corner(self, c, at):
        self.from_corner[c].wait_recv()
        self.ends.append(self.copies.start(self.corner.at[at], self.corner.at[at], self.near))

    def finish(self):
        for copy in self.ends:
            copy.wait_recv()


def branch_kernel(
    heads, q_ref, k_ref, vt_ref, rowinfo_ref, colinfo_ref, cot_ref,
    out_ref, tok_ref, gain_ref, carried_ref, mix_ref, picked_ref,
    att_ref, total_ref, hidden_ref, aux_ref, rows_ref, cots_ref,
    near_send, near_recv, far_send, far_recv, own, send_sems, recv_sems, local_sems,
):
    devices = enter()
    near, far, _ = devices
    copies = Copies(send_sems, recv_sems)
    rows, width = tok_ref.shape
    weights = out_ref[...]
    size = rows // SLICES
    slices = [pl.ds(c * size, size) for c in range(SLICES)]
    locals_ = [pltpu.make_async_copy(cot_ref, quarter(cots_ref.at[0], 0, rows), local_sems.at[0])]
    locals_[0].start()
    cots = Spread(copies, devices, cots_ref, rows)
    for c, at in enumerate(slices):
        cots.send(cot_ref, at, c)

    def part(bits):
        if bits == 0:
            for c, at in enumerate(slices):
                cots.pass_on(c, at)
        place = other(lax.axis_index("tensor"), bits)
        for block in range(rows // BLOCK):
            attend_block(
                heads, place * (rows // BLOCK) + block,
                q_ref, k_ref, vt_ref, rowinfo_ref, colinfo_ref, att_ref, total_ref,
            )
        return dot_nt(quarter(att_ref, bits, rows)[...], weights)

    mine, moves = sum_of_quarters(
        part, copies, near, far, near_send, near_recv, far_send, far_recv
    )
    hidden_ref[...] = tok_ref[...].astype(F32) + mine
    spread = Spread(copies, devices, rows_ref, rows)
    for c, at in enumerate(slices):
        moves[c].wait_recv()
        hidden = hidden_ref[at, :] + far_recv[at, :].astype(F32)
        hidden_ref[at, :] = hidden
        scale = lax.rsqrt(jnp.mean(hidden * hidden, axis=1, keepdims=True) + epsilon)
        normed_two = hidden * scale * gain_ref[...]
        logits = carried_ref[at, :] + lax.dot_general(
            normed_two,
            mix_ref[...],
            (((1,), (0,)), ((), ())),
            precision=HIGHEST,
            preferred_element_type=F32,
        )
        picked = picked_ref[at, :] > 0
        top = jnp.max(jnp.where(picked, logits, -1e30), axis=1, keepdims=True)
        weight = jnp.where(picked, jnp.exp(jnp.where(picked, logits - top, 0.0)), 0.0)
        gate = weight / jnp.sum(weight, axis=1, keepdims=True)
        lane = lax.broadcasted_iota(jnp.int32, logits.shape, 1)
        turned = jnp.where(
            lane % 2 == 0, pltpu.roll(logits, 127, 1), pltpu.roll(logits, 1, 1)
        )
        top = jnp.maximum(logits, turned)
        mixture = jnp.exp(logits - top) / (jnp.exp(logits - top) + jnp.exp(turned - top))
        aux_ref[at, :] = jnp.where(lane < MIX, gate, jnp.where(lane < MIX + 4, mixture, 0.0))
        own[at, :width] = normed_two.astype(BF16)
        own[at, width:] = jnp.where(lane < NF, gate, 0.0).astype(BF16)
        spread.send(own, at, c)
        local = pltpu.make_async_copy(
            own.at[at], quarter(rows_ref.at[0], 0, rows).at[at], local_sems.at[1 + c]
        )
        local.start()
        locals_.append(local)
    for c, at in enumerate(slices):
        cots.pass_corner(c, at)
    for c, at in enumerate(slices):
        spread.pass_on(c, at)
    for c, at in enumerate(slices):
        spread.pass_corner(c, at)
    cots.finish()
    spread.finish()
    for local in locals_:
        local.wait()
    copies.finish()


def branch(
    heads, queries, keys, values_t, rowinfo, colinfo, cotangent, head_full, tokens, gain, carried, mix,
    picked,
):
    rows, width = tokens.shape
    total = queries.shape[0]
    vmem, anywhere = pl.BlockSpec(memory_space=pltpu.VMEM), pl.BlockSpec(memory_space=pl.ANY)
    copies = 2 + 15 * SLICES
    return pl.pallas_call(
        functools.partial(branch_kernel, heads),
        in_specs=[vmem] * 12,
        out_specs=[vmem] * 4 + [anywhere] * 2,
        out_shape=[
            jax.ShapeDtypeStruct((total, PAD), BF16),
            jax.ShapeDtypeStruct((8, total), F32),
            jax.ShapeDtypeStruct((rows, width), F32),
            jax.ShapeDtypeStruct((rows, 128), F32),
            jax.ShapeDtypeStruct((2, total, width + 128), BF16),
            jax.ShapeDtypeStruct((2, total, width), BF16),
        ],
        scratch_shapes=[
            pltpu.VMEM((2, rows, width), BF16),
            pltpu.VMEM((2, rows, width), BF16),
            pltpu.VMEM((rows, width), BF16),
            pltpu.VMEM((rows, width), BF16),
            pltpu.VMEM((rows, width + 128), BF16),
            pltpu.SemaphoreType.DMA((copies,)),
            pltpu.SemaphoreType.DMA((copies,)),
            pltpu.SemaphoreType.DMA((1 + SLICES,)),
        ],
        compiler_params=pltpu.CompilerParams(
            collective_id=1, has_side_effects=True, vmem_limit_bytes=48 << 20
        ),
        cost_estimate=pl.CostEstimate(
            flops=64 * rows * width * PAD, bytes_accessed=64 * rows * width, transcendentals=0
        ),
    )(
        queries, keys, values_t, rowinfo, colinfo, cotangent, head_full[:, 3 * PAD :], tokens, gain[None],
        carried, mix, picked,
    )


class PairSum:
    def __init__(self, copies, devices, source, refs, local_sems):
        self.copies, (self.near, self.far, self.across) = copies, devices
        self.source, self.local_sems = source, local_sems
        self.kept, self.near_recv, self.corner_send, self.corner_recv = refs[:4]
        self.far_send, self.far_recv, self.across_send, self.across_recv = refs[4:]
        self.rows = self.far_send.shape[0]
        half = self.rows // 2
        self.halves = [pl.ds(0, half), pl.ds(half, half)]
        self.arrivals, self.locals_, self.from_far, self.from_across = {}, {}, {}, {}

    @staticmethod
    def shapes(rows, wide):
        one, two = (rows, wide), (2, rows // 2, wide)
        return [
            pltpu.VMEM(shape, BF16)
            for shape in ((4, *one), (4, *one), one, two, one, one, one, one)
        ]

    def start(self):
        for b in (3, 1, 2, 0):
            tree, bits = self.source.at[b // 2], 2 * (b % 2)
            self.arrivals[b] = self.copies.start(
                quarter(tree, bits + 1, self.rows), self.near_recv.at[b], self.near
            )
            self.locals_[b] = pltpu.make_async_copy(
                quarter(tree, bits, self.rows), self.kept.at[b], self.local_sems.at[b]
            )
            self.locals_[b].start()

    def joined(self, b, at):
        return self.kept[b, at, :].astype(F32) + self.near_recv[b, at, :].astype(F32)

    def arrived(self, b):
        self.arrivals[b].wait_recv()
        self.locals_[b].wait()

    def first_round(self):
        low, high = self.halves
        self.arrived(3)
        self.corner_send[...] = self.joined(3, pl.ds(0, self.rows)).astype(BF16)
        start = self.copies.start
        self.corner_far = start(self.corner_send.at[low], self.corner_recv.at[0], self.far)
        self.corner_across = start(self.corner_send.at[high], self.corner_recv.at[1], self.across)
        self.arrived(1)
        self.far_send[low, :] = self.joined(1, low).astype(BF16)
        self.from_far[0] = start(self.far_send.at[low], self.far_recv.at[low], self.far)
        self.arrived(2)
        self.across_send[high, :] = self.joined(2, high).astype(BF16)
        self.from_across[1] = start(self.across_send.at[high], self.across_recv.at[high], self.across)

    def second_round(self):
        low, high = self.halves
        start = self.copies.start
        self.corner_far.wait_recv()
        self.across_send[low, :] = (
            self.joined(2, low) + self.corner_recv[0].astype(F32)
        ).astype(BF16)
        self.from_across[0] = start(self.across_send.at[low], self.across_recv.at[low], self.across)
        self.corner_across.wait_recv()
        self.far_send[high, :] = (
            self.joined(1, high) + self.corner_recv[1].astype(F32)
        ).astype(BF16)
        self.from_far[1] = start(self.far_send.at[high], self.far_recv.at[high], self.far)
        self.arrived(0)

    def total(self, h):
        self.from_far[h].wait_recv()
        self.from_across[h].wait_recv()
        at = self.halves[h]
        return (
            self.joined(0, at)
            + self.far_recv[at, :].astype(F32)
            + self.across_recv[at, :].astype(F32)
        )


def attend_back_block(
    heads, i, q_ref, g_ref, o_ref, k_ref, v_ref, kt_ref, rowinfo_ref, colinfo_ref, total_ref, angle_ref,
    grad_ref, key_sum, value_sum, query_sum,
):
    here = pl.ds(pl.multiple_of(i * BLOCK, BLOCK), BLOCK)
    query_sum[...] = jnp.zeros_like(query_sum)
    queries, grads = q_ref[here, :], g_ref[here, :]
    q_heads = [head_mask(queries, h) for h in range(heads)]
    g_heads = [head_mask(grads, h) for h in range(heads)]
    seg_row, par_row = rowinfo_ref[0:1, here], rowinfo_ref[1:2, here]
    product = grads.astype(F32) * o_ref[here, :].astype(F32)
    lane = lax.broadcasted_iota(jnp.int32, (8, PAD), 1)
    which = lax.broadcasted_iota(jnp.int32, (8, PAD), 0)
    delta = lax.dot_general(
        (lane // HEAD == which).astype(F32),
        product,
        (((1,), (1,)), ((), ())),
        precision=HIGHEST,
        preferred_element_type=F32,
    )
    totals = total_ref[:, here]

    def step(j, carry):
        at = pl.ds(pl.multiple_of(j * BLOCK, BLOCK), BLOCK)
        keys, values = k_ref[at, :], v_ref[at, :]
        visible = seen(i, j, seg_row, par_row, colinfo_ref[at, 0:1])
        key_part, value_part = key_sum[at, :], value_sum[at, :]
        for h in range(heads):
            scores = jnp.where(visible, dot_nt(keys, q_heads[h]), -1e30)
            probs = jnp.exp(scores - totals[h : h + 1, :])
            value_part = value_part + dot_nn(probs.astype(BF16), g_heads[h])
            grad_probs = dot_nt(values, g_heads[h])
            grad_scores = (probs * (grad_probs - delta[h : h + 1, :])).astype(BF16)
            key_part = key_part + dot_nn(grad_scores, q_heads[h])
            lanes = slice(h * HEAD, (h + 1) * HEAD)
            query_sum[lanes, :] += dot_nn(kt_ref[lanes, at], grad_scores)
        key_sum[at, :] = key_part
        value_sum[at, :] = value_part
        return carry

    lax.fori_loop(0, i + 1, step, 0)
    grad_ref[here, :PAD] = turned_back(query_sum[...].T * HEAD**-0.5, angle_ref[here, :])


def turned_back(values, angles):
    cosine, sine = rotation(angles)
    return (values * cosine - swap_halves(values) * sine).astype(BF16)


def branch_back_kernel(
    heads, hidden_ref, aux_ref, cot_ref, gain_ref, mix_ref, vector_ref, carried_ref, att_ref, out_ref,
    q_ref, k_ref, v_ref, kt_ref, rowinfo_ref, colinfo_ref, total_ref, angle_ref, sums_ref, grad_ins_ref,
    grad_hidden_ref, grad_logits_ref, grad_out_ref, small_ref, grad_ref, result_ref,
    normed_two, base, gathered, grad_att, key_sum, value_sum, query_sum,
    send_sems, recv_sems, local_sems, *buffers,
):
    devices = enter()
    near, far, _ = devices
    copies = Copies(send_sems, recv_sems)
    rows, width = hidden_ref.shape
    half = rows // 2
    halves = [pl.ds(0, half), pl.ds(half, half)]
    incoming = PairSum(copies, devices, grad_ins_ref, buffers[:8], local_sems.at[0])
    results = PairSum(copies, devices, sums_ref, buffers[8:], local_sems.at[1])
    incoming.start()
    key_sum[...] = jnp.zeros_like(key_sum)
    value_sum[...] = jnp.zeros_like(value_sum)

    gain = gain_ref[...]
    lane = lax.broadcasted_iota(jnp.int32, (half, 128), 1)

    def column(values, at):
        return jnp.sum(jnp.where(lane == at, values, 0.0), axis=1, keepdims=True)

    known = []
    for at in halves:
        hidden, aux, grads = hidden_ref[at, :], aux_ref[at, :], cot_ref[at, :].astype(F32)
        scale = lax.rsqrt(jnp.mean(hidden * hidden, axis=1, keepdims=True) + epsilon)
        normed = hidden * scale * gain
        normed_two[at, :] = normed
        gates = [column(aux, NF + 1 + k) for k in range(3)]
        mixes = [column(aux, MIX + k) for k in range(4)]
        along = jnp.sum(grads * normed, axis=1, keepdims=True)
        vectors = [
            jnp.sum(grads * vector_ref[c : c + 1, :], axis=1, keepdims=True) for c in range(2)
        ]
        kept = gates[0] + gates[1] * mixes[0] + gates[2] * mixes[2]
        base[at, :] = grads * kept
        sums = []
        for c in range(2):
            sums.append(
                jnp.sum(grads * (gates[1 + c] * mixes[2 * c + 1]), axis=0, keepdims=True)
            )
        by_gate = jnp.where(lane == NF + 1, along, 0.0)
        by_mix = jnp.zeros((half, 128), F32)
        for c in range(2):
            first, second = mixes[2 * c], mixes[2 * c + 1]
            by_gate = by_gate + jnp.where(
                lane == NF + 2 + c, first * along + second * vectors[c], 0.0
            )
            d_first, d_second = gates[1 + c] * along, gates[1 + c] * vectors[c]
            inner = first * d_first + second * d_second
            by_mix = by_mix + jnp.where(lane == MIX + 2 * c, first * (d_first - inner), 0.0)
            by_mix = by_mix + jnp.where(lane == MIX + 2 * c + 1, second * (d_second - inner), 0.0)
        known.append((scale, by_gate, by_mix, sums))
    incoming.first_round()
    incoming.second_round()

    gain_sum = jnp.zeros((1, width), F32)
    far_moves, near_moves = [], []
    for h, at in enumerate(halves):
        scale, by_gate, by_mix, _ = known[h]
        arriving = incoming.total(h)
        by_gate = by_gate + jnp.where(lane < NF, arriving[:, width:], 0.0)
        gates = jnp.where(lane < MIX, aux_ref[at, :], 0.0)
        grad_logits = by_mix + gates * (
            by_gate - jnp.sum(gates * by_gate, axis=1, keepdims=True)
        )
        grad_logits_ref[at, :] = grad_logits
        grad_normed = arriving[:, :width] + base[at, :] + lax.dot_general(
            grad_logits,
            mix_ref[...],
            (((1,), (1,)), ((), ())),
            precision=HIGHEST,
            preferred_element_type=F32,
        )
        hidden = hidden_ref[at, :]
        gain_sum = gain_sum + jnp.sum(hidden * scale * grad_normed, axis=0, keepdims=True)
        weighted = gain * grad_normed
        inner = jnp.mean(hidden * weighted, axis=1, keepdims=True)
        grad_hidden = (
            cot_ref[at, :].astype(F32) + scale * weighted - hidden * (scale * scale * scale * inner)
        )
        grad_hidden_ref[at, :] = grad_hidden
        gathered[0, at, :] = grad_hidden.astype(BF16)
        far_moves.append(copies.start(gathered.at[0, at], gathered.at[2, at], far))
        near_moves.append(copies.start(gathered.at[0, at], gathered.at[1, at], near))
    results.start()

    def over_tokens(a, b):
        return lax.dot_general(
            a, b, (((0,), (0,)), ((), ())), precision=HIGHEST, preferred_element_type=F32
        )

    small_ref[...] = jnp.zeros_like(small_ref)
    small_ref[:16, :width] = over_tokens(grad_logits_ref[...], normed_two[...])[:16]
    small_ref[16:, :width] = jnp.concatenate(
        [gain_sum] + [known[0][3][c] + known[1][3][c] for c in range(2)]
        + [jnp.zeros((5, width), F32)],
        axis=0,
    )
    small_ref[:16, width:] = over_tokens(carried_ref[...], grad_logits_ref[...])[:16]

    def attention_back(bits):
        values = gathered[bits]
        quarter(grad_att, bits, rows)[...] = dot_nn(values, out_ref[...]).astype(BF16)
        product = dot_tn(values, quarter(att_ref, bits, rows)[...])
        grad_out_ref[...] = grad_out_ref[...] + product if bits else product
        place = other(lax.axis_index("tensor"), bits)
        for block in range(rows // BLOCK):
            attend_back_block(
                heads, place * (rows // BLOCK) + block, q_ref, grad_att, att_ref, k_ref, v_ref, kt_ref,
                rowinfo_ref, colinfo_ref, total_ref, angle_ref, grad_ref, key_sum, value_sum, query_sum,
            )

    attention_back(0)
    results.first_round()
    for move in near_moves:
        move.wait_recv()
    last = []
    for h, at in enumerate(halves):
        far_moves[h].wait_recv()
        last.append(copies.start(gathered.at[2, at], gathered.at[3, at], near))
    attention_back(1)
    results.second_round()
    attention_back(2)
    for move in last:
        move.wait_recv()
    attention_back(3)
    for h, at in enumerate(halves):
        aux = aux_ref[at, :]
        gates = [column(aux, NF + 1 + k) for k in range(3)]
        mixes = [column(aux, MIX + k) for k in range(4)]
        kept = gates[0] + gates[1] * mixes[0] + gates[2] * mixes[2]
        result = hidden_ref[at, :] + kept * normed_two[at, :] + results.total(h)
        for c in range(2):
            result = result + (gates[1 + c] * mixes[2 * c + 1]) * vector_ref[c : c + 1, :]
        result_ref[at, :] = result.astype(BF16)

    def finish_keys(j, carry):
        at = pl.ds(pl.multiple_of(j * BLOCK, BLOCK), BLOCK)
        grad_ref[at, PAD : 2 * PAD] = turned_back(key_sum[at, :], angle_ref[at, :])
        grad_ref[at, 2 * PAD :] = value_sum[at, :].astype(BF16)
        return carry

    lax.fori_loop(0, grad_ref.shape[0] // BLOCK, finish_keys, 0)
    copies.finish()


def branch_back(
    heads, hidden, aux, cotangent, gain, mix, vectors, carried, attended, head_full, queries, keys, values,
    keys_t, rowinfo, colinfo, totals, angles, sums, grad_ins,
):
    rows, width = hidden.shape
    total = queries.shape[0]
    vmem, anywhere = pl.BlockSpec(memory_space=pltpu.VMEM), pl.BlockSpec(memory_space=pl.ANY)
    copies = 2 * 10 + 6
    return pl.pallas_call(
        functools.partial(branch_back_kernel, heads),
        in_specs=[vmem] * 17 + [anywhere] * 2,
        out_specs=[vmem] * 6,
        out_shape=[
            jax.ShapeDtypeStruct((rows, width), F32),
            jax.ShapeDtypeStruct((rows, 128), F32),
            jax.ShapeDtypeStruct((width, PAD), F32),
            jax.ShapeDtypeStruct((24, width + 128), F32),
            jax.ShapeDtypeStruct((total, 3 * PAD), BF16),
            jax.ShapeDtypeStruct((rows, width), BF16),
        ],
        scratch_shapes=[
            pltpu.VMEM((rows, width), F32),
            pltpu.VMEM((rows, width), F32),
            pltpu.VMEM((4, rows, width), BF16),
            pltpu.VMEM((total, PAD), BF16),
            pltpu.VMEM((total, PAD), F32),
            pltpu.VMEM((total, PAD), F32),
            pltpu.VMEM((PAD, BLOCK), F32),
            pltpu.SemaphoreType.DMA((copies,)),
            pltpu.SemaphoreType.DMA((copies,)),
            pltpu.SemaphoreType.DMA((2, 4)),
        ]
        + PairSum.shapes(rows, grad_ins.shape[2])
        + PairSum.shapes(rows, width),
        compiler_params=pltpu.CompilerParams(
            collective_id=2, has_side_effects=True, vmem_limit_bytes=61 << 20
        ),
        cost_estimate=pl.CostEstimate(
            flops=256 * rows * width * PAD, bytes_accessed=64 * rows * width, transcendentals=0
        ),
    )(
        hidden, aux, cotangent, gain[None], mix, vectors, carried, attended, head_full[:, 3 * PAD :],
        queries, keys, values, keys_t, rowinfo, colinfo, totals, angles, sums, grad_ins,
    )


def finish_kernel(
    columns, grad_ref, one_ref, head_ref, grad_out_ref, small_ref, grad_hidden_ref, tok_ref, gain_ref,
    *refs
):
    grad_tok_ref, pack_ref, sum_ref, refs = refs[0], refs[1], refs[2], refs[3:]
    near_send, near_recv, far_send, far_recv, send_sems, recv_sems = refs[:6]
    near, far, across, *column = enter(columns)
    copies = Copies(send_sems, recv_sems)
    dp = lax.axis_index("dp")
    rows, width = tok_ref.shape
    share = width // 8

    def part(bits):
        return dot_nt(quarter(grad_ref, bits, rows)[...], head_ref[:, : 3 * PAD])

    mine, moves = sum_of_quarters(
        part, copies, near, far, near_send, near_recv, far_send, far_recv
    )
    grad_tok_ref[...] = mine

    packed = refs[6] if columns else pack_ref
    along = jnp.zeros((8, width), F32)
    rest = None
    for section in range(4):
        at = slice(section * PAD, (section + 1) * PAD)
        if section < 3:
            grad = dot_tn(one_ref[...], grad_ref[:, at])
            along = along + lax.dot_general(
                jnp.ones((8, PAD), F32),
                grad * head_ref[:, at].astype(F32),
                (((1,), (1,)), ((), ())),
                precision=HIGHEST,
                preferred_element_type=F32,
            )
        else:
            grad = grad_out_ref[...]
        if not columns:
            packed[:, at] = grad.astype(BF16)
            continue
        low, high = grad[:, :128].astype(BF16), grad[:, 128:]
        if section % 2 == 0:
            rest = high
        else:
            lane = lax.broadcasted_iota(jnp.int32, high.shape, 1)
            rest = jnp.where(lane < 64, rest, pltpu.roll(high, 64, 1)).astype(BF16)
        for d in range(8):
            cut = slice(d * share, (d + 1) * share)
            packed[d, :, section * 128 : (section + 1) * 128] = low[cut]
            if section % 2:
                start = 512 + 128 * (section // 2)
                packed[d, :, start : start + 128] = rest[cut]
    small = small_ref[...]
    row = lax.broadcasted_iota(jnp.int32, (24, width), 0)
    small = jnp.concatenate(
        [
            jnp.where(row == 19, along[:1] / gain_ref[...], small[:, :width]),
            small[:, width:],
        ],
        axis=1,
    )
    if columns:
        _, pair_recv, column_send, column_recv, sums, sum_recv = refs[6:]
        pair_moves = []
        for j in range(4):
            there = lax.rem(other(dp, 1) + 2 * j, 8)
            pair_moves.append(copies.start(packed.at[there], pair_recv.at[j], across))
        sums[0] = small
        steps = [near, far, across, (other(dp, 2), lax.axis_index("tensor")), column[1]]
        sum_moves = [copies.start(sums.at[0], sum_recv.at[0], steps[0])]

        def add_up():
            k = len(sum_moves)
            sum_moves[-1].wait_recv()
            if k < 5:
                sums[k] = sums[k - 1] + sum_recv[k - 1]
                sum_moves.append(copies.start(sums.at[k], sum_recv.at[k], steps[k]))
            else:
                sum_ref[...] = sums[4] + sum_recv[4]

        add_up()
        add_up()
        column_moves = []
        for j in (1, 2, 3, 0):
            pair_moves[j].wait_recv()
            paired = packed[lax.rem(dp + 2 * j, 8)].astype(F32) + pair_recv[j].astype(F32)
            if j:
                column_send[j - 1] = paired.astype(BF16)
                column_moves.append(
                    copies.start(column_send.at[j - 1], column_recv.at[j - 1], column[j - 1])
                )
            else:
                pack_ref[...] = paired
        add_up()
    else:
        sum_ref[...] = small

    size = rows // SLICES
    for c in range(SLICES):
        at = pl.ds(c * size, size)
        moves[c].wait_recv()
        grad_normed = grad_tok_ref[at, :] + far_recv[at, :].astype(F32)
        values = tok_ref[at, :].astype(F32)
        scale = lax.rsqrt(jnp.mean(values * values, axis=1, keepdims=True) + epsilon)
        weighted = gain_ref[...] * grad_normed
        inner = jnp.mean(values * weighted, axis=1, keepdims=True)
        grad_tok_ref[at, :] = (
            grad_hidden_ref[at, :] + scale * weighted - values * (scale * scale * scale * inner)
        )
    if columns:
        add_up()
        for j in range(3):
            column_moves[j].wait_recv()
            pack_ref[...] = pack_ref[...] + column_recv[j].astype(F32)
        add_up()
    copies.finish()


def finish(columns, grads, ones, head_full, grad_out, small, grad_hidden, tokens, gain):
    rows, width = tokens.shape
    share = width // 8
    vmem = pl.BlockSpec(memory_space=pltpu.VMEM)
    copies = 2 + SLICES + 12
    pack = (
        jax.ShapeDtypeStruct((share, width), F32)
        if columns
        else jax.ShapeDtypeStruct(head_full.shape, BF16)
    )
    scratch = [
        pltpu.VMEM((2, rows, width), BF16),
        pltpu.VMEM((2, rows, width), BF16),
        pltpu.VMEM((rows, width), BF16),
        pltpu.VMEM((rows, width), BF16),
        pltpu.SemaphoreType.DMA((copies,)),
        pltpu.SemaphoreType.DMA((copies,)),
    ]
    if columns:
        scratch += [
            pltpu.VMEM((8, share, width), BF16),
            pltpu.VMEM((4, share, width), BF16),
            pltpu.VMEM((3, share, width), BF16),
            pltpu.VMEM((3, share, width), BF16),
            pltpu.VMEM((5, *small.shape), F32),
            pltpu.VMEM((5, *small.shape), F32),
        ]
    return pl.pallas_call(
        functools.partial(finish_kernel, columns),
        in_specs=[vmem] * 8,
        out_specs=[vmem] * 3,
        out_shape=[
            jax.ShapeDtypeStruct((rows, width), F32),
            pack,
            jax.ShapeDtypeStruct(small.shape, F32),
        ],
        scratch_shapes=scratch,
        compiler_params=pltpu.CompilerParams(
            collective_id=4, has_side_effects=True, vmem_limit_bytes=56 << 20
        ),
        cost_estimate=pl.CostEstimate(
            flops=32 * rows * width * PAD, bytes_accessed=64 * rows * width, transcendentals=0
        ),
    )(grads, ones, head_full, grad_out, small, grad_hidden, tokens, gain[None])


def route_kernel(routes_ref, rows_ref, cols_ref, info_ref):
    tokens = routes_ref.shape[2]
    expert = lax.broadcasted_iota(jnp.int32, (NF, tokens), 0)
    step = 256
    down = lax.broadcasted_iota(jnp.int32, (step, step), 0)
    across = lax.broadcasted_iota(jnp.int32, (step, step), 1)
    before = jnp.where(down < across, 1.0, 0.0).astype(BF16)
    for a in range(2):
        hot = (expert == routes_ref[a, 0:1, :]) | (expert == routes_ref[a, 1:2, :])
        ones = jnp.where(hot, 1.0, 0.0)
        ranks, so_far = [], jnp.zeros((NF, 1), F32)
        for b in range(tokens // step):
            part = ones[:, b * step : (b + 1) * step]
            ranks.append(dot_nn(part.astype(BF16), before) + so_far)
            so_far = so_far + jnp.sum(part, axis=1, keepdims=True)
        rank = jnp.concatenate(ranks, axis=1)
        slots = jnp.where(hot, rank, -1.0)
        rows_ref[a] = slots.astype(jnp.int32)
        spread = jnp.concatenate([slots, jnp.zeros((128 - NF, tokens), F32)], axis=0)
        cols_ref[a] = spread.T.astype(jnp.int32)
        lane = lax.broadcasted_iota(jnp.int32, (NF, 128), 1)
        info = jnp.where(lane == 0, so_far, 0.0)
        for c in range(2):
            first = jnp.sum(jnp.where(rank + ones <= c * TILE, 1.0, 0.0), axis=1, keepdims=True)
            after = jnp.sum(jnp.where(rank < (c + 1) * TILE, 1.0, 0.0), axis=1, keepdims=True)
            info = jnp.where(lane == 1 + 2 * c, first, jnp.where(lane == 2 + 2 * c, after, info))
        info_ref[a] = info.astype(jnp.int32)


def route(routes):
    tokens = routes.shape[2]
    return pl.pallas_call(
        route_kernel,
        out_shape=[
            jax.ShapeDtypeStruct((2, NF, tokens), jnp.int32),
            jax.ShapeDtypeStruct((2, tokens, 128), jnp.int32),
            jax.ShapeDtypeStruct((2, NF, 128), jnp.int32),
        ],
        cost_estimate=pl.CostEstimate(flops=10**7, bytes_accessed=10**6, transcendentals=0),
    )(routes)


def experts_kernel(
    whole_weights, n_before, base_ref, info_ref, slot_rows_ref, slot_cols_ref, weights_ref, *refs
):
    (rows_in, grads_in), before, refs = refs[:2], refs[2 : 2 + n_before], refs[2 + n_before :]
    sums_out, grad_ins_out, out_ref, rows, grads, sums, grad_ins = refs[:7]
    weight, row_acc, grad_acc, slot_col, inputs, grad_outs, acts, gates, ups, in_sems, out_sems = refs[7:]
    step = pl.program_id(0)
    expert = base_ref[0] + step
    tokens, width = grads.shape[1:]
    wide = rows.shape[2]
    arrivals = [
        [pltpu.make_async_copy(rows_in.at[a], rows.at[a], in_sems.at[a, 0]),
         pltpu.make_async_copy(grads_in.at[a], grads.at[a], in_sems.at[a, 1])]
        + [pltpu.make_async_copy(source.at[a], target.at[a], in_sems.at[a, 2 + k])
           for k, (source, target) in enumerate(zip(before, (sums, grad_ins)))]
        for a in range(2)
    ]
    leaving = [
        [pltpu.make_async_copy(source.at[a], target.at[a], out_sems.at[a, k])
         for k, (source, target) in enumerate(((sums, sums_out), (grad_ins, grad_ins_out)))]
        for a in range(2)
    ]

    @pl.when(step == 0)
    def _():
        for copy in arrivals[0] + arrivals[1]:
            copy.start()
        if not n_before:
            sums[...] = jnp.zeros_like(sums)
            grad_ins[...] = jnp.zeros_like(grad_ins)

    if whole_weights:
        weight[...] = weights_ref[0]
    else:
        depth, _, _, _, share, _ = weights_ref.shape
        for z in range(depth):
            for y in range(2):
                weight[:, pl.ds((2 * z + y) * share, share), :] = weights_ref[z, y, 0]

    def tree(a):
        def dispatch(c, start, count):
            down = c * TILE + lax.broadcasted_iota(jnp.int32, (TILE, 1), 0)
            at = pl.ds(start, count)
            picked = slot_rows_ref[a, pl.ds(expert, 1), at] == down
            picked = jnp.where(picked, 1.0, 0.0).astype(BF16)
            row_acc[...] = dot_nn(picked, rows[a, at, :])
            grad_acc[...] = dot_nn(picked, grads[a, at, :])

        slot_col[...] = pltpu.roll(slot_cols_ref[a], 128 - expert, 1)

        def combine(c, start, count, back):
            across = c * TILE + lax.broadcasted_iota(jnp.int32, (1, TILE), 1)
            size = 256
            for b in range(count // size):
                at = pl.ds(pl.multiple_of(start + b * size, 128), size)
                here = jnp.where(slot_col[at, 0:1] == across, 1.0, 0.0).astype(BF16)
                part = dot_nn(here, back)
                sums[a, at, :] = (sums[a, at, :].astype(F32) + part[:, :width]).astype(BF16)
                grad_ins[a, at, :] = (
                    grad_ins[a, at, :].astype(F32) + part[:, width:]
                ).astype(BF16)

        def tile(c, carry):
            k = 8 * a + expert
            first, after = info_ref[k, 1 + 2 * c], info_ref[k, 2 + 2 * c]
            start = pl.multiple_of(jnp.minimum(first // 128 * 128, tokens - WINDOW), 128)
            narrow = after <= start + WINDOW

            @pl.when(narrow)
            def _():
                dispatch(c, start, WINDOW)

            @pl.when(jnp.logical_not(narrow))
            def _():
                dispatch(c, 0, tokens)

            at = pl.ds(pl.multiple_of((2 * a + c) * TILE, TILE), TILE)
            inputs[at, :] = row_acc[:, :width].astype(BF16)
            lane = lax.broadcasted_iota(jnp.int32, (TILE, wide - width), 1)
            gate = jnp.sum(
                jnp.where(lane == expert, row_acc[:, width:], 0.0), axis=1, keepdims=True
            )
            grad_out = (gate * grad_acc[...]).astype(BF16)
            grad_outs[at, :] = grad_out
            gate_part = dot_nn(inputs[at, :], weight[0])
            up_part = dot_nn(inputs[at, :], weight[1])
            sigmoid = 1.0 / (1.0 + jnp.exp(-gate_part))
            swish = gate_part * sigmoid
            act = (swish * up_part).astype(BF16)
            acts[at, :] = act
            expert_out = dot_nt(act, weight[2])
            along = jnp.sum(expert_out * grad_acc[...], axis=1, keepdims=True)
            grad_act = dot_nn(grad_out, weight[2])
            grad_gate = (
                grad_act * up_part * sigmoid * (1.0 + gate_part * (1.0 - sigmoid))
            ).astype(BF16)
            grad_up = (grad_act * swish).astype(BF16)
            gates[at, :] = grad_gate
            ups[at, :] = grad_up
            grad_in = dot_nt(grad_gate, weight[0]) + dot_nt(grad_up, weight[1])
            back = jnp.concatenate(
                [
                    (gate * expert_out).astype(BF16),
                    grad_in.astype(BF16),
                    jnp.where(lane == expert, along, 0.0).astype(BF16),
                ],
                axis=1,
            )

            @pl.when(narrow)
            def _():
                combine(c, start, WINDOW, back)

            @pl.when(jnp.logical_not(narrow))
            def _():
                combine(c, 0, tokens, back)

            return carry

        tiles = (info_ref[8 * a + expert, 0] + TILE - 1) // TILE

        def empty(c, carry):
            at = pl.ds(pl.multiple_of((2 * a + c) * TILE, TILE), TILE)
            for ref in (inputs, grad_outs, acts, gates, ups):
                ref[at, :] = jnp.zeros((TILE, ref.shape[1]), BF16)
            return carry

        lax.fori_loop(0, tiles, tile, 0)
        lax.fori_loop(tiles, 2, empty, 0)

    for a in range(2):

        @pl.when(step == 0)
        def _(a=a):
            for copy in arrivals[a]:
                copy.wait()

        tree(a)

        @pl.when(step == pl.num_programs(0) - 1)
        def _(a=a):
            for copy in leaving[a]:
                copy.start()

    for k, (left, right) in enumerate(((inputs, gates), (inputs, ups), (grad_outs, acts))):
        size = 256
        for b in range(width // size):
            at = slice(b * size, (b + 1) * size)
            if whole_weights:
                out_ref[0, k, at, :] = dot_tn(left[:, at], right[...]).astype(BF16)
            else:
                weight[k, at, :] = dot_tn(left[:, at], right[...]).astype(BF16)
    if not whole_weights:
        for z in range(depth):
            for y in range(2):
                out_ref[z, y, 0] = weight[:, pl.ds((2 * z + y) * share, share), :]

    @pl.when(step == pl.num_programs(0) - 1)
    def _():
        for copy in leaving[0] + leaving[1]:
            copy.wait()


def experts(base, weights, info, rows, grads, slot_rows, slot_cols, before):
    _, tokens, width = grads.shape
    wide = rows.shape[2]
    whole_weights = weights.ndim == 4
    kinds, share, hidden = weights.shape[-3:]
    group = weights.shape[0] if whole_weights else weights.shape[2]
    depth = width if whole_weights else 2 * weights.shape[0] * share
    whole = lambda a: pl.BlockSpec(a.shape, lambda e, *_: (0,) * a.ndim, pipeline_mode=pl.Buffered(1))
    anywhere = pl.BlockSpec(memory_space=pl.ANY)
    if whole_weights:
        weight_spec = pl.BlockSpec((1, kinds, share, hidden), lambda e, *_: (e, 0, 0, 0))
    else:
        weight_spec = pl.BlockSpec(
            (weights.shape[0], 2, 1, kinds, share, hidden), lambda e, *_: (0, 0, e, 0, 0, 0)
        )
    sums = jax.ShapeDtypeStruct((2, tokens, width), BF16)
    grad_ins = jax.ShapeDtypeStruct((2, tokens, wide), BF16)
    return pl.pallas_call(
        functools.partial(experts_kernel, whole_weights, len(before)),
        grid_spec=pltpu.PrefetchScalarGridSpec(
            num_scalar_prefetch=2,
            grid=(group,),
            in_specs=[whole(slot_rows), whole(slot_cols), weight_spec]
            + [anywhere] * (2 + len(before)),
            out_specs=[anywhere, anywhere, weight_spec],
            scratch_shapes=[
                pltpu.VMEM((2, tokens, wide), BF16),
                pltpu.VMEM((2, tokens, width), BF16),
                pltpu.VMEM((2, tokens, width), BF16),
                pltpu.VMEM((2, tokens, wide), BF16),
                pltpu.VMEM((kinds, depth, hidden), BF16),
                pltpu.VMEM((TILE, wide), F32),
                pltpu.VMEM((TILE, width), F32),
                pltpu.VMEM((tokens, 128), jnp.int32),
                pltpu.VMEM((4 * TILE, width), BF16),
                pltpu.VMEM((4 * TILE, width), BF16),
                pltpu.VMEM((4 * TILE, hidden), BF16),
                pltpu.VMEM((4 * TILE, hidden), BF16),
                pltpu.VMEM((4 * TILE, hidden), BF16),
                pltpu.SemaphoreType.DMA((2, 4)),
                pltpu.SemaphoreType.DMA((2, 2)),
            ],
        ),
        out_shape=[sums, grad_ins, jax.ShapeDtypeStruct(weights.shape, BF16)],
        compiler_params=pltpu.CompilerParams(vmem_limit_bytes=60 << 20),
        cost_estimate=pl.CostEstimate(
            flops=group * tokens * width * (9 * hidden + 4 * tokens),
            bytes_accessed=16 * tokens * width,
            transcendentals=0,
        ),
    )(base, info, slot_rows, slot_cols, weights, rows, grads, *before)


def per_device(
    tokens_in,
    carried_logits,
    cotangent,
    segment_ids,
    parent_ids,
    routes,
    attention_gain,
    head_weight,
    output_weight,
    expert_gain,
    router_weight,
    carry_weight,
    constant_gate,
    constant_vector,
    expert_first,
    expert_second,
):
    row_count, width = tokens_in.shape
    tree_len = segment_ids.shape[0]
    head_width = head_weight.shape[2]
    heads = head_width // HEAD
    share = head_weight.shape[1]
    parity = lax.axis_index("dp") % 2
    index = lax.axis_index("tensor")
    own_experts = NF // 2
    group = own_experts // GROUPS
    layered = share % 16 == 0

    columns = lax.axis_size("dp") == 8

    def gather_experts(shards):
        gathered = gather_column(shards)
        if layered:
            return gathered
        return gathered.transpose(2, 3, 0, 1, 4, 5).reshape(group, 3, width, -1)

    sections = jnp.concatenate([head_weight, output_weight.T[None]], axis=0).astype(BF16)
    spread = lambda a, to: jnp.pad(a, ((0, 0), (0, to - a.shape[1])))
    if columns:
        pack = jnp.concatenate(
            [sections[k, :, :128] for k in range(4)] + [sections[k, :, 128:] for k in range(4)], axis=1
        )
    else:
        pack = jnp.concatenate([spread(sections[k], PAD) for k in range(4)], axis=1)
        pack = gather_column(pack)
        pack = jnp.moveaxis(by_parity(pack, swap(pack, "dp", 1)), 0, 1).reshape(width, 4 * PAD)
    expert_pack = jnp.concatenate(
        [expert_first.astype(BF16), expert_second.astype(BF16).transpose(0, 2, 1)[:, None]], axis=1
    )
    kept = lax.dynamic_slice_in_dim(expert_pack, parity * own_experts, own_experts, 0)
    given = lax.dynamic_slice_in_dim(expert_pack, (1 - parity) * own_experts, own_experts, 0)
    first = slice(0, group)
    shards = by_parity(kept[first], swap(given[first], "dp", 1))
    pack, shards = together(pack, shards)
    expert_weights = [gather_experts(shards)]

    slot_rows, slot_cols, info = route(jnp.stack([routes.T, swap(routes.T, "dp", 1)]))
    info = info.reshape(2 * NF, -1)[:, :8]

    angles = rotary_angles(segment_ids, parent_ids)
    rowinfo = jnp.pad(jnp.stack([segment_ids, parent_ids]), ((0, 6), (0, 0)))
    colinfo = rowinfo.T
    queries, keys, values, keys_t, values_t, gathered_one, head_full = project(
        columns, tokens_in, attention_gain, angles, pack
    )
    queries, kept, given = together(queries, kept, given)
    shards = [
        by_parity(kept[at], swap(given[at], "dp", 1))
        for at in [slice(g * group, (g + 1) * group) for g in range(1, GROUPS)]
    ]
    expert_weights += [gather_experts(s) for s in shards]
    local_routes = lax.dynamic_slice_in_dim(routes, index * row_count, row_count, 0)
    picked = jnp.sum(
        (local_routes[:, :, None] == jnp.arange(128, dtype=jnp.int32)).astype(F32), axis=1
    )
    carried_part = spread(jnp.dot(carried_logits, carry_weight, precision=HIGHEST), 128)
    mix_weight = spread(jnp.concatenate([spread(router_weight, MIX), constant_gate], axis=1), 128)
    attended, totals, hidden, aux, expert_rows, grad_rows = branch(
        heads, queries, keys, values_t, rowinfo, colinfo, cotangent, head_full, tokens_in, expert_gain,
        carried_part, mix_weight, picked,
    )

    parts, own_grads = [], []
    for g in range(GROUPS):
        base = (parity * own_experts + g * group).astype(jnp.int32).reshape(1)
        *parts, weight_grads = experts(
            base, expert_weights[g], info, expert_rows, grad_rows, slot_rows, slot_cols, parts
        )
        if not layered:
            weight_grads = weight_grads.reshape(group, 3, -1, 2, share, weight_grads.shape[-1])
            weight_grads = weight_grads.transpose(2, 3, 0, 1, 4, 5)
        own_grads.append(scatter_column(weight_grads))
    sums, grad_ins = parts

    vectors = jnp.pad(constant_vector, ((0, 6), (0, 0)))
    grad_hidden, grad_logits, grad_output_t, small, grad_projected, output = branch_back(
        heads, hidden, aux, cotangent, expert_gain, mix_weight, vectors, spread(carried_logits, 128),
        attended, head_full, queries, keys, values, keys_t, rowinfo, colinfo, totals, angles, sums,
        grad_ins,
    )
    grad_carried = lax.dot_general(
        grad_logits[:, :NE], carry_weight, (((1,), (1,)), ((), ())), precision=HIGHEST
    )
    grad_projected, own_grads[0] = together(grad_projected, own_grads[0])
    grad_tokens, own_pack, small = finish(
        columns, grad_projected, gathered_one, head_full, grad_output_t, small, grad_hidden, tokens_in,
        attention_gain,
    )
    if columns:
        own_sections = [
            jnp.concatenate(
                [own_pack[:, 128 * k : 128 * (k + 1)], own_pack[:, 512 + 64 * k : 576 + 64 * k]], axis=1
            )
            for k in range(4)
        ]
    else:
        blocks = own_pack.reshape(-1, 2, share, 4 * PAD)
        kept = lax.dynamic_index_in_dim(blocks, parity, 1, keepdims=False)
        given = lax.dynamic_index_in_dim(blocks, 1 - parity, 1, keepdims=False)
        paired = kept.astype(F32) + swap(given, "dp", 1).astype(F32)
        own_pack = scatter_column(paired.astype(BF16)).astype(F32)
        own_sections = [own_pack[:, k * PAD : k * PAD + head_width] for k in range(4)]
        small = lax.psum(small, ("dp", "tensor"))
    own_grads = jnp.concatenate(own_grads, axis=1)
    kept = lax.dynamic_index_in_dim(own_grads, parity, 0, keepdims=False)
    given = lax.dynamic_index_in_dim(own_grads, 1 - parity, 0, keepdims=False)
    own_grads = by_parity(kept, swap(given, "dp", 1)).reshape(NF, 3, share, -1).astype(F32)
    grad_first = own_grads[:, :2]
    grad_second = own_grads[:, 2].transpose(0, 2, 1)
    return (
        output,
        grad_tokens,
        grad_carried,
        small[19, :width],
        jnp.stack(own_sections[:3]),
        own_sections[3].T,
        small[16, :width],
        small[:NE, :width].T,
        small[:NE, width : width + NE],
        small[MIX : MIX + 4, :width].T,
        small[17:19, :width],
        grad_first,
        grad_second,
    )


def solution(mesh):
    in_specs = (
        P(("dp", "tensor"), None),
        P(("dp", "tensor"), None),
        P(("dp", "tensor"), None),
        P("dp"),
        P("dp"),
        P("dp", None),
        P(),
        P(None, "dp", "tensor"),
        P("tensor", "dp"),
        P(),
        P(),
        P(),
        P(),
        P(),
        P(None, None, "dp", "tensor"),
        P(None, "tensor", "dp"),
    )
    out_specs = (
        P(("dp", "tensor"), None),
        P(("dp", "tensor"), None),
        P(("dp", "tensor"), None),
        P(),
        P(None, "dp", "tensor"),
        P("tensor", "dp"),
        P(),
        P(),
        P(),
        P(),
        P(),
        P(None, None, "dp", "tensor"),
        P(None, "tensor", "dp"),
    )
    return jax.shard_map(
        per_device, mesh=mesh, in_specs=in_specs, out_specs=out_specs, check_vma=False
    )
```

```python
import functools

import jax
import jax.numpy as jnp
from jax import lax
from jax.experimental import pallas as pl
from jax.experimental.pallas import tpu as pltpu
from jax.sharding import PartitionSpec as P

HEAD = 64
NF = 8
NSEG = 13
NE = 12
PAD = 256
BLOCK = 512
SLICES = 4
MIX = 12
WINDOW = 1280
TILE = 256
GROUPS = 2

epsilon = 1e-06
HIGHEST = lax.Precision.HIGHEST
F32 = jnp.float32
BF16 = jnp.bfloat16
MESH = pl.DeviceIdType.MESH


def dot_nn(a, b):
    return lax.dot_general(a, b, (((1,), (0,)), ((), ())), preferred_element_type=F32)


def dot_nt(a, b):
    return lax.dot_general(a, b, (((1,), (1,)), ((), ())), preferred_element_type=F32)


def dot_tn(a, b):
    return lax.dot_general(a, b, (((0,), (0,)), ((), ())), preferred_element_type=F32)


def normed(values, gain_vector):
    return (
        values
        * lax.rsqrt(jnp.mean(values * values, axis=-1, keepdims=True) + epsilon)
        * gain_vector
    )


def tree_positions(segment, parent):
    token_count = segment.shape[0]
    labels = jnp.arange(NSEG, dtype=jnp.int32)
    own_hot = (segment[:, None] == labels[None, :]).astype(jnp.int32)
    parent_hot = (parent[:, None] == labels[None, :]).astype(jnp.int32)
    lengths = jnp.sum(own_hot, axis=0)
    starts = jnp.cumsum(lengths) - lengths
    own_start = jnp.sum(own_hot * starts[None, :], axis=1)
    parent_length = jnp.sum(parent_hot * lengths[None, :], axis=1)
    position_index = jnp.arange(token_count, dtype=jnp.int32)
    return (
        position_index
        - own_start
        + jnp.where(segment > 0, lengths[0], 0)
        + jnp.where(parent > 0, parent_length, 0)
    )


def rotary_angles(segment, parent):
    angle_rate = 10000.0 ** (-2.0 * jnp.arange(HEAD // 2, dtype=F32) / HEAD)
    angles = tree_positions(segment, parent).astype(F32)[:, None] * angle_rate[None, :]
    return jnp.concatenate([jnp.cos(angles), jnp.sin(angles)], axis=1)


def swap(values, axis, bits):
    size = lax.axis_size(axis)
    return lax.ppermute(values, axis, [(i, i ^ bits) for i in range(size)])


def together(*values):
    return lax.optimization_barrier(values)


def column_groups():
    size = lax.axis_size("dp")
    return [list(range(first, size, 2)) for first in range(2)]


def gather_column(own):
    return lax.all_gather(own, "dp", axis=0, tiled=False, axis_index_groups=column_groups())


def scatter_column(parts):
    return lax.psum_scatter(
        parts, "dp", scatter_dimension=0, tiled=False, axis_index_groups=column_groups()
    )


def by_parity(mine, other):
    even = lax.axis_index("dp") % 2 == 0
    return jnp.stack([jnp.where(even, mine, other), jnp.where(even, other, mine)])


def swap_halves(values):
    lane = lax.broadcasted_iota(jnp.int32, values.shape, 1)
    half = HEAD // 2
    return jnp.where(
        lane % HEAD < half, pltpu.roll(values, PAD - half, 1), pltpu.roll(values, half, 1)
    )


def rotation(angles):
    half = HEAD // 2
    source = lax.broadcasted_iota(jnp.int32, (2 * half, PAD), 0)
    lane = lax.broadcasted_iota(jnp.int32, (2 * half, PAD), 1)
    to_cos = (source == lane % half).astype(F32)
    to_sin = jnp.where(
        source == half + lane % half, jnp.where(lane % HEAD < half, -1.0, 1.0), 0.0
    )
    return [
        lax.dot_general(
            angles, where, (((1,), (0,)), ((), ())), precision=HIGHEST, preferred_element_type=F32
        )
        for where in (to_cos, to_sin)
    ]


def project_kernel(columns, tok_ref, gain_ref, angle_ref, pack_ref, *refs):
    if columns:
        given_ref, refs = refs[0], refs[1:]
    q_ref, k_ref, v_ref, kt_ref, vt_ref, one_ref = refs[:6]
    if columns:
        head_ref, received_ref, gathered, shards, send_sems, recv_sems = refs[6:]
    else:
        head_ref, (gathered, send_sems, recv_sems) = pack_ref, refs[6:]
    near, far, across, *column = enter(columns)
    copies = Copies(send_sems, recv_sems)
    dp, tensor = lax.axis_index("dp"), lax.axis_index("tensor")
    rows, width = tok_ref.shape
    share = pack_ref.shape[0]
    heads, last = [], []
    if columns:
        heads = [copies.start(pack_ref, shards.at[dp], device) for device in column]
        last.append(copies.start(pack_ref, shards.at[dp], across))
        shards[dp] = pack_ref[...]
    size = rows // SLICES
    slices = [pl.ds(c * size, size) for c in range(SLICES)]
    far_moves, near_moves = [], []
    for at in slices:
        values = tok_ref[at, :].astype(F32)
        scale = lax.rsqrt(jnp.mean(values * values, axis=1, keepdims=True) + epsilon)
        gathered[0, at, :] = (values * scale * gain_ref[...]).astype(BF16)
        far_moves.append(copies.start(gathered.at[0, at], gathered.at[2, at], far))
        near_moves.append(copies.start(gathered.at[0, at], gathered.at[1, at], near))
    corner_moves = []
    for c, at in enumerate(slices):
        far_moves[c].wait_recv()
        corner_moves.append(copies.start(gathered.at[2, at], gathered.at[3, at], near))
        if c < len(heads):
            heads[c].wait_recv()
            origin = lax.rem(dp + 8 - 2 * (c + 1), 8)
            last.append(copies.start(shards.at[origin], shards.at[origin], across))
    beside = [copies.start(given_ref, received_ref, across)] if columns else []
    for move in last + near_moves + corner_moves:
        move.wait_recv()
    if columns:
        for d in range(8):
            at = pl.ds(d * share, share)
            piece = shards[d]
            for section in range(4):
                head_ref[at, section * PAD : section * PAD + 128] = piece[
                    :, section * 128 : (section + 1) * 128
                ]
                start = 512 + 128 * (section // 2)
                rest = piece[:, start : start + 128].astype(F32)
                if section % 2:
                    rest = pltpu.roll(rest, 64, 1)
                lane = lax.broadcasted_iota(jnp.int32, rest.shape, 1)
                head_ref[at, section * PAD + 128 : (section + 1) * PAD] = jnp.where(
                    lane < 64, rest, 0.0
                ).astype(BF16)
    for bits in range(4):
        start = pl.multiple_of(other(tensor, bits) * rows, rows)
        at = pl.ds(start, rows)
        values = gathered[bits]
        one_ref[at, :] = values
        cosine, sine = rotation(angle_ref[at, :])
        part = dot_nn(values, head_ref[:, :PAD])
        q_ref[at, :] = ((part * cosine + swap_halves(part) * sine) * HEAD**-0.5).astype(BF16)
        part = dot_nn(values, head_ref[:, PAD : 2 * PAD])
        part = part * cosine + swap_halves(part) * sine
        k_ref[at, :] = part.astype(BF16)
        kt_ref[:, at] = part.T.astype(BF16)
        part = dot_nn(values, head_ref[:, 2 * PAD : 3 * PAD])
        v_ref[at, :] = part.astype(BF16)
        vt_ref[:, at] = part.T.astype(BF16)
    for move in beside:
        move.wait_recv()
    copies.finish()


def project(columns, tokens, gain, angles, pack, given):
    rows, width = tokens.shape
    total = angles.shape[0]
    vmem = pl.BlockSpec(memory_space=pltpu.VMEM)
    copies = 3 * SLICES + 8
    anywhere = pl.BlockSpec(memory_space=pl.ANY)
    wide = jax.ShapeDtypeStruct((total, PAD), BF16)
    tall = jax.ShapeDtypeStruct((PAD, total), BF16)
    shapes = [wide, wide, wide, tall, tall, jax.ShapeDtypeStruct((total, width), BF16)]
    scratch = [pltpu.VMEM((4, rows, width), BF16)]
    arguments, extra = [tokens, gain[None], angles, pack], []
    if columns:
        shapes.append(jax.ShapeDtypeStruct((width, 4 * PAD), BF16))
        scratch.append(pltpu.VMEM((8, *pack.shape), BF16))
        arguments.append(given)
        extra.append(jax.ShapeDtypeStruct(given.shape, BF16))
    out = pl.pallas_call(
        functools.partial(project_kernel, columns),
        in_specs=[vmem] * 4 + [anywhere] * len(extra),
        out_specs=[vmem] * len(shapes) + [anywhere] * len(extra),
        out_shape=shapes + extra,
        scratch_shapes=scratch
        + [pltpu.SemaphoreType.DMA((copies,)), pltpu.SemaphoreType.DMA((copies,))],
        compiler_params=pltpu.CompilerParams(
            collective_id=3, has_side_effects=True, vmem_limit_bytes=56 << 20
        ),
        cost_estimate=pl.CostEstimate(
            flops=6 * total * width * PAD, bytes_accessed=16 * total * width, transcendentals=0
        ),
    )(*arguments)
    return out if columns else [*out, pack, swap(given, "dp", 1)]


def head_mask(values, head):
    lane = lax.broadcasted_iota(jnp.int32, values.shape, 1)
    return jnp.where(lane // HEAD == head, values, jnp.zeros_like(values))


def seen(i, j, seg_row, par_row, seg_col):
    key_at = j * BLOCK + lax.broadcasted_iota(jnp.int32, (BLOCK, 1), 0)
    query_at = i * BLOCK + lax.broadcasted_iota(jnp.int32, (1, BLOCK), 1)
    related = (seg_col == seg_row) | (seg_col == par_row) | (seg_col == 0)
    return related & (key_at <= query_at)


def attend_block(heads, i, q_ref, k_ref, vt_ref, rowinfo_ref, colinfo_ref, o_ref, total_ref):
    here = pl.ds(pl.multiple_of(i * BLOCK, BLOCK), BLOCK)
    queries = q_ref[here, :]
    by_head = [head_mask(queries, h) for h in range(heads)]
    seg_row, par_row = rowinfo_ref[0:1, here], rowinfo_ref[1:2, here]

    def step(j, carry):
        at = pl.ds(pl.multiple_of(j * BLOCK, BLOCK), BLOCK)
        keys = k_ref[at, :]
        visible = seen(i, j, seg_row, par_row, colinfo_ref[at, 0:1])
        out = []
        for h in range(heads):
            top, total, mixed = carry[h]
            scores = jnp.where(visible, dot_nt(keys, by_head[h]), -1e30)
            new_top = jnp.maximum(top, jnp.max(scores, axis=0, keepdims=True))
            shrink = jnp.exp(top - new_top)
            probs = jnp.exp(scores - new_top)
            total = total * shrink + jnp.sum(probs, axis=0, keepdims=True)
            mixed = mixed * shrink + dot_nn(
                vt_ref[h * HEAD : (h + 1) * HEAD, at], probs.astype(BF16)
            )
            out.append((new_top, total, mixed))
        return tuple(out)

    start = tuple(
        (
            jnp.full((1, BLOCK), -1e30, F32),
            jnp.zeros((1, BLOCK), F32),
            jnp.zeros((HEAD, BLOCK), F32),
        )
        for _ in range(heads)
    )
    done = lax.fori_loop(0, i + 1, step, start)
    mixed = [m / t for _, t, m in done] + [jnp.zeros((PAD - heads * HEAD, BLOCK), F32)]
    o_ref[here, :] = jnp.concatenate(mixed, axis=0).T.astype(BF16)
    total_ref[:, here] = jnp.concatenate(
        [m + jnp.log(t) for m, t, _ in done] + [jnp.zeros((8 - heads, BLOCK), F32)], axis=0
    )


def other(place, bits):
    if bits & 2:
        place = place + 2 - 4 * lax.rem(lax.div(place, 2), 2)
    if bits & 1:
        place = place + 1 - 2 * lax.rem(place, 2)
    return place


def enter(columns=False):
    dp, tensor = lax.axis_index("dp"), lax.axis_index("tensor")
    others = [(dp, other(tensor, 1)), (dp, other(tensor, 2)), (other(dp, 1), tensor)]
    if columns:
        others += [(lax.rem(dp + 2 * j, 8), tensor) for j in (1, 2, 3)]
    barrier = pltpu.get_barrier_semaphore()
    for device in others:
        pl.semaphore_signal(barrier, inc=1, device_id=device, device_id_type=MESH)
    pl.semaphore_wait(barrier, len(others))
    return others


class Copies:
    def __init__(self, send_sems, recv_sems):
        self.send_sems, self.recv_sems, self.made = send_sems, recv_sems, []

    def start(self, source, target, device):
        k = len(self.made)
        copy = pltpu.make_async_remote_copy(
            src_ref=source,
            dst_ref=target,
            send_sem=self.send_sems.at[k],
            recv_sem=self.recv_sems.at[k],
            device_id=device,
            device_id_type=MESH,
        )
        copy.start()
        self.made.append(copy)
        return copy

    def finish(self):
        for copy in self.made:
            copy.wait_send()


def quarter(ref, bits, rows):
    place = other(lax.axis_index("tensor"), bits)
    return ref.at[pl.ds(pl.multiple_of(place * rows, rows), rows)]


def sum_of_quarters(part, copies, near, far, near_send, near_recv, far_send, far_recv):
    rows = far_send.shape[0]
    near_send[0] = part(3).astype(BF16)
    first = copies.start(near_send.at[0], near_recv.at[0], near)
    near_send[1] = part(1).astype(BF16)
    second = copies.start(near_send.at[1], near_recv.at[1], near)
    mine = part(2)
    first.wait_recv()
    far_send[...] = (mine + near_recv[0].astype(F32)).astype(BF16)
    moves = []
    for c in range(SLICES):
        at = pl.ds(c * rows // SLICES, rows // SLICES)
        moves.append(copies.start(far_send.at[at], far_recv.at[at], far))
    mine = part(0)
    second.wait_recv()
    return mine + near_recv[1].astype(F32), moves


class Spread:
    def __init__(self, copies, devices, target, rows):
        self.copies, (self.near, self.far, self.across) = copies, devices
        self.rows, self.own, self.beside = rows, quarter(target.at[0], 0, rows), quarter(target.at[1], 0, rows)
        self.over, self.corner = quarter(target.at[0], 2, rows), quarter(target.at[1], 2, rows)
        self.from_far, self.from_across, self.from_corner, self.ends = {}, {}, {}, []

    def send(self, source, at, c):
        copies = self.copies
        self.from_far[c] = copies.start(source.at[at], self.own.at[at], self.far)
        self.from_across[c] = copies.start(source.at[at], self.beside.at[at], self.across)
        self.ends.append(copies.start(source.at[at], self.own.at[at], self.near))

    def pass_on(self, c, at):
        copies = self.copies
        self.from_far[c].wait_recv()
        if c >= SLICES // 2:
            self.from_corner[c] = copies.start(self.over.at[at], self.corner.at[at], self.across)
        self.ends.append(copies.start(self.over.at[at], self.over.at[at], self.near))
        self.from_across[c].wait_recv()
        if c < SLICES // 2:
            self.from_corner[c] = copies.start(self.beside.at[at], self.beside.at[at], self.far)
        self.ends.append(copies.start(self.beside.at[at], self.beside.at[at], self.near))

    def pass_corner(self, c, at):
        self.from_corner[c].wait_recv()
        self.ends.append(self.copies.start(self.corner.at[at], self.corner.at[at], self.near))

    def finish(self):
        for copy in self.ends:
            copy.wait_recv()


def branch_kernel(
    heads, q_ref, k_ref, vt_ref, rowinfo_ref, colinfo_ref, cot_ref,
    out_ref, tok_ref, gain_ref, carried_ref, mix_ref, picked_ref,
    att_ref, total_ref, hidden_ref, aux_ref, rows_ref, cots_ref,
    near_send, near_recv, far_send, far_recv, own, send_sems, recv_sems, local_sems,
):
    devices = enter()
    near, far, _ = devices
    copies = Copies(send_sems, recv_sems)
    rows, width = tok_ref.shape
    weights = out_ref[:, 3 * PAD :]
    size = rows // SLICES
    slices = [pl.ds(c * size, size) for c in range(SLICES)]
    locals_ = [pltpu.make_async_copy(cot_ref, quarter(cots_ref.at[0], 0, rows), local_sems.at[0])]
    locals_[0].start()
    cots = Spread(copies, devices, cots_ref, rows)
    for c, at in enumerate(slices):
        cots.send(cot_ref, at, c)

    def part(bits):
        if bits == 0:
            for c, at in enumerate(slices):
                cots.pass_on(c, at)
        place = other(lax.axis_index("tensor"), bits)
        for block in range(rows // BLOCK):
            attend_block(
                heads, place * (rows // BLOCK) + block,
                q_ref, k_ref, vt_ref, rowinfo_ref, colinfo_ref, att_ref, total_ref,
            )
        return dot_nt(quarter(att_ref, bits, rows)[...], weights)

    mine, moves = sum_of_quarters(
        part, copies, near, far, near_send, near_recv, far_send, far_recv
    )
    hidden_ref[...] = tok_ref[...].astype(F32) + mine
    spread = Spread(copies, devices, rows_ref, rows)
    for c, at in enumerate(slices):
        moves[c].wait_recv()
        hidden = hidden_ref[at, :] + far_recv[at, :].astype(F32)
        hidden_ref[at, :] = hidden
        scale = lax.rsqrt(jnp.mean(hidden * hidden, axis=1, keepdims=True) + epsilon)
        normed_two = hidden * scale * gain_ref[...]
        logits = carried_ref[at, :] + lax.dot_general(
            normed_two,
            mix_ref[...],
            (((1,), (0,)), ((), ())),
            precision=HIGHEST,
            preferred_element_type=F32,
        )
        picked = picked_ref[at, :] > 0
        top = jnp.max(jnp.where(picked, logits, -1e30), axis=1, keepdims=True)
        weight = jnp.where(picked, jnp.exp(jnp.where(picked, logits - top, 0.0)), 0.0)
        gate = weight / jnp.sum(weight, axis=1, keepdims=True)
        lane = lax.broadcasted_iota(jnp.int32, logits.shape, 1)
        turned = jnp.where(
            lane % 2 == 0, pltpu.roll(logits, 127, 1), pltpu.roll(logits, 1, 1)
        )
        top = jnp.maximum(logits, turned)
        mixture = jnp.exp(logits - top) / (jnp.exp(logits - top) + jnp.exp(turned - top))
        aux_ref[at, :] = jnp.where(lane < MIX, gate, jnp.where(lane < MIX + 4, mixture, 0.0))
        own[at, :width] = normed_two.astype(BF16)
        own[at, width:] = jnp.where(lane < NF, gate, 0.0).astype(BF16)
        spread.send(own, at, c)
        local = pltpu.make_async_copy(
            own.at[at], quarter(rows_ref.at[0], 0, rows).at[at], local_sems.at[1 + c]
        )
        local.start()
        locals_.append(local)
    for c, at in enumerate(slices):
        cots.pass_corner(c, at)
    for c, at in enumerate(slices):
        spread.pass_on(c, at)
    for c, at in enumerate(slices):
        spread.pass_corner(c, at)
    cots.finish()
    spread.finish()
    for local in locals_:
        local.wait()
    copies.finish()


def branch(
    heads, queries, keys, values_t, rowinfo, colinfo, cotangent, head_full, tokens, gain, carried, mix,
    picked,
):
    rows, width = tokens.shape
    total = queries.shape[0]
    vmem, anywhere = pl.BlockSpec(memory_space=pltpu.VMEM), pl.BlockSpec(memory_space=pl.ANY)
    copies = 2 + 15 * SLICES
    return pl.pallas_call(
        functools.partial(branch_kernel, heads),
        in_specs=[vmem] * 12,
        out_specs=[vmem] * 4 + [anywhere] * 2,
        out_shape=[
            jax.ShapeDtypeStruct((total, PAD), BF16),
            jax.ShapeDtypeStruct((8, total), F32),
            jax.ShapeDtypeStruct((rows, width), F32),
            jax.ShapeDtypeStruct((rows, 128), F32),
            jax.ShapeDtypeStruct((2, total, width + 128), BF16),
            jax.ShapeDtypeStruct((2, total, width), BF16),
        ],
        scratch_shapes=[
            pltpu.VMEM((2, rows, width), BF16),
            pltpu.VMEM((2, rows, width), BF16),
            pltpu.VMEM((rows, width), BF16),
            pltpu.VMEM((rows, width), BF16),
            pltpu.VMEM((rows, width + 128), BF16),
            pltpu.SemaphoreType.DMA((copies,)),
            pltpu.SemaphoreType.DMA((copies,)),
            pltpu.SemaphoreType.DMA((1 + SLICES,)),
        ],
        compiler_params=pltpu.CompilerParams(
            collective_id=1, has_side_effects=True, vmem_limit_bytes=48 << 20
        ),
        cost_estimate=pl.CostEstimate(
            flops=64 * rows * width * PAD, bytes_accessed=64 * rows * width, transcendentals=0
        ),
    )(
        queries, keys, values_t, rowinfo, colinfo, cotangent, head_full, tokens, gain[None],
        carried, mix, picked,
    )


class PairSum:
    def __init__(self, copies, devices, source, refs, local_sems):
        self.copies, (self.near, self.far, self.across) = copies, devices
        self.source, self.local_sems = source, local_sems
        self.kept, self.near_recv, self.corner_send, self.corner_recv = refs[:4]
        self.far_send, self.far_recv, self.across_send, self.across_recv = refs[4:]
        self.rows = self.far_send.shape[0]
        half = self.rows // 2
        self.halves = [pl.ds(0, half), pl.ds(half, half)]
        self.arrivals, self.locals_, self.from_far, self.from_across = {}, {}, {}, {}

    @staticmethod
    def shapes(rows, wide):
        one, two = (rows, wide), (2, rows // 2, wide)
        return [
            pltpu.VMEM(shape, BF16)
            for shape in ((4, *one), (4, *one), one, two, one, one, one, one)
        ]

    def start(self):
        for b in (3, 1, 2, 0):
            tree, bits = self.source.at[b // 2], 2 * (b % 2)
            self.arrivals[b] = self.copies.start(
                quarter(tree, bits + 1, self.rows), self.near_recv.at[b], self.near
            )
            self.locals_[b] = pltpu.make_async_copy(
                quarter(tree, bits, self.rows), self.kept.at[b], self.local_sems.at[b]
            )
            self.locals_[b].start()

    def joined(self, b, at):
        return self.kept[b, at, :].astype(F32) + self.near_recv[b, at, :].astype(F32)

    def arrived(self, b):
        self.arrivals[b].wait_recv()
        self.locals_[b].wait()

    def first_round(self):
        low, high = self.halves
        self.arrived(3)
        self.corner_send[...] = self.joined(3, pl.ds(0, self.rows)).astype(BF16)
        start = self.copies.start
        self.corner_far = start(self.corner_send.at[low], self.corner_recv.at[0], self.far)
        self.corner_across = start(self.corner_send.at[high], self.corner_recv.at[1], self.across)
        self.arrived(1)
        self.far_send[low, :] = self.joined(1, low).astype(BF16)
        self.from_far[0] = start(self.far_send.at[low], self.far_recv.at[low], self.far)
        self.arrived(2)
        self.across_send[high, :] = self.joined(2, high).astype(BF16)
        self.from_across[1] = start(self.across_send.at[high], self.across_recv.at[high], self.across)

    def second_round(self):
        low, high = self.halves
        start = self.copies.start
        self.corner_far.wait_recv()
        self.across_send[low, :] = (
            self.joined(2, low) + self.corner_recv[0].astype(F32)
        ).astype(BF16)
        self.from_across[0] = start(self.across_send.at[low], self.across_recv.at[low], self.across)
        self.corner_across.wait_recv()
        self.far_send[high, :] = (
            self.joined(1, high) + self.corner_recv[1].astype(F32)
        ).astype(BF16)
        self.from_far[1] = start(self.far_send.at[high], self.far_recv.at[high], self.far)
        self.arrived(0)

    def total(self, h):
        self.from_far[h].wait_recv()
        self.from_across[h].wait_recv()
        at = self.halves[h]
        return (
            self.joined(0, at)
            + self.far_recv[at, :].astype(F32)
            + self.across_recv[at, :].astype(F32)
        )


def attend_back_block(
    heads, i, q_ref, g_ref, o_ref, k_ref, v_ref, kt_ref, rowinfo_ref, colinfo_ref, total_ref, angle_ref,
    grad_ref, key_sum, value_sum, query_sum,
):
    here = pl.ds(pl.multiple_of(i * BLOCK, BLOCK), BLOCK)
    query_sum[...] = jnp.zeros_like(query_sum)
    queries, grads = q_ref[here, :], g_ref[here, :]
    q_heads = [head_mask(queries, h) for h in range(heads)]
    g_heads = [head_mask(grads, h) for h in range(heads)]
    seg_row, par_row = rowinfo_ref[0:1, here], rowinfo_ref[1:2, here]
    product = grads.astype(F32) * o_ref[here, :].astype(F32)
    lane = lax.broadcasted_iota(jnp.int32, (8, PAD), 1)
    which = lax.broadcasted_iota(jnp.int32, (8, PAD), 0)
    delta = lax.dot_general(
        (lane // HEAD == which).astype(F32),
        product,
        (((1,), (1,)), ((), ())),
        precision=HIGHEST,
        preferred_element_type=F32,
    )
    totals = total_ref[:, here]

    def step(j, carry):
        at = pl.ds(pl.multiple_of(j * BLOCK, BLOCK), BLOCK)
        keys, values = k_ref[at, :], v_ref[at, :]
        visible = seen(i, j, seg_row, par_row, colinfo_ref[at, 0:1])
        key_part, value_part = key_sum[at, :], value_sum[at, :]
        for h in range(heads):
            scores = jnp.where(visible, dot_nt(keys, q_heads[h]), -1e30)
            probs = jnp.exp(scores - totals[h : h + 1, :])
            value_part = value_part + dot_nn(probs.astype(BF16), g_heads[h])
            grad_probs = dot_nt(values, g_heads[h])
            grad_scores = (probs * (grad_probs - delta[h : h + 1, :])).astype(BF16)
            key_part = key_part + dot_nn(grad_scores, q_heads[h])
            lanes = slice(h * HEAD, (h + 1) * HEAD)
            query_sum[lanes, :] += dot_nn(kt_ref[lanes, at], grad_scores)
        key_sum[at, :] = key_part
        value_sum[at, :] = value_part
        return carry

    lax.fori_loop(0, i + 1, step, 0)
    grad_ref[here, :PAD] = turned_back(query_sum[...].T * HEAD**-0.5, angle_ref[here, :])


def turned_back(values, angles):
    cosine, sine = rotation(angles)
    return (values * cosine - swap_halves(values) * sine).astype(BF16)


def branch_back_kernel(
    heads, hidden_ref, aux_ref, cot_ref, gain_ref, mix_ref, vector_ref, carried_ref, att_ref, out_ref,
    q_ref, k_ref, v_ref, kt_ref, rowinfo_ref, colinfo_ref, total_ref, angle_ref, sums_ref, grad_ins_ref,
    grad_hidden_ref, grad_logits_ref, grad_out_ref, small_ref, grad_ref, result_ref,
    normed_two, base, gathered, grad_att, key_sum, value_sum, query_sum,
    send_sems, recv_sems, local_sems, *buffers,
):
    devices = enter()
    near, far, _ = devices
    copies = Copies(send_sems, recv_sems)
    rows, width = hidden_ref.shape
    half = rows // 2
    halves = [pl.ds(0, half), pl.ds(half, half)]
    incoming = PairSum(copies, devices, grad_ins_ref, buffers[:8], local_sems.at[0])
    results = PairSum(copies, devices, sums_ref, buffers[8:], local_sems.at[1])
    incoming.start()
    key_sum[...] = jnp.zeros_like(key_sum)
    value_sum[...] = jnp.zeros_like(value_sum)

    gain = gain_ref[...]
    lane = lax.broadcasted_iota(jnp.int32, (half, 128), 1)

    def column(values, at):
        return jnp.sum(jnp.where(lane == at, values, 0.0), axis=1, keepdims=True)

    known = []
    for at in halves:
        hidden, aux, grads = hidden_ref[at, :], aux_ref[at, :], cot_ref[at, :].astype(F32)
        scale = lax.rsqrt(jnp.mean(hidden * hidden, axis=1, keepdims=True) + epsilon)
        normed = hidden * scale * gain
        normed_two[at, :] = normed
        gates = [column(aux, NF + 1 + k) for k in range(3)]
        mixes = [column(aux, MIX + k) for k in range(4)]
        along = jnp.sum(grads * normed, axis=1, keepdims=True)
        vectors = [
            jnp.sum(grads * vector_ref[c : c + 1, :], axis=1, keepdims=True) for c in range(2)
        ]
        kept = gates[0] + gates[1] * mixes[0] + gates[2] * mixes[2]
        base[at, :] = grads * kept
        sums = []
        for c in range(2):
            sums.append(
                jnp.sum(grads * (gates[1 + c] * mixes[2 * c + 1]), axis=0, keepdims=True)
            )
        by_gate = jnp.where(lane == NF + 1, along, 0.0)
        by_mix = jnp.zeros((half, 128), F32)
        for c in range(2):
            first, second = mixes[2 * c], mixes[2 * c + 1]
            by_gate = by_gate + jnp.where(
                lane == NF + 2 + c, first * along + second * vectors[c], 0.0
            )
            d_first, d_second = gates[1 + c] * along, gates[1 + c] * vectors[c]
            inner = first * d_first + second * d_second
            by_mix = by_mix + jnp.where(lane == MIX + 2 * c, first * (d_first - inner), 0.0)
            by_mix = by_mix + jnp.where(lane == MIX + 2 * c + 1, second * (d_second - inner), 0.0)
        known.append((scale, by_gate, by_mix, sums))
    incoming.first_round()
    incoming.second_round()

    gain_sum = jnp.zeros((1, width), F32)
    far_moves, near_moves = [], []
    for h, at in enumerate(halves):
        scale, by_gate, by_mix, _ = known[h]
        arriving = incoming.total(h)
        by_gate = by_gate + jnp.where(lane < NF, arriving[:, width:], 0.0)
        gates = jnp.where(lane < MIX, aux_ref[at, :], 0.0)
        grad_logits = by_mix + gates * (
            by_gate - jnp.sum(gates * by_gate, axis=1, keepdims=True)
        )
        grad_logits_ref[at, :] = grad_logits
        grad_normed = arriving[:, :width] + base[at, :] + lax.dot_general(
            grad_logits,
            mix_ref[...],
            (((1,), (1,)), ((), ())),
            precision=HIGHEST,
            preferred_element_type=F32,
        )
        hidden = hidden_ref[at, :]
        gain_sum = gain_sum + jnp.sum(hidden * scale * grad_normed, axis=0, keepdims=True)
        weighted = gain * grad_normed
        inner = jnp.mean(hidden * weighted, axis=1, keepdims=True)
        grad_hidden = (
            cot_ref[at, :].astype(F32) + scale * weighted - hidden * (scale * scale * scale * inner)
        )
        grad_hidden_ref[at, :] = grad_hidden
        gathered[0, at, :] = grad_hidden.astype(BF16)
        far_moves.append(copies.start(gathered.at[0, at], gathered.at[2, at], far))
        near_moves.append(copies.start(gathered.at[0, at], gathered.at[1, at], near))
    results.start()

    def over_tokens(a, b):
        return lax.dot_general(
            a, b, (((0,), (0,)), ((), ())), precision=HIGHEST, preferred_element_type=F32
        )

    small_ref[...] = jnp.zeros_like(small_ref)
    small_ref[:16, :width] = over_tokens(grad_logits_ref[...], normed_two[...])[:16]
    small_ref[16:, :width] = jnp.concatenate(
        [gain_sum] + [known[0][3][c] + known[1][3][c] for c in range(2)]
        + [jnp.zeros((5, width), F32)],
        axis=0,
    )
    small_ref[:16, width:] = over_tokens(carried_ref[...], grad_logits_ref[...])[:16]

    def attention_back(bits):
        values = gathered[bits]
        quarter(grad_att, bits, rows)[...] = dot_nn(values, out_ref[:, 3 * PAD :]).astype(BF16)
        product = dot_tn(values, quarter(att_ref, bits, rows)[...])
        grad_out_ref[...] = grad_out_ref[...] + product if bits else product
        place = other(lax.axis_index("tensor"), bits)
        for block in range(rows // BLOCK):
            attend_back_block(
                heads, place * (rows // BLOCK) + block, q_ref, grad_att, att_ref, k_ref, v_ref, kt_ref,
                rowinfo_ref, colinfo_ref, total_ref, angle_ref, grad_ref, key_sum, value_sum, query_sum,
            )

    attention_back(0)
    results.first_round()
    for move in near_moves:
        move.wait_recv()
    last = []
    for h, at in enumerate(halves):
        far_moves[h].wait_recv()
        last.append(copies.start(gathered.at[2, at], gathered.at[3, at], near))
    attention_back(1)
    results.second_round()
    attention_back(2)
    for move in last:
        move.wait_recv()
    attention_back(3)
    for h, at in enumerate(halves):
        aux = aux_ref[at, :]
        gates = [column(aux, NF + 1 + k) for k in range(3)]
        mixes = [column(aux, MIX + k) for k in range(4)]
        kept = gates[0] + gates[1] * mixes[0] + gates[2] * mixes[2]
        result = hidden_ref[at, :] + kept * normed_two[at, :] + results.total(h)
        for c in range(2):
            result = result + (gates[1 + c] * mixes[2 * c + 1]) * vector_ref[c : c + 1, :]
        result_ref[at, :] = result.astype(BF16)

    def finish_keys(j, carry):
        at = pl.ds(pl.multiple_of(j * BLOCK, BLOCK), BLOCK)
        grad_ref[at, PAD : 2 * PAD] = turned_back(key_sum[at, :], angle_ref[at, :])
        grad_ref[at, 2 * PAD :] = value_sum[at, :].astype(BF16)
        return carry

    lax.fori_loop(0, grad_ref.shape[0] // BLOCK, finish_keys, 0)
    copies.finish()


def branch_back(
    heads, hidden, aux, cotangent, gain, mix, vectors, carried, attended, head_full, queries, keys, values,
    keys_t, rowinfo, colinfo, totals, angles, sums, grad_ins,
):
    rows, width = hidden.shape
    total = queries.shape[0]
    vmem, anywhere = pl.BlockSpec(memory_space=pltpu.VMEM), pl.BlockSpec(memory_space=pl.ANY)
    copies = 2 * 10 + 6
    return pl.pallas_call(
        functools.partial(branch_back_kernel, heads),
        in_specs=[vmem] * 17 + [anywhere] * 2,
        out_specs=[vmem] * 6,
        out_shape=[
            jax.ShapeDtypeStruct((rows, width), F32),
            jax.ShapeDtypeStruct((rows, 128), F32),
            jax.ShapeDtypeStruct((width, PAD), F32),
            jax.ShapeDtypeStruct((24, width + 128), F32),
            jax.ShapeDtypeStruct((total, 3 * PAD), BF16),
            jax.ShapeDtypeStruct((rows, width), BF16),
        ],
        scratch_shapes=[
            pltpu.VMEM((rows, width), F32),
            pltpu.VMEM((rows, width), F32),
            pltpu.VMEM((4, rows, width), BF16),
            pltpu.VMEM((total, PAD), BF16),
            pltpu.VMEM((total, PAD), F32),
            pltpu.VMEM((total, PAD), F32),
            pltpu.VMEM((PAD, BLOCK), F32),
            pltpu.SemaphoreType.DMA((copies,)),
            pltpu.SemaphoreType.DMA((copies,)),
            pltpu.SemaphoreType.DMA((2, 4)),
        ]
        + PairSum.shapes(rows, grad_ins.shape[2])
        + PairSum.shapes(rows, width),
        compiler_params=pltpu.CompilerParams(
            collective_id=2, has_side_effects=True, vmem_limit_bytes=61 << 20
        ),
        cost_estimate=pl.CostEstimate(
            flops=256 * rows * width * PAD, bytes_accessed=64 * rows * width, transcendentals=0
        ),
    )(
        hidden, aux, cotangent, gain[None], mix, vectors, carried, attended, head_full,
        queries, keys, values, keys_t, rowinfo, colinfo, totals, angles, sums, grad_ins,
    )


def finish_kernel(
    columns, grad_ref, one_ref, head_ref, grad_out_ref, small_ref, grad_hidden_ref, tok_ref, gain_ref,
    *refs
):
    if columns:
        given_ref, received_ref, refs = refs[0], refs[4], refs[1:4] + refs[5:]
    grad_tok_ref, pack_ref, sum_ref, refs = refs[0], refs[1], refs[2], refs[3:]
    near_send, near_recv, far_send, far_recv, send_sems, recv_sems = refs[:6]
    near, far, across, *column = enter(columns)
    copies = Copies(send_sems, recv_sems)
    dp = lax.axis_index("dp")
    rows, width = tok_ref.shape
    share = width // 8

    def part(bits):
        return dot_nt(quarter(grad_ref, bits, rows)[...], head_ref[:, : 3 * PAD])

    mine, moves = sum_of_quarters(
        part, copies, near, far, near_send, near_recv, far_send, far_recv
    )
    grad_tok_ref[...] = mine

    packed = refs[6] if columns else pack_ref
    along = jnp.zeros((8, width), F32)
    rest = None
    for section in range(4):
        at = slice(section * PAD, (section + 1) * PAD)
        if section < 3:
            grad = dot_tn(one_ref[...], grad_ref[:, at])
            along = along + lax.dot_general(
                jnp.ones((8, PAD), F32),
                grad * head_ref[:, at].astype(F32),
                (((1,), (1,)), ((), ())),
                precision=HIGHEST,
                preferred_element_type=F32,
            )
        else:
            grad = grad_out_ref[...]
        if not columns:
            packed[:, at] = grad.astype(BF16)
            continue
        low, high = grad[:, :128].astype(BF16), grad[:, 128:]
        if section % 2 == 0:
            rest = high
        else:
            lane = lax.broadcasted_iota(jnp.int32, high.shape, 1)
            rest = jnp.where(lane < 64, rest, pltpu.roll(high, 64, 1)).astype(BF16)
        for d in range(8):
            cut = slice(d * share, (d + 1) * share)
            packed[d, :, section * 128 : (section + 1) * 128] = low[cut]
            if section % 2:
                start = 512 + 128 * (section // 2)
                packed[d, :, start : start + 128] = rest[cut]
    small = small_ref[...]
    row = lax.broadcasted_iota(jnp.int32, (24, width), 0)
    small = jnp.concatenate(
        [
            jnp.where(row == 19, along[:1] / gain_ref[...], small[:, :width]),
            small[:, width:],
        ],
        axis=1,
    )
    if columns:
        _, pair_recv, column_send, column_recv, sums, sum_recv = refs[6:]
        pair_moves = []
        for j in range(4):
            there = lax.rem(other(dp, 1) + 2 * j, 8)
            pair_moves.append(copies.start(packed.at[there], pair_recv.at[j], across))
        beside = copies.start(given_ref, received_ref, across)
        sums[0] = small
        steps = [near, far, across, (other(dp, 2), lax.axis_index("tensor")), column[1]]
        sum_moves = [copies.start(sums.at[0], sum_recv.at[0], steps[0])]

        def add_up():
            k = len(sum_moves)
            sum_moves[-1].wait_recv()
            if k < 5:
                sums[k] = sums[k - 1] + sum_recv[k - 1]
                sum_moves.append(copies.start(sums.at[k], sum_recv.at[k], steps[k]))
            else:
                sum_ref[...] = sums[4] + sum_recv[4]

        add_up()
        add_up()
        column_moves = []
        for j in (1, 2, 3, 0):
            pair_moves[j].wait_recv()
            paired = packed[lax.rem(dp + 2 * j, 8)].astype(F32) + pair_recv[j].astype(F32)
            if j:
                column_send[j - 1] = paired.astype(BF16)
                column_moves.append(
                    copies.start(column_send.at[j - 1], column_recv.at[j - 1], column[j - 1])
                )
            else:
                pack_ref[...] = paired
        add_up()
    else:
        sum_ref[...] = small

    size = rows // SLICES
    for c in range(SLICES):
        at = pl.ds(c * size, size)
        moves[c].wait_recv()
        grad_normed = grad_tok_ref[at, :] + far_recv[at, :].astype(F32)
        values = tok_ref[at, :].astype(F32)
        scale = lax.rsqrt(jnp.mean(values * values, axis=1, keepdims=True) + epsilon)
        weighted = gain_ref[...] * grad_normed
        inner = jnp.mean(values * weighted, axis=1, keepdims=True)
        grad_tok_ref[at, :] = (
            grad_hidden_ref[at, :] + scale * weighted - values * (scale * scale * scale * inner)
        )
    if columns:
        add_up()
        for j in range(3):
            column_moves[j].wait_recv()
            pack_ref[...] = pack_ref[...] + column_recv[j].astype(F32)
        add_up()
        beside.wait_recv()
    copies.finish()


def finish(columns, grads, ones, head_full, grad_out, small, grad_hidden, tokens, gain, given):
    rows, width = tokens.shape
    share = width // 8
    vmem = pl.BlockSpec(memory_space=pltpu.VMEM)
    copies = 2 + SLICES + 13
    anywhere = pl.BlockSpec(memory_space=pl.ANY)
    pack = (
        jax.ShapeDtypeStruct((share, width), F32)
        if columns
        else jax.ShapeDtypeStruct(head_full.shape, BF16)
    )
    scratch = [
        pltpu.VMEM((2, rows, width), BF16),
        pltpu.VMEM((2, rows, width), BF16),
        pltpu.VMEM((rows, width), BF16),
        pltpu.VMEM((rows, width), BF16),
        pltpu.SemaphoreType.DMA((copies,)),
        pltpu.SemaphoreType.DMA((copies,)),
    ]
    if columns:
        scratch += [
            pltpu.VMEM((8, share, width), BF16),
            pltpu.VMEM((4, share, width), BF16),
            pltpu.VMEM((3, share, width), BF16),
            pltpu.VMEM((3, share, width), BF16),
            pltpu.VMEM((5, *small.shape), F32),
            pltpu.VMEM((5, *small.shape), F32),
        ]
    extra = [given] if columns else []
    out = pl.pallas_call(
        functools.partial(finish_kernel, columns),
        in_specs=[vmem] * 8 + [anywhere] * len(extra),
        out_specs=[vmem] * 3 + [anywhere] * len(extra),
        out_shape=[
            jax.ShapeDtypeStruct((rows, width), F32),
            pack,
            jax.ShapeDtypeStruct(small.shape, F32),
        ]
        + [jax.ShapeDtypeStruct(a.shape, a.dtype) for a in extra],
        scratch_shapes=scratch,
        compiler_params=pltpu.CompilerParams(
            collective_id=4, has_side_effects=True, vmem_limit_bytes=56 << 20
        ),
        cost_estimate=pl.CostEstimate(
            flops=32 * rows * width * PAD, bytes_accessed=64 * rows * width, transcendentals=0
        ),
    )(grads, ones, head_full, grad_out, small, grad_hidden, tokens, gain[None], *extra)
    return out if columns else [*out, swap(given, "dp", 1)]


def route_kernel(routes_ref, rows_ref, cols_ref, info_ref):
    tokens = routes_ref.shape[2]
    expert = lax.broadcasted_iota(jnp.int32, (NF, tokens), 0)
    step = 256
    down = lax.broadcasted_iota(jnp.int32, (step, step), 0)
    across = lax.broadcasted_iota(jnp.int32, (step, step), 1)
    before = jnp.where(down < across, 1.0, 0.0).astype(BF16)
    for a in range(2):
        hot = (expert == routes_ref[a, 0:1, :]) | (expert == routes_ref[a, 1:2, :])
        ones = jnp.where(hot, 1.0, 0.0)
        ranks, so_far = [], jnp.zeros((NF, 1), F32)
        for b in range(tokens // step):
            part = ones[:, b * step : (b + 1) * step]
            ranks.append(dot_nn(part.astype(BF16), before) + so_far)
            so_far = so_far + jnp.sum(part, axis=1, keepdims=True)
        rank = jnp.concatenate(ranks, axis=1)
        slots = jnp.where(hot, rank, -1.0)
        rows_ref[a] = slots.astype(jnp.int32)
        spread = jnp.concatenate([slots, jnp.zeros((128 - NF, tokens), F32)], axis=0)
        cols_ref[a] = spread.T.astype(jnp.int32)
        lane = lax.broadcasted_iota(jnp.int32, (NF, 128), 1)
        info = jnp.where(lane == 0, so_far, 0.0)
        for c in range(2):
            first = jnp.sum(jnp.where(rank + ones <= c * TILE, 1.0, 0.0), axis=1, keepdims=True)
            after = jnp.sum(jnp.where(rank < (c + 1) * TILE, 1.0, 0.0), axis=1, keepdims=True)
            info = jnp.where(lane == 1 + 2 * c, first, jnp.where(lane == 2 + 2 * c, after, info))
        info_ref[a] = info.astype(jnp.int32)


def route(routes):
    tokens = routes.shape[2]
    return pl.pallas_call(
        route_kernel,
        out_shape=[
            jax.ShapeDtypeStruct((2, NF, tokens), jnp.int32),
            jax.ShapeDtypeStruct((2, tokens, 128), jnp.int32),
            jax.ShapeDtypeStruct((2, NF, 128), jnp.int32),
        ],
        cost_estimate=pl.CostEstimate(flops=10**7, bytes_accessed=10**6, transcendentals=0),
    )(routes)


def experts_kernel(
    whole_weights, n_before, base_ref, info_ref, slot_rows_ref, slot_cols_ref, weights_ref, *refs
):
    (rows_in, grads_in), before, refs = refs[:2], refs[2 : 2 + n_before], refs[2 + n_before :]
    sums_out, grad_ins_out, out_ref, rows, grads, sums, grad_ins = refs[:7]
    weight, row_acc, grad_acc, slot_col, inputs, grad_outs, acts, gates, ups, in_sems, out_sems = refs[7:]
    step = pl.program_id(0)
    expert = base_ref[0] + step
    tokens, width = grads.shape[1:]
    wide = rows.shape[2]
    arrivals = [
        [pltpu.make_async_copy(rows_in.at[a], rows.at[a], in_sems.at[a, 0]),
         pltpu.make_async_copy(grads_in.at[a], grads.at[a], in_sems.at[a, 1])]
        + [pltpu.make_async_copy(source.at[a], target.at[a], in_sems.at[a, 2 + k])
           for k, (source, target) in enumerate(zip(before, (sums, grad_ins)))]
        for a in range(2)
    ]
    leaving = [
        [pltpu.make_async_copy(source.at[a], target.at[a], out_sems.at[a, k])
         for k, (source, target) in enumerate(((sums, sums_out), (grad_ins, grad_ins_out)))]
        for a in range(2)
    ]

    @pl.when(step == 0)
    def _():
        for copy in arrivals[0] + arrivals[1]:
            copy.start()
        if not n_before:
            sums[...] = jnp.zeros_like(sums)
            grad_ins[...] = jnp.zeros_like(grad_ins)

    if whole_weights:
        weight[...] = weights_ref[0]
    else:
        depth, _, _, _, share, _ = weights_ref.shape
        for z in range(depth):
            for y in range(2):
                weight[:, pl.ds((2 * z + y) * share, share), :] = weights_ref[z, y, 0]

    def tree(a):
        def dispatch(c, start, count):
            down = c * TILE + lax.broadcasted_iota(jnp.int32, (TILE, 1), 0)
            at = pl.ds(start, count)
            picked = slot_rows_ref[a, pl.ds(expert, 1), at] == down
            picked = jnp.where(picked, 1.0, 0.0).astype(BF16)
            row_acc[...] = dot_nn(picked, rows[a, at, :])
            grad_acc[...] = dot_nn(picked, grads[a, at, :])

        slot_col[...] = pltpu.roll(slot_cols_ref[a], 128 - expert, 1)

        def combine(c, start, count, back):
            across = c * TILE + lax.broadcasted_iota(jnp.int32, (1, TILE), 1)
            size = 256
            for b in range(count // size):
                at = pl.ds(pl.multiple_of(start + b * size, 128), size)
                here = jnp.where(slot_col[at, 0:1] == across, 1.0, 0.0).astype(BF16)
                part = dot_nn(here, back)
                sums[a, at, :] = (sums[a, at, :].astype(F32) + part[:, :width]).astype(BF16)
                grad_ins[a, at, :] = (
                    grad_ins[a, at, :].astype(F32) + part[:, width:]
                ).astype(BF16)

        def tile(c, carry):
            k = 8 * a + expert
            first, after = info_ref[k, 1 + 2 * c], info_ref[k, 2 + 2 * c]
            start = pl.multiple_of(jnp.minimum(first // 128 * 128, tokens - WINDOW), 128)
            narrow = after <= start + WINDOW

            @pl.when(narrow)
            def _():
                dispatch(c, start, WINDOW)

            @pl.when(jnp.logical_not(narrow))
            def _():
                dispatch(c, 0, tokens)

            at = pl.ds(pl.multiple_of((2 * a + c) * TILE, TILE), TILE)
            inputs[at, :] = row_acc[:, :width].astype(BF16)
            lane = lax.broadcasted_iota(jnp.int32, (TILE, wide - width), 1)
            gate = jnp.sum(
                jnp.where(lane == expert, row_acc[:, width:], 0.0), axis=1, keepdims=True
            )
            grad_out = (gate * grad_acc[...]).astype(BF16)
            grad_outs[at, :] = grad_out
            gate_part = dot_nn(inputs[at, :], weight[0])
            up_part = dot_nn(inputs[at, :], weight[1])
            sigmoid = 1.0 / (1.0 + jnp.exp(-gate_part))
            swish = gate_part * sigmoid
            act = (swish * up_part).astype(BF16)
            acts[at, :] = act
            expert_out = dot_nt(act, weight[2])
            along = jnp.sum(expert_out * grad_acc[...], axis=1, keepdims=True)
            grad_act = dot_nn(grad_out, weight[2])
            grad_gate = (
                grad_act * up_part * sigmoid * (1.0 + gate_part * (1.0 - sigmoid))
            ).astype(BF16)
            grad_up = (grad_act * swish).astype(BF16)
            gates[at, :] = grad_gate
            ups[at, :] = grad_up
            grad_in = dot_nt(grad_gate, weight[0]) + dot_nt(grad_up, weight[1])
            back = jnp.concatenate(
                [
                    (gate * expert_out).astype(BF16),
                    grad_in.astype(BF16),
                    jnp.where(lane == expert, along, 0.0).astype(BF16),
                ],
                axis=1,
            )

            @pl.when(narrow)
            def _():
                combine(c, start, WINDOW, back)

            @pl.when(jnp.logical_not(narrow))
            def _():
                combine(c, 0, tokens, back)

            return carry

        tiles = (info_ref[8 * a + expert, 0] + TILE - 1) // TILE

        def empty(c, carry):
            at = pl.ds(pl.multiple_of((2 * a + c) * TILE, TILE), TILE)
            for ref in (inputs, grad_outs, acts, gates, ups):
                ref[at, :] = jnp.zeros((TILE, ref.shape[1]), BF16)
            return carry

        lax.fori_loop(0, tiles, tile, 0)
        lax.fori_loop(tiles, 2, empty, 0)

    def one_tree(a, carry):
        for k in range(2):

            @pl.when(jnp.logical_and(step == 0, a == k))
            def _(k=k):
                for copy in arrivals[k]:
                    copy.wait()

        tree(a)
        for k in range(2):

            @pl.when(jnp.logical_and(step == pl.num_programs(0) - 1, a == k))
            def _(k=k):
                for copy in leaving[k]:
                    copy.start()

        return carry

    lax.fori_loop(0, 2, one_tree, 0)

    for k, (left, right) in enumerate(((inputs, gates), (inputs, ups), (grad_outs, acts))):
        size = 256
        for b in range(width // size):
            at = slice(b * size, (b + 1) * size)
            if whole_weights:
                out_ref[0, k, at, :] = dot_tn(left[:, at], right[...]).astype(BF16)
            else:
                weight[k, at, :] = dot_tn(left[:, at], right[...]).astype(BF16)
    if not whole_weights:
        for z in range(depth):
            for y in range(2):
                out_ref[z, y, 0] = weight[:, pl.ds((2 * z + y) * share, share), :]

    @pl.when(step == pl.num_programs(0) - 1)
    def _():
        for copy in leaving[0] + leaving[1]:
            copy.wait()


def experts(base, weights, info, rows, grads, slot_rows, slot_cols, before):
    _, tokens, width = grads.shape
    wide = rows.shape[2]
    whole_weights = weights.ndim == 4
    kinds, share, hidden = weights.shape[-3:]
    group = weights.shape[0] if whole_weights else weights.shape[2]
    depth = width if whole_weights else 2 * weights.shape[0] * share
    whole = lambda a: pl.BlockSpec(a.shape, lambda e, *_: (0,) * a.ndim, pipeline_mode=pl.Buffered(1))
    anywhere = pl.BlockSpec(memory_space=pl.ANY)
    if whole_weights:
        weight_spec = pl.BlockSpec((1, kinds, share, hidden), lambda e, *_: (e, 0, 0, 0))
    else:
        weight_spec = pl.BlockSpec(
            (weights.shape[0], 2, 1, kinds, share, hidden), lambda e, *_: (0, 0, e, 0, 0, 0)
        )
    sums = jax.ShapeDtypeStruct((2, tokens, width), BF16)
    grad_ins = jax.ShapeDtypeStruct((2, tokens, wide), BF16)
    return pl.pallas_call(
        functools.partial(experts_kernel, whole_weights, len(before)),
        grid_spec=pltpu.PrefetchScalarGridSpec(
            num_scalar_prefetch=2,
            grid=(group,),
            in_specs=[whole(slot_rows), whole(slot_cols), weight_spec]
            + [anywhere] * (2 + len(before)),
            out_specs=[anywhere, anywhere, weight_spec],
            scratch_shapes=[
                pltpu.VMEM((2, tokens, wide), BF16),
                pltpu.VMEM((2, tokens, width), BF16),
                pltpu.VMEM((2, tokens, width), BF16),
                pltpu.VMEM((2, tokens, wide), BF16),
                pltpu.VMEM((kinds, depth, hidden), BF16),
                pltpu.VMEM((TILE, wide), F32),
                pltpu.VMEM((TILE, width), F32),
                pltpu.VMEM((tokens, 128), jnp.int32),
                pltpu.VMEM((4 * TILE, width), BF16),
                pltpu.VMEM((4 * TILE, width), BF16),
                pltpu.VMEM((4 * TILE, hidden), BF16),
                pltpu.VMEM((4 * TILE, hidden), BF16),
                pltpu.VMEM((4 * TILE, hidden), BF16),
                pltpu.SemaphoreType.DMA((2, 4)),
                pltpu.SemaphoreType.DMA((2, 2)),
            ],
        ),
        out_shape=[sums, grad_ins, jax.ShapeDtypeStruct(weights.shape, BF16)],
        compiler_params=pltpu.CompilerParams(vmem_limit_bytes=60 << 20),
        cost_estimate=pl.CostEstimate(
            flops=group * tokens * width * (9 * hidden + 4 * tokens),
            bytes_accessed=16 * tokens * width,
            transcendentals=0,
        ),
    )(base, info, slot_rows, slot_cols, weights, rows, grads, *before)


def per_device(
    tokens_in,
    carried_logits,
    cotangent,
    segment_ids,
    parent_ids,
    routes,
    attention_gain,
    head_weight,
    output_weight,
    expert_gain,
    router_weight,
    carry_weight,
    constant_gate,
    constant_vector,
    expert_first,
    expert_second,
):
    row_count, width = tokens_in.shape
    tree_len = segment_ids.shape[0]
    head_width = head_weight.shape[2]
    heads = head_width // HEAD
    share = head_weight.shape[1]
    parity = lax.axis_index("dp") % 2
    index = lax.axis_index("tensor")
    own_experts = NF // 2
    group = own_experts // GROUPS
    layered = share % 16 == 0

    columns = lax.axis_size("dp") == 8

    def gather_experts(shards):
        gathered = gather_column(shards)
        if layered:
            return gathered
        return gathered.transpose(2, 3, 0, 1, 4, 5).reshape(group, 3, width, -1)

    sections = jnp.concatenate([head_weight, output_weight.T[None]], axis=0).astype(BF16)
    spread = lambda a, to: jnp.pad(a, ((0, 0), (0, to - a.shape[1])))
    if columns:
        pack = jnp.concatenate(
            [sections[k, :, :128] for k in range(4)] + [sections[k, :, 128:] for k in range(4)], axis=1
        )
    else:
        pack = jnp.concatenate([spread(sections[k], PAD) for k in range(4)], axis=1)
        pack = gather_column(pack)
        pack = jnp.moveaxis(by_parity(pack, swap(pack, "dp", 1)), 0, 1).reshape(width, 4 * PAD)
    expert_pack = jnp.concatenate(
        [expert_first.astype(BF16), expert_second.astype(BF16).transpose(0, 2, 1)[:, None]], axis=1
    )
    kept = lax.dynamic_slice_in_dim(expert_pack, parity * own_experts, own_experts, 0)
    given = lax.dynamic_slice_in_dim(expert_pack, (1 - parity) * own_experts, own_experts, 0)
    cut = lambda a, g: a[g * group : (g + 1) * group]
    shards = by_parity(cut(kept, 0), swap(cut(given, 0), "dp", 1))

    routes_both = jnp.stack([routes.T, swap(routes.T, "dp", 1)])
    slot_rows, slot_cols, info = route(routes_both)
    info = info.reshape(2 * NF, -1)[:, :8]
    angles = rotary_angles(segment_ids, parent_ids)
    rowinfo = jnp.pad(jnp.stack([segment_ids, parent_ids]), ((0, 6), (0, 0)))
    colinfo = rowinfo.T
    local_routes = lax.dynamic_slice_in_dim(routes, index * row_count, row_count, 0)
    picked = jnp.sum(
        (local_routes[:, :, None] == jnp.arange(128, dtype=jnp.int32)).astype(F32), axis=1
    )
    carried_part = spread(jnp.dot(carried_logits, carry_weight, precision=HIGHEST), 128)
    mix_weight = spread(jnp.concatenate([spread(router_weight, MIX), constant_gate], axis=1), 128)
    vectors = jnp.pad(constant_vector, ((0, 6), (0, 0)))
    (
        pack, shards, slot_rows, slot_cols, info, rowinfo, colinfo, picked, carried_part, mix_weight,
        vectors,
    ) = together(
        pack, shards, slot_rows, slot_cols, info, rowinfo, colinfo, picked, carried_part, mix_weight,
        vectors,
    )
    expert_weights = [gather_experts(shards)]

    queries, keys, values, keys_t, values_t, gathered_one, head_full, received = project(
        columns, tokens_in, attention_gain, angles, pack, given[group:]
    )
    for g in range(1, GROUPS):
        shards = by_parity(cut(kept, g), cut(received, g - 1))
        queries, shards = together(queries, shards)
        expert_weights.append(gather_experts(shards))
    attended, totals, hidden, aux, expert_rows, grad_rows = branch(
        heads, queries, keys, values_t, rowinfo, colinfo, cotangent, head_full, tokens_in, expert_gain,
        carried_part, mix_weight, picked,
    )

    parts, own_grads = [], []
    for g in range(GROUPS):
        base = (parity * own_experts + g * group).astype(jnp.int32).reshape(1)
        *parts, weight_grads = experts(
            base, expert_weights[g], info, expert_rows, grad_rows, slot_rows, slot_cols, parts
        )
        if not layered:
            weight_grads = weight_grads.reshape(group, 3, -1, 2, share, weight_grads.shape[-1])
            weight_grads = weight_grads.transpose(2, 3, 0, 1, 4, 5)
        own_grads.append(scatter_column(weight_grads))
    sums, grad_ins = parts

    grad_hidden, grad_logits, grad_output_t, small, grad_projected, output = branch_back(
        heads, hidden, aux, cotangent, expert_gain, mix_weight, vectors, spread(carried_logits, 128),
        attended, head_full, queries, keys, values, keys_t, rowinfo, colinfo, totals, angles, sums,
        grad_ins,
    )
    grad_carried = lax.dot_general(
        grad_logits[:, :NE], carry_weight, (((1,), (1,)), ((), ())), precision=HIGHEST
    )
    mine = lambda a: lax.dynamic_index_in_dim(a, parity, 0, keepdims=False)
    theirs = lambda a: lax.dynamic_index_in_dim(a, 1 - parity, 0, keepdims=False)
    grad_projected, own_grads[0] = together(grad_projected, own_grads[0])
    grad_tokens, own_pack, small, received = finish(
        columns, grad_projected, gathered_one, head_full, grad_output_t, small, grad_hidden, tokens_in,
        attention_gain, theirs(own_grads[0]),
    )
    if columns:
        own_sections = [
            jnp.concatenate(
                [own_pack[:, 128 * k : 128 * (k + 1)], own_pack[:, 512 + 64 * k : 576 + 64 * k]], axis=1
            )
            for k in range(4)
        ]
    else:
        blocks = own_pack.reshape(-1, 2, share, 4 * PAD)
        kept = lax.dynamic_index_in_dim(blocks, parity, 1, keepdims=False)
        given = lax.dynamic_index_in_dim(blocks, 1 - parity, 1, keepdims=False)
        paired = kept.astype(F32) + swap(given, "dp", 1).astype(F32)
        own_pack = scatter_column(paired.astype(BF16)).astype(F32)
        own_sections = [own_pack[:, k * PAD : k * PAD + head_width] for k in range(4)]
        small = lax.psum(small, ("dp", "tensor"))
    kept = jnp.concatenate([mine(a) for a in own_grads], axis=0)
    received = jnp.concatenate([received] + [swap(theirs(a), "dp", 1) for a in own_grads[1:]], axis=0)
    own_grads = by_parity(kept, received).reshape(NF, 3, share, -1).astype(F32)
    grad_first = own_grads[:, :2]
    grad_second = own_grads[:, 2].transpose(0, 2, 1)
    return (
        output,
        grad_tokens,
        grad_carried,
        small[19, :width],
        jnp.stack(own_sections[:3]),
        own_sections[3].T,
        small[16, :width],
        small[:NE, :width].T,
        small[:NE, width : width + NE],
        small[MIX : MIX + 4, :width].T,
        small[17:19, :width],
        grad_first,
        grad_second,
    )


def solution(mesh):
    in_specs = (
        P(("dp", "tensor"), None),
        P(("dp", "tensor"), None),
        P(("dp", "tensor"), None),
        P("dp"),
        P("dp"),
        P("dp", None),
        P(),
        P(None, "dp", "tensor"),
        P("tensor", "dp"),
        P(),
        P(),
        P(),
        P(),
        P(),
        P(None, None, "dp", "tensor"),
        P(None, "tensor", "dp"),
    )
    out_specs = (
        P(("dp", "tensor"), None),
        P(("dp", "tensor"), None),
        P(("dp", "tensor"), None),
        P(),
        P(None, "dp", "tensor"),
        P("tensor", "dp"),
        P(),
        P(),
        P(),
        P(),
        P(),
        P(None, None, "dp", "tensor"),
        P(None, "tensor", "dp"),
    )
    return jax.shard_map(
        per_device, mesh=mesh, in_specs=in_specs, out_specs=out_specs, check_vma=False
    )
```

```python
import functools

import jax
import jax.numpy as jnp
from jax import lax
from jax.experimental import pallas as pl
from jax.experimental.pallas import tpu as pltpu
from jax.sharding import PartitionSpec as P

HEAD = 64
NF = 8
NSEG = 13
NE = 12
PAD = 256
BLOCK = 512
SLICES = 4
MIX = 12
WINDOW = 1280
TILE = 256
GROUPS = 2

epsilon = 1e-06
HIGHEST = lax.Precision.HIGHEST
F32 = jnp.float32
BF16 = jnp.bfloat16
MESH = pl.DeviceIdType.MESH


def dot_nn(a, b):
    return lax.dot_general(a, b, (((1,), (0,)), ((), ())), preferred_element_type=F32)


def dot_nt(a, b):
    return lax.dot_general(a, b, (((1,), (1,)), ((), ())), preferred_element_type=F32)


def dot_tn(a, b):
    return lax.dot_general(a, b, (((0,), (0,)), ((), ())), preferred_element_type=F32)


def normed(values, gain_vector):
    return (
        values
        * lax.rsqrt(jnp.mean(values * values, axis=-1, keepdims=True) + epsilon)
        * gain_vector
    )


def tree_positions(segment, parent):
    token_count = segment.shape[0]
    labels = jnp.arange(NSEG, dtype=jnp.int32)
    own_hot = (segment[:, None] == labels[None, :]).astype(jnp.int32)
    parent_hot = (parent[:, None] == labels[None, :]).astype(jnp.int32)
    lengths = jnp.sum(own_hot, axis=0)
    starts = jnp.cumsum(lengths) - lengths
    own_start = jnp.sum(own_hot * starts[None, :], axis=1)
    parent_length = jnp.sum(parent_hot * lengths[None, :], axis=1)
    position_index = jnp.arange(token_count, dtype=jnp.int32)
    return (
        position_index
        - own_start
        + jnp.where(segment > 0, lengths[0], 0)
        + jnp.where(parent > 0, parent_length, 0)
    )


def rotary_angles(segment, parent):
    angle_rate = 10000.0 ** (-2.0 * jnp.arange(HEAD // 2, dtype=F32) / HEAD)
    angles = tree_positions(segment, parent).astype(F32)[:, None] * angle_rate[None, :]
    return jnp.concatenate([jnp.cos(angles), jnp.sin(angles)], axis=1)


def swap(values, axis, bits):
    size = lax.axis_size(axis)
    return lax.ppermute(values, axis, [(i, i ^ bits) for i in range(size)])


def together(*values):
    return lax.optimization_barrier(values)


def column_groups():
    size = lax.axis_size("dp")
    return [list(range(first, size, 2)) for first in range(2)]


def gather_column(own):
    return lax.all_gather(own, "dp", axis=0, tiled=False, axis_index_groups=column_groups())


def scatter_column(parts):
    return lax.psum_scatter(
        parts, "dp", scatter_dimension=0, tiled=False, axis_index_groups=column_groups()
    )


def by_parity(mine, other):
    even = lax.axis_index("dp") % 2 == 0
    return jnp.stack([jnp.where(even, mine, other), jnp.where(even, other, mine)])


def swap_halves(values):
    lane = lax.broadcasted_iota(jnp.int32, values.shape, 1)
    half = HEAD // 2
    return jnp.where(
        lane % HEAD < half, pltpu.roll(values, PAD - half, 1), pltpu.roll(values, half, 1)
    )


def rotation(angles):
    half = HEAD // 2
    source = lax.broadcasted_iota(jnp.int32, (2 * half, PAD), 0)
    lane = lax.broadcasted_iota(jnp.int32, (2 * half, PAD), 1)
    to_cos = (source == lane % half).astype(F32)
    to_sin = jnp.where(
        source == half + lane % half, jnp.where(lane % HEAD < half, -1.0, 1.0), 0.0
    )
    return [
        lax.dot_general(
            angles, where, (((1,), (0,)), ((), ())), precision=HIGHEST, preferred_element_type=F32
        )
        for where in (to_cos, to_sin)
    ]


def project_kernel(columns, tok_ref, gain_ref, angle_ref, pack_ref, *refs):
    if columns:
        given_ref, refs = refs[0], refs[1:]
    q_ref, k_ref, v_ref, kt_ref, vt_ref, one_ref = refs[:6]
    if columns:
        head_ref, received_ref, gathered, shards, send_sems, recv_sems = refs[6:]
    else:
        head_ref, (gathered, send_sems, recv_sems) = pack_ref, refs[6:]
    near, far, across, *column = enter(columns)
    copies = Copies(send_sems, recv_sems)
    dp, tensor = lax.axis_index("dp"), lax.axis_index("tensor")
    rows, width = tok_ref.shape
    share = pack_ref.shape[0]
    heads, last = [], []
    if columns:
        heads = [copies.start(pack_ref, shards.at[dp], device) for device in column]
        last.append(copies.start(pack_ref, shards.at[dp], across))
        shards[dp] = pack_ref[...]
    size = rows // SLICES
    slices = [pl.ds(c * size, size) for c in range(SLICES)]
    far_moves, near_moves = [], []
    for at in slices:
        values = tok_ref[at, :].astype(F32)
        scale = lax.rsqrt(jnp.mean(values * values, axis=1, keepdims=True) + epsilon)
        gathered[0, at, :] = (values * scale * gain_ref[...]).astype(BF16)
        far_moves.append(copies.start(gathered.at[0, at], gathered.at[2, at], far))
        near_moves.append(copies.start(gathered.at[0, at], gathered.at[1, at], near))
    corner_moves = []
    for c, at in enumerate(slices):
        far_moves[c].wait_recv()
        corner_moves.append(copies.start(gathered.at[2, at], gathered.at[3, at], near))
        if c < len(heads):
            heads[c].wait_recv()
            origin = lax.rem(dp + 8 - 2 * (c + 1), 8)
            last.append(copies.start(shards.at[origin], shards.at[origin], across))
    for move in last:
        move.wait_recv()
    beside = [copies.start(given_ref, received_ref, across)] if columns else []
    for move in near_moves + corner_moves:
        move.wait_recv()
    if columns:
        for d in range(8):
            at = pl.ds(d * share, share)
            piece = shards[d]
            for section in range(4):
                head_ref[at, section * PAD : section * PAD + 128] = piece[
                    :, section * 128 : (section + 1) * 128
                ]
                start = 512 + 128 * (section // 2)
                rest = piece[:, start : start + 128].astype(F32)
                if section % 2:
                    rest = pltpu.roll(rest, 64, 1)
                lane = lax.broadcasted_iota(jnp.int32, rest.shape, 1)
                head_ref[at, section * PAD + 128 : (section + 1) * PAD] = jnp.where(
                    lane < 64, rest, 0.0
                ).astype(BF16)
    for bits in range(4):
        start = pl.multiple_of(other(tensor, bits) * rows, rows)
        at = pl.ds(start, rows)
        values = gathered[bits]
        one_ref[at, :] = values
        cosine, sine = rotation(angle_ref[at, :])
        part = dot_nn(values, head_ref[:, :PAD])
        q_ref[at, :] = ((part * cosine + swap_halves(part) * sine) * HEAD**-0.5).astype(BF16)
        part = dot_nn(values, head_ref[:, PAD : 2 * PAD])
        part = part * cosine + swap_halves(part) * sine
        k_ref[at, :] = part.astype(BF16)
        kt_ref[:, at] = part.T.astype(BF16)
        part = dot_nn(values, head_ref[:, 2 * PAD : 3 * PAD])
        v_ref[at, :] = part.astype(BF16)
        vt_ref[:, at] = part.T.astype(BF16)
    for move in beside:
        move.wait_recv()
    copies.finish()


def project(columns, tokens, gain, angles, pack, given):
    rows, width = tokens.shape
    total = angles.shape[0]
    vmem = pl.BlockSpec(memory_space=pltpu.VMEM)
    copies = 3 * SLICES + 8
    anywhere = pl.BlockSpec(memory_space=pl.ANY)
    wide = jax.ShapeDtypeStruct((total, PAD), BF16)
    tall = jax.ShapeDtypeStruct((PAD, total), BF16)
    shapes = [wide, wide, wide, tall, tall, jax.ShapeDtypeStruct((total, width), BF16)]
    scratch = [pltpu.VMEM((4, rows, width), BF16)]
    arguments, extra = [tokens, gain[None], angles, pack], []
    if columns:
        shapes.append(jax.ShapeDtypeStruct((width, 4 * PAD), BF16))
        scratch.append(pltpu.VMEM((8, *pack.shape), BF16))
        arguments.append(given)
        extra.append(jax.ShapeDtypeStruct(given.shape, BF16))
    out = pl.pallas_call(
        functools.partial(project_kernel, columns),
        in_specs=[vmem] * 4 + [anywhere] * len(extra),
        out_specs=[vmem] * len(shapes) + [anywhere] * len(extra),
        out_shape=shapes + extra,
        scratch_shapes=scratch
        + [pltpu.SemaphoreType.DMA((copies,)), pltpu.SemaphoreType.DMA((copies,))],
        compiler_params=pltpu.CompilerParams(
            collective_id=3, has_side_effects=True, vmem_limit_bytes=56 << 20
        ),
        cost_estimate=pl.CostEstimate(
            flops=6 * total * width * PAD, bytes_accessed=16 * total * width, transcendentals=0
        ),
    )(*arguments)
    return out if columns else [*out, pack, swap(given, "dp", 1)]


def head_mask(values, head):
    lane = lax.broadcasted_iota(jnp.int32, values.shape, 1)
    return jnp.where(lane // HEAD == head, values, jnp.zeros_like(values))


def seen(i, j, seg_row, par_row, seg_col):
    key_at = j * BLOCK + lax.broadcasted_iota(jnp.int32, (BLOCK, 1), 0)
    query_at = i * BLOCK + lax.broadcasted_iota(jnp.int32, (1, BLOCK), 1)
    related = (seg_col == seg_row) | (seg_col == par_row) | (seg_col == 0)
    return related & (key_at <= query_at)


def attend_block(heads, i, q_ref, k_ref, vt_ref, rowinfo_ref, colinfo_ref, o_ref, total_ref):
    here = pl.ds(pl.multiple_of(i * BLOCK, BLOCK), BLOCK)
    queries = q_ref[here, :]
    by_head = [head_mask(queries, h) for h in range(heads)]
    seg_row, par_row = rowinfo_ref[0:1, here], rowinfo_ref[1:2, here]

    def step(j, carry):
        at = pl.ds(pl.multiple_of(j * BLOCK, BLOCK), BLOCK)
        keys = k_ref[at, :]
        visible = seen(i, j, seg_row, par_row, colinfo_ref[at, 0:1])
        out = []
        for h in range(heads):
            top, total, mixed = carry[h]
            scores = jnp.where(visible, dot_nt(keys, by_head[h]), -1e30)
            new_top = jnp.maximum(top, jnp.max(scores, axis=0, keepdims=True))
            shrink = jnp.exp(top - new_top)
            probs = jnp.exp(scores - new_top)
            total = total * shrink + jnp.sum(probs, axis=0, keepdims=True)
            mixed = mixed * shrink + dot_nn(
                vt_ref[h * HEAD : (h + 1) * HEAD, at], probs.astype(BF16)
            )
            out.append((new_top, total, mixed))
        return tuple(out)

    start = tuple(
        (
            jnp.full((1, BLOCK), -1e30, F32),
            jnp.zeros((1, BLOCK), F32),
            jnp.zeros((HEAD, BLOCK), F32),
        )
        for _ in range(heads)
    )
    done = lax.fori_loop(0, i + 1, step, start)
    mixed = [m / t for _, t, m in done] + [jnp.zeros((PAD - heads * HEAD, BLOCK), F32)]
    o_ref[here, :] = jnp.concatenate(mixed, axis=0).T.astype(BF16)
    total_ref[:, here] = jnp.concatenate(
        [m + jnp.log(t) for m, t, _ in done] + [jnp.zeros((8 - heads, BLOCK), F32)], axis=0
    )


def other(place, bits):
    if bits & 2:
        place = place + 2 - 4 * lax.rem(lax.div(place, 2), 2)
    if bits & 1:
        place = place + 1 - 2 * lax.rem(place, 2)
    return place


def enter(columns=False):
    dp, tensor = lax.axis_index("dp"), lax.axis_index("tensor")
    others = [(dp, other(tensor, 1)), (dp, other(tensor, 2)), (other(dp, 1), tensor)]
    if columns:
        others += [(lax.rem(dp + 2 * j, 8), tensor) for j in (1, 2, 3)]
    barrier = pltpu.get_barrier_semaphore()
    for device in others:
        pl.semaphore_signal(barrier, inc=1, device_id=device, device_id_type=MESH)
    pl.semaphore_wait(barrier, len(others))
    return others


class Copies:
    def __init__(self, send_sems, recv_sems):
        self.send_sems, self.recv_sems, self.made = send_sems, recv_sems, []

    def start(self, source, target, device):
        k = len(self.made)
        copy = pltpu.make_async_remote_copy(
            src_ref=source,
            dst_ref=target,
            send_sem=self.send_sems.at[k],
            recv_sem=self.recv_sems.at[k],
            device_id=device,
            device_id_type=MESH,
        )
        copy.start()
        self.made.append(copy)
        return copy

    def finish(self):
        for copy in self.made:
            copy.wait_send()


def quarter(ref, bits, rows):
    place = other(lax.axis_index("tensor"), bits)
    return ref.at[pl.ds(pl.multiple_of(place * rows, rows), rows)]


def sum_of_quarters(part, copies, near, far, near_send, near_recv, far_send, far_recv):
    rows = far_send.shape[0]
    near_send[0] = part(3).astype(BF16)
    first = copies.start(near_send.at[0], near_recv.at[0], near)
    near_send[1] = part(1).astype(BF16)
    second = copies.start(near_send.at[1], near_recv.at[1], near)
    mine = part(2)
    first.wait_recv()
    far_send[...] = (mine + near_recv[0].astype(F32)).astype(BF16)
    moves = []
    for c in range(SLICES):
        at = pl.ds(c * rows // SLICES, rows // SLICES)
        moves.append(copies.start(far_send.at[at], far_recv.at[at], far))
    mine = part(0)
    second.wait_recv()
    return mine + near_recv[1].astype(F32), moves


class Spread:
    def __init__(self, copies, devices, target, rows):
        self.copies, (self.near, self.far, self.across) = copies, devices
        self.rows, self.own, self.beside = rows, quarter(target.at[0], 0, rows), quarter(target.at[1], 0, rows)
        self.over, self.corner = quarter(target.at[0], 2, rows), quarter(target.at[1], 2, rows)
        self.from_far, self.from_across, self.from_corner, self.ends = {}, {}, {}, []

    def send(self, source, at, c):
        copies = self.copies
        self.from_far[c] = copies.start(source.at[at], self.own.at[at], self.far)
        self.from_across[c] = copies.start(source.at[at], self.beside.at[at], self.across)
        self.ends.append(copies.start(source.at[at], self.own.at[at], self.near))

    def pass_on(self, c, at):
        copies = self.copies
        self.from_far[c].wait_recv()
        if c >= SLICES // 2:
            self.from_corner[c] = copies.start(self.over.at[at], self.corner.at[at], self.across)
        self.ends.append(copies.start(self.over.at[at], self.over.at[at], self.near))
        self.from_across[c].wait_recv()
        if c < SLICES // 2:
            self.from_corner[c] = copies.start(self.beside.at[at], self.beside.at[at], self.far)
        self.ends.append(copies.start(self.beside.at[at], self.beside.at[at], self.near))

    def pass_corner(self, c, at):
        self.from_corner[c].wait_recv()
        self.ends.append(self.copies.start(self.corner.at[at], self.corner.at[at], self.near))

    def finish(self):
        for copy in self.ends:
            copy.wait_recv()


def branch_kernel(
    heads, q_ref, k_ref, vt_ref, rowinfo_ref, colinfo_ref, cot_ref,
    out_ref, tok_ref, gain_ref, carried_ref, mix_ref, picked_ref,
    att_ref, total_ref, hidden_ref, aux_ref, rows_ref, cots_ref,
    near_send, near_recv, far_send, far_recv, own, send_sems, recv_sems, local_sems,
):
    devices = enter()
    near, far, _ = devices
    copies = Copies(send_sems, recv_sems)
    rows, width = tok_ref.shape
    weights = out_ref[:, 3 * PAD :]
    size = rows // SLICES
    slices = [pl.ds(c * size, size) for c in range(SLICES)]
    locals_ = [pltpu.make_async_copy(cot_ref, quarter(cots_ref.at[0], 0, rows), local_sems.at[0])]
    locals_[0].start()
    cots = Spread(copies, devices, cots_ref, rows)
    for c, at in enumerate(slices):
        cots.send(cot_ref, at, c)

    def part(bits):
        if bits == 0:
            for c, at in enumerate(slices):
                cots.pass_on(c, at)
        place = other(lax.axis_index("tensor"), bits)
        for block in range(rows // BLOCK):
            attend_block(
                heads, place * (rows // BLOCK) + block,
                q_ref, k_ref, vt_ref, rowinfo_ref, colinfo_ref, att_ref, total_ref,
            )
        return dot_nt(quarter(att_ref, bits, rows)[...], weights)

    mine, moves = sum_of_quarters(
        part, copies, near, far, near_send, near_recv, far_send, far_recv
    )
    hidden_ref[...] = tok_ref[...].astype(F32) + mine
    spread = Spread(copies, devices, rows_ref, rows)
    for c, at in enumerate(slices):
        moves[c].wait_recv()
        hidden = hidden_ref[at, :] + far_recv[at, :].astype(F32)
        hidden_ref[at, :] = hidden
        scale = lax.rsqrt(jnp.mean(hidden * hidden, axis=1, keepdims=True) + epsilon)
        normed_two = hidden * scale * gain_ref[...]
        logits = carried_ref[at, :] + lax.dot_general(
            normed_two,
            mix_ref[...],
            (((1,), (0,)), ((), ())),
            precision=HIGHEST,
            preferred_element_type=F32,
        )
        picked = picked_ref[at, :] > 0
        top = jnp.max(jnp.where(picked, logits, -1e30), axis=1, keepdims=True)
        weight = jnp.where(picked, jnp.exp(jnp.where(picked, logits - top, 0.0)), 0.0)
        gate = weight / jnp.sum(weight, axis=1, keepdims=True)
        lane = lax.broadcasted_iota(jnp.int32, logits.shape, 1)
        turned = jnp.where(
            lane % 2 == 0, pltpu.roll(logits, 127, 1), pltpu.roll(logits, 1, 1)
        )
        top = jnp.maximum(logits, turned)
        mixture = jnp.exp(logits - top) / (jnp.exp(logits - top) + jnp.exp(turned - top))
        aux_ref[at, :] = jnp.where(lane < MIX, gate, jnp.where(lane < MIX + 4, mixture, 0.0))
        own[at, :width] = normed_two.astype(BF16)
        own[at, width:] = jnp.where(lane < NF, gate, 0.0).astype(BF16)
        spread.send(own, at, c)
        local = pltpu.make_async_copy(
            own.at[at], quarter(rows_ref.at[0], 0, rows).at[at], local_sems.at[1 + c]
        )
        local.start()
        locals_.append(local)
    for c, at in enumerate(slices):
        cots.pass_corner(c, at)
    for c, at in enumerate(slices):
        spread.pass_on(c, at)
    for c, at in enumerate(slices):
        spread.pass_corner(c, at)
    cots.finish()
    spread.finish()
    for local in locals_:
        local.wait()
    copies.finish()


def branch(
    heads, queries, keys, values_t, rowinfo, colinfo, cotangent, head_full, tokens, gain, carried, mix,
    picked,
):
    rows, width = tokens.shape
    total = queries.shape[0]
    vmem, anywhere = pl.BlockSpec(memory_space=pltpu.VMEM), pl.BlockSpec(memory_space=pl.ANY)
    copies = 2 + 15 * SLICES
    return pl.pallas_call(
        functools.partial(branch_kernel, heads),
        in_specs=[vmem] * 12,
        out_specs=[vmem] * 4 + [anywhere] * 2,
        out_shape=[
            jax.ShapeDtypeStruct((total, PAD), BF16),
            jax.ShapeDtypeStruct((8, total), F32),
            jax.ShapeDtypeStruct((rows, width), F32),
            jax.ShapeDtypeStruct((rows, 128), F32),
            jax.ShapeDtypeStruct((2, total, width + 128), BF16),
            jax.ShapeDtypeStruct((2, total, width), BF16),
        ],
        scratch_shapes=[
            pltpu.VMEM((2, rows, width), BF16),
            pltpu.VMEM((2, rows, width), BF16),
            pltpu.VMEM((rows, width), BF16),
            pltpu.VMEM((rows, width), BF16),
            pltpu.VMEM((rows, width + 128), BF16),
            pltpu.SemaphoreType.DMA((copies,)),
            pltpu.SemaphoreType.DMA((copies,)),
            pltpu.SemaphoreType.DMA((1 + SLICES,)),
        ],
        compiler_params=pltpu.CompilerParams(
            collective_id=1, has_side_effects=True, vmem_limit_bytes=48 << 20
        ),
        cost_estimate=pl.CostEstimate(
            flops=64 * rows * width * PAD, bytes_accessed=64 * rows * width, transcendentals=0
        ),
    )(
        queries, keys, values_t, rowinfo, colinfo, cotangent, head_full, tokens, gain[None],
        carried, mix, picked,
    )


class PairSum:
    def __init__(self, copies, devices, source, refs, local_sems):
        self.copies, (self.near, self.far, self.across) = copies, devices
        self.source, self.local_sems = source, local_sems
        self.kept, self.near_recv, self.corner_send, self.corner_recv = refs[:4]
        self.far_send, self.far_recv, self.across_send, self.across_recv = refs[4:]
        self.rows = self.far_send.shape[0]
        half = self.rows // 2
        self.halves = [pl.ds(0, half), pl.ds(half, half)]
        self.arrivals, self.locals_, self.from_far, self.from_across = {}, {}, {}, {}

    @staticmethod
    def shapes(rows, wide):
        one, two = (rows, wide), (2, rows // 2, wide)
        return [
            pltpu.VMEM(shape, BF16)
            for shape in ((4, *one), (4, *one), one, two, one, one, one, one)
        ]

    def start(self):
        for b in (3, 1, 2, 0):
            tree, bits = self.source.at[b // 2], 2 * (b % 2)
            self.arrivals[b] = self.copies.start(
                quarter(tree, bits + 1, self.rows), self.near_recv.at[b], self.near
            )
            self.locals_[b] = pltpu.make_async_copy(
                quarter(tree, bits, self.rows), self.kept.at[b], self.local_sems.at[b]
            )
            self.locals_[b].start()

    def joined(self, b, at):
        return self.kept[b, at, :].astype(F32) + self.near_recv[b, at, :].astype(F32)

    def arrived(self, b):
        self.arrivals[b].wait_recv()
        self.locals_[b].wait()

    def first_round(self):
        low, high = self.halves
        self.arrived(3)
        self.corner_send[...] = self.joined(3, pl.ds(0, self.rows)).astype(BF16)
        start = self.copies.start
        self.corner_far = start(self.corner_send.at[low], self.corner_recv.at[0], self.far)
        self.corner_across = start(self.corner_send.at[high], self.corner_recv.at[1], self.across)
        self.arrived(1)
        self.far_send[low, :] = self.joined(1, low).astype(BF16)
        self.from_far[0] = start(self.far_send.at[low], self.far_recv.at[low], self.far)
        self.arrived(2)
        self.across_send[high, :] = self.joined(2, high).astype(BF16)
        self.from_across[1] = start(self.across_send.at[high], self.across_recv.at[high], self.across)

    def second_round(self):
        low, high = self.halves
        start = self.copies.start
        self.corner_far.wait_recv()
        self.across_send[low, :] = (
            self.joined(2, low) + self.corner_recv[0].astype(F32)
        ).astype(BF16)
        self.from_across[0] = start(self.across_send.at[low], self.across_recv.at[low], self.across)
        self.corner_across.wait_recv()
        self.far_send[high, :] = (
            self.joined(1, high) + self.corner_recv[1].astype(F32)
        ).astype(BF16)
        self.from_far[1] = start(self.far_send.at[high], self.far_recv.at[high], self.far)
        self.arrived(0)

    def total(self, h):
        self.from_far[h].wait_recv()
        self.from_across[h].wait_recv()
        at = self.halves[h]
        return (
            self.joined(0, at)
            + self.far_recv[at, :].astype(F32)
            + self.across_recv[at, :].astype(F32)
        )


def attend_back_block(
    heads, i, q_ref, g_ref, o_ref, k_ref, v_ref, kt_ref, rowinfo_ref, colinfo_ref, total_ref, angle_ref,
    grad_ref, key_sum, value_sum, query_sum,
):
    here = pl.ds(pl.multiple_of(i * BLOCK, BLOCK), BLOCK)
    query_sum[...] = jnp.zeros_like(query_sum)
    queries, grads = q_ref[here, :], g_ref[here, :]
    q_heads = [head_mask(queries, h) for h in range(heads)]
    g_heads = [head_mask(grads, h) for h in range(heads)]
    seg_row, par_row = rowinfo_ref[0:1, here], rowinfo_ref[1:2, here]
    product = grads.astype(F32) * o_ref[here, :].astype(F32)
    lane = lax.broadcasted_iota(jnp.int32, (8, PAD), 1)
    which = lax.broadcasted_iota(jnp.int32, (8, PAD), 0)
    delta = lax.dot_general(
        (lane // HEAD == which).astype(F32),
        product,
        (((1,), (1,)), ((), ())),
        precision=HIGHEST,
        preferred_element_type=F32,
    )
    totals = total_ref[:, here]

    def step(j, carry):
        at = pl.ds(pl.multiple_of(j * BLOCK, BLOCK), BLOCK)
        keys, values = k_ref[at, :], v_ref[at, :]
        visible = seen(i, j, seg_row, par_row, colinfo_ref[at, 0:1])
        key_part, value_part = key_sum[at, :], value_sum[at, :]
        for h in range(heads):
            scores = jnp.where(visible, dot_nt(keys, q_heads[h]), -1e30)
            probs = jnp.exp(scores - totals[h : h + 1, :])
            value_part = value_part + dot_nn(probs.astype(BF16), g_heads[h])
            grad_probs = dot_nt(values, g_heads[h])
            grad_scores = (probs * (grad_probs - delta[h : h + 1, :])).astype(BF16)
            key_part = key_part + dot_nn(grad_scores, q_heads[h])
            lanes = slice(h * HEAD, (h + 1) * HEAD)
            query_sum[lanes, :] += dot_nn(kt_ref[lanes, at], grad_scores)
        key_sum[at, :] = key_part
        value_sum[at, :] = value_part
        return carry

    lax.fori_loop(0, i + 1, step, 0)
    grad_ref[here, :PAD] = turned_back(query_sum[...].T * HEAD**-0.5, angle_ref[here, :])


def turned_back(values, angles):
    cosine, sine = rotation(angles)
    return (values * cosine - swap_halves(values) * sine).astype(BF16)


def branch_back_kernel(
    heads, hidden_ref, aux_ref, cot_ref, gain_ref, mix_ref, vector_ref, carried_ref, att_ref, out_ref,
    q_ref, k_ref, v_ref, kt_ref, rowinfo_ref, colinfo_ref, total_ref, angle_ref, sums_ref, grad_ins_ref,
    grad_hidden_ref, grad_logits_ref, grad_out_ref, small_ref, grad_ref, result_ref,
    normed_two, base, gathered, grad_att, key_sum, value_sum, query_sum,
    send_sems, recv_sems, local_sems, *buffers,
):
    devices = enter()
    near, far, _ = devices
    copies = Copies(send_sems, recv_sems)
    rows, width = hidden_ref.shape
    half = rows // 2
    halves = [pl.ds(0, half), pl.ds(half, half)]
    incoming = PairSum(copies, devices, grad_ins_ref, buffers[:8], local_sems.at[0])
    results = PairSum(copies, devices, sums_ref, buffers[8:], local_sems.at[1])
    incoming.start()
    key_sum[...] = jnp.zeros_like(key_sum)
    value_sum[...] = jnp.zeros_like(value_sum)

    gain = gain_ref[...]
    lane = lax.broadcasted_iota(jnp.int32, (half, 128), 1)

    def column(values, at):
        return jnp.sum(jnp.where(lane == at, values, 0.0), axis=1, keepdims=True)

    known = []
    for at in halves:
        hidden, aux, grads = hidden_ref[at, :], aux_ref[at, :], cot_ref[at, :].astype(F32)
        scale = lax.rsqrt(jnp.mean(hidden * hidden, axis=1, keepdims=True) + epsilon)
        normed = hidden * scale * gain
        normed_two[at, :] = normed
        gates = [column(aux, NF + 1 + k) for k in range(3)]
        mixes = [column(aux, MIX + k) for k in range(4)]
        along = jnp.sum(grads * normed, axis=1, keepdims=True)
        vectors = [
            jnp.sum(grads * vector_ref[c : c + 1, :], axis=1, keepdims=True) for c in range(2)
        ]
        kept = gates[0] + gates[1] * mixes[0] + gates[2] * mixes[2]
        base[at, :] = grads * kept
        sums = []
        for c in range(2):
            sums.append(
                jnp.sum(grads * (gates[1 + c] * mixes[2 * c + 1]), axis=0, keepdims=True)
            )
        by_gate = jnp.where(lane == NF + 1, along, 0.0)
        by_mix = jnp.zeros((half, 128), F32)
        for c in range(2):
            first, second = mixes[2 * c], mixes[2 * c + 1]
            by_gate = by_gate + jnp.where(
                lane == NF + 2 + c, first * along + second * vectors[c], 0.0
            )
            d_first, d_second = gates[1 + c] * along, gates[1 + c] * vectors[c]
            inner = first * d_first + second * d_second
            by_mix = by_mix + jnp.where(lane == MIX + 2 * c, first * (d_first - inner), 0.0)
            by_mix = by_mix + jnp.where(lane == MIX + 2 * c + 1, second * (d_second - inner), 0.0)
        known.append((scale, by_gate, by_mix, sums))
    incoming.first_round()
    incoming.second_round()

    gain_sum = jnp.zeros((1, width), F32)
    far_moves, near_moves = [], []
    for h, at in enumerate(halves):
        scale, by_gate, by_mix, _ = known[h]
        arriving = incoming.total(h)
        by_gate = by_gate + jnp.where(lane < NF, arriving[:, width:], 0.0)
        gates = jnp.where(lane < MIX, aux_ref[at, :], 0.0)
        grad_logits = by_mix + gates * (
            by_gate - jnp.sum(gates * by_gate, axis=1, keepdims=True)
        )
        grad_logits_ref[at, :] = grad_logits
        grad_normed = arriving[:, :width] + base[at, :] + lax.dot_general(
            grad_logits,
            mix_ref[...],
            (((1,), (1,)), ((), ())),
            precision=HIGHEST,
            preferred_element_type=F32,
        )
        hidden = hidden_ref[at, :]
        gain_sum = gain_sum + jnp.sum(hidden * scale * grad_normed, axis=0, keepdims=True)
        weighted = gain * grad_normed
        inner = jnp.mean(hidden * weighted, axis=1, keepdims=True)
        grad_hidden = (
            cot_ref[at, :].astype(F32) + scale * weighted - hidden * (scale * scale * scale * inner)
        )
        grad_hidden_ref[at, :] = grad_hidden
        gathered[0, at, :] = grad_hidden.astype(BF16)
        far_moves.append(copies.start(gathered.at[0, at], gathered.at[2, at], far))
        near_moves.append(copies.start(gathered.at[0, at], gathered.at[1, at], near))
    results.start()

    def over_tokens(a, b):
        return lax.dot_general(
            a, b, (((0,), (0,)), ((), ())), precision=HIGHEST, preferred_element_type=F32
        )

    small_ref[...] = jnp.zeros_like(small_ref)
    small_ref[:16, :width] = over_tokens(grad_logits_ref[...], normed_two[...])[:16]
    small_ref[16:, :width] = jnp.concatenate(
        [gain_sum] + [known[0][3][c] + known[1][3][c] for c in range(2)]
        + [jnp.zeros((5, width), F32)],
        axis=0,
    )
    small_ref[:16, width:] = over_tokens(carried_ref[...], grad_logits_ref[...])[:16]

    def attention_back(bits):
        values = gathered[bits]
        quarter(grad_att, bits, rows)[...] = dot_nn(values, out_ref[:, 3 * PAD :]).astype(BF16)
        product = dot_tn(values, quarter(att_ref, bits, rows)[...])
        grad_out_ref[...] = grad_out_ref[...] + product if bits else product
        place = other(lax.axis_index("tensor"), bits)
        for block in range(rows // BLOCK):
            attend_back_block(
                heads, place * (rows // BLOCK) + block, q_ref, grad_att, att_ref, k_ref, v_ref, kt_ref,
                rowinfo_ref, colinfo_ref, total_ref, angle_ref, grad_ref, key_sum, value_sum, query_sum,
            )

    attention_back(0)
    results.first_round()
    for move in near_moves:
        move.wait_recv()
    last = []
    for h, at in enumerate(halves):
        far_moves[h].wait_recv()
        last.append(copies.start(gathered.at[2, at], gathered.at[3, at], near))
    attention_back(1)
    results.second_round()
    attention_back(2)
    for move in last:
        move.wait_recv()
    attention_back(3)
    for h, at in enumerate(halves):
        aux = aux_ref[at, :]
        gates = [column(aux, NF + 1 + k) for k in range(3)]
        mixes = [column(aux, MIX + k) for k in range(4)]
        kept = gates[0] + gates[1] * mixes[0] + gates[2] * mixes[2]
        result = hidden_ref[at, :] + kept * normed_two[at, :] + results.total(h)
        for c in range(2):
            result = result + (gates[1 + c] * mixes[2 * c + 1]) * vector_ref[c : c + 1, :]
        result_ref[at, :] = result.astype(BF16)

    def finish_keys(j, carry):
        at = pl.ds(pl.multiple_of(j * BLOCK, BLOCK), BLOCK)
        grad_ref[at, PAD : 2 * PAD] = turned_back(key_sum[at, :], angle_ref[at, :])
        grad_ref[at, 2 * PAD :] = value_sum[at, :].astype(BF16)
        return carry

    lax.fori_loop(0, grad_ref.shape[0] // BLOCK, finish_keys, 0)
    copies.finish()


def branch_back(
    heads, hidden, aux, cotangent, gain, mix, vectors, carried, attended, head_full, queries, keys, values,
    keys_t, rowinfo, colinfo, totals, angles, sums, grad_ins,
):
    rows, width = hidden.shape
    total = queries.shape[0]
    vmem, anywhere = pl.BlockSpec(memory_space=pltpu.VMEM), pl.BlockSpec(memory_space=pl.ANY)
    copies = 2 * 10 + 6
    return pl.pallas_call(
        functools.partial(branch_back_kernel, heads),
        in_specs=[vmem] * 17 + [anywhere] * 2,
        out_specs=[vmem] * 6,
        out_shape=[
            jax.ShapeDtypeStruct((rows, width), F32),
            jax.ShapeDtypeStruct((rows, 128), F32),
            jax.ShapeDtypeStruct((width, PAD), F32),
            jax.ShapeDtypeStruct((24, width + 128), F32),
            jax.ShapeDtypeStruct((total, 3 * PAD), BF16),
            jax.ShapeDtypeStruct((rows, width), BF16),
        ],
        scratch_shapes=[
            pltpu.VMEM((rows, width), F32),
            pltpu.VMEM((rows, width), F32),
            pltpu.VMEM((4, rows, width), BF16),
            pltpu.VMEM((total, PAD), BF16),
            pltpu.VMEM((total, PAD), F32),
            pltpu.VMEM((total, PAD), F32),
            pltpu.VMEM((PAD, BLOCK), F32),
            pltpu.SemaphoreType.DMA((copies,)),
            pltpu.SemaphoreType.DMA((copies,)),
            pltpu.SemaphoreType.DMA((2, 4)),
        ]
        + PairSum.shapes(rows, grad_ins.shape[2])
        + PairSum.shapes(rows, width),
        compiler_params=pltpu.CompilerParams(
            collective_id=2, has_side_effects=True, vmem_limit_bytes=61 << 20
        ),
        cost_estimate=pl.CostEstimate(
            flops=256 * rows * width * PAD, bytes_accessed=64 * rows * width, transcendentals=0
        ),
    )(
        hidden, aux, cotangent, gain[None], mix, vectors, carried, attended, head_full,
        queries, keys, values, keys_t, rowinfo, colinfo, totals, angles, sums, grad_ins,
    )


def finish_kernel(
    columns, grad_ref, one_ref, head_ref, grad_out_ref, small_ref, grad_hidden_ref, tok_ref, gain_ref,
    *refs
):
    if columns:
        given_ref, received_ref, refs = refs[0], refs[4], refs[1:4] + refs[5:]
    grad_tok_ref, pack_ref, sum_ref, refs = refs[0], refs[1], refs[2], refs[3:]
    near_send, near_recv, far_send, far_recv, send_sems, recv_sems = refs[:6]
    near, far, across, *column = enter(columns)
    copies = Copies(send_sems, recv_sems)
    dp = lax.axis_index("dp")
    rows, width = tok_ref.shape
    share = width // 8

    def part(bits):
        return dot_nt(quarter(grad_ref, bits, rows)[...], head_ref[:, : 3 * PAD])

    mine, moves = sum_of_quarters(
        part, copies, near, far, near_send, near_recv, far_send, far_recv
    )
    grad_tok_ref[...] = mine

    packed = refs[6] if columns else pack_ref
    products = refs[-1]
    products[...] = dot_tn(one_ref[...], grad_ref[...])
    along = jnp.zeros((8, width), F32)
    rest = None
    for section in range(4):
        at = slice(section * PAD, (section + 1) * PAD)
        if section < 3:
            grad = products[:, at]
            along = along + lax.dot_general(
                jnp.ones((8, PAD), F32),
                grad * head_ref[:, at].astype(F32),
                (((1,), (1,)), ((), ())),
                precision=HIGHEST,
                preferred_element_type=F32,
            )
        else:
            grad = grad_out_ref[...]
        if not columns:
            packed[:, at] = grad.astype(BF16)
            continue
        low, high = grad[:, :128].astype(BF16), grad[:, 128:]
        if section % 2 == 0:
            rest = high
        else:
            lane = lax.broadcasted_iota(jnp.int32, high.shape, 1)
            rest = jnp.where(lane < 64, rest, pltpu.roll(high, 64, 1)).astype(BF16)
        for d in range(8):
            cut = slice(d * share, (d + 1) * share)
            packed[d, :, section * 128 : (section + 1) * 128] = low[cut]
            if section % 2:
                start = 512 + 128 * (section // 2)
                packed[d, :, start : start + 128] = rest[cut]
    small = small_ref[...]
    row = lax.broadcasted_iota(jnp.int32, (24, width), 0)
    small = jnp.concatenate(
        [
            jnp.where(row == 19, along[:1] / gain_ref[...], small[:, :width]),
            small[:, width:],
        ],
        axis=1,
    )
    if columns:
        _, pair_recv, column_send, column_recv, sums, sum_recv = refs[6:-1]
        pair_moves = []
        for j in range(4):
            there = lax.rem(other(dp, 1) + 2 * j, 8)
            pair_moves.append(copies.start(packed.at[there], pair_recv.at[j], across))
        sums[0] = small
        steps = [near, far, across, (other(dp, 2), lax.axis_index("tensor")), column[1]]
        sum_moves = [copies.start(sums.at[0], sum_recv.at[0], steps[0])]

        def add_up():
            k = len(sum_moves)
            sum_moves[-1].wait_recv()
            if k < 5:
                sums[k] = sums[k - 1] + sum_recv[k - 1]
                sum_moves.append(copies.start(sums.at[k], sum_recv.at[k], steps[k]))
            else:
                sum_ref[...] = sums[4] + sum_recv[4]

        add_up()
        add_up()
        column_moves = []
        for j in (1, 2, 3, 0):
            pair_moves[j].wait_recv()
            paired = packed[lax.rem(dp + 2 * j, 8)].astype(F32) + pair_recv[j].astype(F32)
            if j:
                column_send[j - 1] = paired.astype(BF16)
                column_moves.append(
                    copies.start(column_send.at[j - 1], column_recv.at[j - 1], column[j - 1])
                )
            else:
                pack_ref[...] = paired
        beside = copies.start(given_ref, received_ref, across)
        add_up()
    else:
        sum_ref[...] = small

    size = rows // SLICES
    for c in range(SLICES):
        at = pl.ds(c * size, size)
        moves[c].wait_recv()
        grad_normed = grad_tok_ref[at, :] + far_recv[at, :].astype(F32)
        values = tok_ref[at, :].astype(F32)
        scale = lax.rsqrt(jnp.mean(values * values, axis=1, keepdims=True) + epsilon)
        weighted = gain_ref[...] * grad_normed
        inner = jnp.mean(values * weighted, axis=1, keepdims=True)
        grad_tok_ref[at, :] = (
            grad_hidden_ref[at, :] + scale * weighted - values * (scale * scale * scale * inner)
        )
    if columns:
        add_up()
        for j in range(3):
            column_moves[j].wait_recv()
            pack_ref[...] = pack_ref[...] + column_recv[j].astype(F32)
        add_up()
        beside.wait_recv()
    copies.finish()


def finish(columns, grads, ones, head_full, grad_out, small, grad_hidden, tokens, gain, given):
    rows, width = tokens.shape
    share = width // 8
    vmem = pl.BlockSpec(memory_space=pltpu.VMEM)
    copies = 2 + SLICES + 13
    anywhere = pl.BlockSpec(memory_space=pl.ANY)
    pack = (
        jax.ShapeDtypeStruct((share, width), F32)
        if columns
        else jax.ShapeDtypeStruct(head_full.shape, BF16)
    )
    scratch = [
        pltpu.VMEM((2, rows, width), BF16),
        pltpu.VMEM((2, rows, width), BF16),
        pltpu.VMEM((rows, width), BF16),
        pltpu.VMEM((rows, width), BF16),
        pltpu.SemaphoreType.DMA((copies,)),
        pltpu.SemaphoreType.DMA((copies,)),
    ]
    if columns:
        scratch += [
            pltpu.VMEM((8, share, width), BF16),
            pltpu.VMEM((4, share, width), BF16),
            pltpu.VMEM((3, share, width), BF16),
            pltpu.VMEM((3, share, width), BF16),
            pltpu.VMEM((5, *small.shape), F32),
            pltpu.VMEM((5, *small.shape), F32),
        ]
    scratch.append(pltpu.VMEM((width, 3 * PAD), F32))
    extra = [given] if columns else []
    out = pl.pallas_call(
        functools.partial(finish_kernel, columns),
        in_specs=[vmem] * 8 + [anywhere] * len(extra),
        out_specs=[vmem] * 3 + [anywhere] * len(extra),
        out_shape=[
            jax.ShapeDtypeStruct((rows, width), F32),
            pack,
            jax.ShapeDtypeStruct(small.shape, F32),
        ]
        + [jax.ShapeDtypeStruct(a.shape, a.dtype) for a in extra],
        scratch_shapes=scratch,
        compiler_params=pltpu.CompilerParams(
            collective_id=4, has_side_effects=True, vmem_limit_bytes=56 << 20
        ),
        cost_estimate=pl.CostEstimate(
            flops=32 * rows * width * PAD, bytes_accessed=64 * rows * width, transcendentals=0
        ),
    )(grads, ones, head_full, grad_out, small, grad_hidden, tokens, gain[None], *extra)
    return out if columns else [*out, swap(given, "dp", 1)]


def route_kernel(routes_ref, rows_ref, cols_ref, info_ref):
    tokens = routes_ref.shape[2]
    expert = lax.broadcasted_iota(jnp.int32, (NF, tokens), 0)
    step = 256
    down = lax.broadcasted_iota(jnp.int32, (step, step), 0)
    across = lax.broadcasted_iota(jnp.int32, (step, step), 1)
    before = jnp.where(down < across, 1.0, 0.0).astype(BF16)
    for a in range(2):
        hot = (expert == routes_ref[a, 0:1, :]) | (expert == routes_ref[a, 1:2, :])
        ones = jnp.where(hot, 1.0, 0.0)
        ranks, so_far = [], jnp.zeros((NF, 1), F32)
        for b in range(tokens // step):
            part = ones[:, b * step : (b + 1) * step]
            ranks.append(dot_nn(part.astype(BF16), before) + so_far)
            so_far = so_far + jnp.sum(part, axis=1, keepdims=True)
        rank = jnp.concatenate(ranks, axis=1)
        slots = jnp.where(hot, rank, -1.0)
        rows_ref[a] = slots.astype(jnp.int32)
        spread = jnp.concatenate([slots, jnp.zeros((128 - NF, tokens), F32)], axis=0)
        cols_ref[a] = spread.T.astype(jnp.int32)
        lane = lax.broadcasted_iota(jnp.int32, (NF, 128), 1)
        info = jnp.where(lane == 0, so_far, 0.0)
        for c in range(2):
            first = jnp.sum(jnp.where(rank + ones <= c * TILE, 1.0, 0.0), axis=1, keepdims=True)
            after = jnp.sum(jnp.where(rank < (c + 1) * TILE, 1.0, 0.0), axis=1, keepdims=True)
            info = jnp.where(lane == 1 + 2 * c, first, jnp.where(lane == 2 + 2 * c, after, info))
        info_ref[a] = info.astype(jnp.int32)


def route(routes):
    tokens = routes.shape[2]
    return pl.pallas_call(
        route_kernel,
        out_shape=[
            jax.ShapeDtypeStruct((2, NF, tokens), jnp.int32),
            jax.ShapeDtypeStruct((2, tokens, 128), jnp.int32),
            jax.ShapeDtypeStruct((2, NF, 128), jnp.int32),
        ],
        cost_estimate=pl.CostEstimate(flops=10**7, bytes_accessed=10**6, transcendentals=0),
    )(routes)


def experts_kernel(
    whole_weights, n_before, base_ref, info_ref, slot_rows_ref, slot_cols_ref, weights_ref, *refs
):
    (rows_in, grads_in), before, refs = refs[:2], refs[2 : 2 + n_before], refs[2 + n_before :]
    sums_out, grad_ins_out, out_ref, rows, grads, sums, grad_ins = refs[:7]
    weight, row_acc, grad_acc, slot_col, inputs, grad_outs, acts, gates, ups, in_sems, out_sems = refs[7:]
    step = pl.program_id(0)
    expert = base_ref[0] + step
    tokens, width = grads.shape[1:]
    wide = rows.shape[2]
    arrivals = [
        [pltpu.make_async_copy(rows_in.at[a], rows.at[a], in_sems.at[a, 0]),
         pltpu.make_async_copy(grads_in.at[a], grads.at[a], in_sems.at[a, 1])]
        + [pltpu.make_async_copy(source.at[a], target.at[a], in_sems.at[a, 2 + k])
           for k, (source, target) in enumerate(zip(before, (sums, grad_ins)))]
        for a in range(2)
    ]
    leaving = [
        [pltpu.make_async_copy(source.at[a], target.at[a], out_sems.at[a, k])
         for k, (source, target) in enumerate(((sums, sums_out), (grad_ins, grad_ins_out)))]
        for a in range(2)
    ]

    @pl.when(step == 0)
    def _():
        for copy in arrivals[0] + arrivals[1]:
            copy.start()
        if not n_before:
            sums[...] = jnp.zeros_like(sums)
            grad_ins[...] = jnp.zeros_like(grad_ins)

    if whole_weights:
        weight[...] = weights_ref[0]
    else:
        depth, _, _, _, share, _ = weights_ref.shape
        for z in range(depth):
            for y in range(2):
                weight[:, pl.ds((2 * z + y) * share, share), :] = weights_ref[z, y, 0]

    def tree(a):
        def dispatch(c, start, count):
            down = c * TILE + lax.broadcasted_iota(jnp.int32, (TILE, 1), 0)
            at = pl.ds(start, count)
            picked = slot_rows_ref[a, pl.ds(expert, 1), at] == down
            picked = jnp.where(picked, 1.0, 0.0).astype(BF16)
            row_acc[...] = dot_nn(picked, rows[a, at, :])
            grad_acc[...] = dot_nn(picked, grads[a, at, :])

        slot_col[...] = pltpu.roll(slot_cols_ref[a], 128 - expert, 1)

        def combine(c, start, count, back):
            across = c * TILE + lax.broadcasted_iota(jnp.int32, (1, TILE), 1)
            size = 256
            for b in range(count // size):
                at = pl.ds(pl.multiple_of(start + b * size, 128), size)
                here = jnp.where(slot_col[at, 0:1] == across, 1.0, 0.0).astype(BF16)
                part = dot_nn(here, back)
                sums[a, at, :] = (sums[a, at, :].astype(F32) + part[:, :width]).astype(BF16)
                grad_ins[a, at, :] = (
                    grad_ins[a, at, :].astype(F32) + part[:, width:]
                ).astype(BF16)

        def tile(c, carry):
            k = 8 * a + expert
            first, after = info_ref[k, 1 + 2 * c], info_ref[k, 2 + 2 * c]
            start = pl.multiple_of(jnp.minimum(first // 128 * 128, tokens - WINDOW), 128)
            narrow = after <= start + WINDOW

            @pl.when(narrow)
            def _():
                dispatch(c, start, WINDOW)

            @pl.when(jnp.logical_not(narrow))
            def _():
                dispatch(c, 0, tokens)

            at = pl.ds(pl.multiple_of((2 * a + c) * TILE, TILE), TILE)
            inputs[at, :] = row_acc[:, :width].astype(BF16)
            lane = lax.broadcasted_iota(jnp.int32, (TILE, wide - width), 1)
            gate = jnp.sum(
                jnp.where(lane == expert, row_acc[:, width:], 0.0), axis=1, keepdims=True
            )
            grad_out = (gate * grad_acc[...]).astype(BF16)
            grad_outs[at, :] = grad_out
            gate_part = dot_nn(inputs[at, :], weight[0])
            up_part = dot_nn(inputs[at, :], weight[1])
            sigmoid = 1.0 / (1.0 + jnp.exp(-gate_part))
            swish = gate_part * sigmoid
            act = (swish * up_part).astype(BF16)
            acts[at, :] = act
            expert_out = dot_nt(act, weight[2])
            along = jnp.sum(expert_out * grad_acc[...], axis=1, keepdims=True)
            grad_act = dot_nn(grad_out, weight[2])
            grad_gate = (
                grad_act * up_part * sigmoid * (1.0 + gate_part * (1.0 - sigmoid))
            ).astype(BF16)
            grad_up = (grad_act * swish).astype(BF16)
            gates[at, :] = grad_gate
            ups[at, :] = grad_up
            grad_in = dot_nt(grad_gate, weight[0]) + dot_nt(grad_up, weight[1])
            back = jnp.concatenate(
                [
                    (gate * expert_out).astype(BF16),
                    grad_in.astype(BF16),
                    jnp.where(lane == expert, along, 0.0).astype(BF16),
                ],
                axis=1,
            )

            @pl.when(narrow)
            def _():
                combine(c, start, WINDOW, back)

            @pl.when(jnp.logical_not(narrow))
            def _():
                combine(c, 0, tokens, back)

            return carry

        tiles = (info_ref[8 * a + expert, 0] + TILE - 1) // TILE

        def empty(c, carry):
            at = pl.ds(pl.multiple_of((2 * a + c) * TILE, TILE), TILE)
            for ref in (inputs, grad_outs, acts, gates, ups):
                ref[at, :] = jnp.zeros((TILE, ref.shape[1]), BF16)
            return carry

        lax.fori_loop(0, tiles, tile, 0)
        lax.fori_loop(tiles, 2, empty, 0)

    def one_tree(a, carry):
        for k in range(2):

            @pl.when(jnp.logical_and(step == 0, a == k))
            def _(k=k):
                for copy in arrivals[k]:
                    copy.wait()

        tree(a)
        for k in range(2):

            @pl.when(jnp.logical_and(step == pl.num_programs(0) - 1, a == k))
            def _(k=k):
                for copy in leaving[k]:
                    copy.start()

        return carry

    lax.fori_loop(0, 2, one_tree, 0)

    for k, (left, right) in enumerate(((inputs, gates), (inputs, ups), (grad_outs, acts))):
        size = 256
        for b in range(width // size):
            at = slice(b * size, (b + 1) * size)
            if whole_weights:
                out_ref[0, k, at, :] = dot_tn(left[:, at], right[...]).astype(BF16)
            else:
                weight[k, at, :] = dot_tn(left[:, at], right[...]).astype(BF16)
    if not whole_weights:
        for z in range(depth):
            for y in range(2):
                out_ref[z, y, 0] = weight[:, pl.ds((2 * z + y) * share, share), :]

    @pl.when(step == pl.num_programs(0) - 1)
    def _():
        for copy in leaving[0] + leaving[1]:
            copy.wait()


def experts(base, weights, info, rows, grads, slot_rows, slot_cols, before):
    _, tokens, width = grads.shape
    wide = rows.shape[2]
    whole_weights = weights.ndim == 4
    kinds, share, hidden = weights.shape[-3:]
    group = weights.shape[0] if whole_weights else weights.shape[2]
    depth = width if whole_weights else 2 * weights.shape[0] * share
    whole = lambda a: pl.BlockSpec(a.shape, lambda e, *_: (0,) * a.ndim, pipeline_mode=pl.Buffered(1))
    anywhere = pl.BlockSpec(memory_space=pl.ANY)
    if whole_weights:
        weight_spec = pl.BlockSpec((1, kinds, share, hidden), lambda e, *_: (e, 0, 0, 0))
    else:
        weight_spec = pl.BlockSpec(
            (weights.shape[0], 2, 1, kinds, share, hidden), lambda e, *_: (0, 0, e, 0, 0, 0)
        )
    sums = jax.ShapeDtypeStruct((2, tokens, width), BF16)
    grad_ins = jax.ShapeDtypeStruct((2, tokens, wide), BF16)
    return pl.pallas_call(
        functools.partial(experts_kernel, whole_weights, len(before)),
        grid_spec=pltpu.PrefetchScalarGridSpec(
            num_scalar_prefetch=2,
            grid=(group,),
            in_specs=[whole(slot_rows), whole(slot_cols), weight_spec]
            + [anywhere] * (2 + len(before)),
            out_specs=[anywhere, anywhere, weight_spec],
            scratch_shapes=[
                pltpu.VMEM((2, tokens, wide), BF16),
                pltpu.VMEM((2, tokens, width), BF16),
                pltpu.VMEM((2, tokens, width), BF16),
                pltpu.VMEM((2, tokens, wide), BF16),
                pltpu.VMEM((kinds, depth, hidden), BF16),
                pltpu.VMEM((TILE, wide), F32),
                pltpu.VMEM((TILE, width), F32),
                pltpu.VMEM((tokens, 128), jnp.int32),
                pltpu.VMEM((4 * TILE, width), BF16),
                pltpu.VMEM((4 * TILE, width), BF16),
                pltpu.VMEM((4 * TILE, hidden), BF16),
                pltpu.VMEM((4 * TILE, hidden), BF16),
                pltpu.VMEM((4 * TILE, hidden), BF16),
                pltpu.SemaphoreType.DMA((2, 4)),
                pltpu.SemaphoreType.DMA((2, 2)),
            ],
        ),
        out_shape=[sums, grad_ins, jax.ShapeDtypeStruct(weights.shape, BF16)],
        compiler_params=pltpu.CompilerParams(vmem_limit_bytes=60 << 20),
        cost_estimate=pl.CostEstimate(
            flops=group * tokens * width * (9 * hidden + 4 * tokens),
            bytes_accessed=16 * tokens * width,
            transcendentals=0,
        ),
    )(base, info, slot_rows, slot_cols, weights, rows, grads, *before)


def per_device(
    tokens_in,
    carried_logits,
    cotangent,
    segment_ids,
    parent_ids,
    routes,
    attention_gain,
    head_weight,
    output_weight,
    expert_gain,
    router_weight,
    carry_weight,
    constant_gate,
    constant_vector,
    expert_first,
    expert_second,
):
    row_count, width = tokens_in.shape
    tree_len = segment_ids.shape[0]
    head_width = head_weight.shape[2]
    heads = head_width // HEAD
    share = head_weight.shape[1]
    parity = lax.axis_index("dp") % 2
    index = lax.axis_index("tensor")
    own_experts = NF // 2
    group = own_experts // GROUPS
    layered = share % 16 == 0

    columns = lax.axis_size("dp") == 8

    def gather_experts(shards):
        gathered = gather_column(shards)
        if layered:
            return gathered
        return gathered.transpose(2, 3, 0, 1, 4, 5).reshape(group, 3, width, -1)

    sections = jnp.concatenate([head_weight, output_weight.T[None]], axis=0).astype(BF16)
    spread = lambda a, to: jnp.pad(a, ((0, 0), (0, to - a.shape[1])))
    if columns:
        pack = jnp.concatenate(
            [sections[k, :, :128] for k in range(4)] + [sections[k, :, 128:] for k in range(4)], axis=1
        )
    else:
        pack = jnp.concatenate([spread(sections[k], PAD) for k in range(4)], axis=1)
        pack = gather_column(pack)
        pack = jnp.moveaxis(by_parity(pack, swap(pack, "dp", 1)), 0, 1).reshape(width, 4 * PAD)
    expert_pack = jnp.concatenate(
        [expert_first.astype(BF16), expert_second.astype(BF16).transpose(0, 2, 1)[:, None]], axis=1
    )
    kept = lax.dynamic_slice_in_dim(expert_pack, parity * own_experts, own_experts, 0)
    given = lax.dynamic_slice_in_dim(expert_pack, (1 - parity) * own_experts, own_experts, 0)
    cut = lambda a, g: a[g * group : (g + 1) * group]
    shards = by_parity(cut(kept, 0), swap(cut(given, 0), "dp", 1))

    angles, routes_there = together(
        rotary_angles(segment_ids, parent_ids), swap(routes.T, "dp", 1)
    )
    slot_rows, slot_cols, info = route(jnp.stack([routes.T, routes_there]))
    info = info.reshape(2 * NF, -1)[:, :8]
    rowinfo = jnp.pad(jnp.stack([segment_ids, parent_ids]), ((0, 6), (0, 0)))
    colinfo = rowinfo.T
    local_routes = lax.dynamic_slice_in_dim(routes, index * row_count, row_count, 0)
    picked = jnp.sum(
        (local_routes[:, :, None] == jnp.arange(128, dtype=jnp.int32)).astype(F32), axis=1
    )
    carried_part = spread(jnp.dot(carried_logits, carry_weight, precision=HIGHEST), 128)
    mix_weight = spread(jnp.concatenate([spread(router_weight, MIX), constant_gate], axis=1), 128)
    vectors = jnp.pad(constant_vector, ((0, 6), (0, 0)))
    (
        pack, shards, slot_rows, slot_cols, info, rowinfo, colinfo, picked, carried_part, mix_weight,
        vectors,
    ) = together(
        pack, shards, slot_rows, slot_cols, info, rowinfo, colinfo, picked, carried_part, mix_weight,
        vectors,
    )
    expert_weights = [gather_experts(shards)]

    queries, keys, values, keys_t, values_t, gathered_one, head_full, received = project(
        columns, tokens_in, attention_gain, angles, pack, given[group:]
    )
    for g in range(1, GROUPS):
        shards = by_parity(cut(kept, g), cut(received, g - 1))
        queries, shards = together(queries, shards)
        expert_weights.append(gather_experts(shards))
    attended, totals, hidden, aux, expert_rows, grad_rows = branch(
        heads, queries, keys, values_t, rowinfo, colinfo, cotangent, head_full, tokens_in, expert_gain,
        carried_part, mix_weight, picked,
    )

    parts, own_grads = [], []
    for g in range(GROUPS):
        base = (parity * own_experts + g * group).astype(jnp.int32).reshape(1)
        *parts, weight_grads = experts(
            base, expert_weights[g], info, expert_rows, grad_rows, slot_rows, slot_cols, parts
        )
        if not layered:
            weight_grads = weight_grads.reshape(group, 3, -1, 2, share, weight_grads.shape[-1])
            weight_grads = weight_grads.transpose(2, 3, 0, 1, 4, 5)
        own_grads.append(scatter_column(weight_grads))
    sums, grad_ins = parts

    grad_hidden, grad_logits, grad_output_t, small, grad_projected, output = branch_back(
        heads, hidden, aux, cotangent, expert_gain, mix_weight, vectors, spread(carried_logits, 128),
        attended, head_full, queries, keys, values, keys_t, rowinfo, colinfo, totals, angles, sums,
        grad_ins,
    )
    grad_carried = lax.dot_general(
        grad_logits[:, :NE], carry_weight, (((1,), (1,)), ((), ())), precision=HIGHEST
    )
    mine = lambda a: lax.dynamic_index_in_dim(a, parity, 0, keepdims=False)
    theirs = lambda a: lax.dynamic_index_in_dim(a, 1 - parity, 0, keepdims=False)
    grad_projected, own_grads[0] = together(grad_projected, own_grads[0])
    grad_tokens, own_pack, small, received = finish(
        columns, grad_projected, gathered_one, head_full, grad_output_t, small, grad_hidden, tokens_in,
        attention_gain, theirs(own_grads[0]),
    )
    if columns:
        own_sections = [
            jnp.concatenate(
                [own_pack[:, 128 * k : 128 * (k + 1)], own_pack[:, 512 + 64 * k : 576 + 64 * k]], axis=1
            )
            for k in range(4)
        ]
    else:
        blocks = own_pack.reshape(-1, 2, share, 4 * PAD)
        kept = lax.dynamic_index_in_dim(blocks, parity, 1, keepdims=False)
        given = lax.dynamic_index_in_dim(blocks, 1 - parity, 1, keepdims=False)
        paired = kept.astype(F32) + swap(given, "dp", 1).astype(F32)
        own_pack = scatter_column(paired.astype(BF16)).astype(F32)
        own_sections = [own_pack[:, k * PAD : k * PAD + head_width] for k in range(4)]
        small = lax.psum(small, ("dp", "tensor"))
    kept = jnp.concatenate([mine(a) for a in own_grads], axis=0)
    received = jnp.concatenate([received] + [swap(theirs(a), "dp", 1) for a in own_grads[1:]], axis=0)
    own_grads = by_parity(kept, received).reshape(NF, 3, share, -1).astype(F32)
    grad_first = own_grads[:, :2]
    grad_second = own_grads[:, 2].transpose(0, 2, 1)
    return (
        output,
        grad_tokens,
        grad_carried,
        small[19, :width],
        jnp.stack(own_sections[:3]),
        own_sections[3].T,
        small[16, :width],
        small[:NE, :width].T,
        small[:NE, width : width + NE],
        small[MIX : MIX + 4, :width].T,
        small[17:19, :width],
        grad_first,
        grad_second,
    )


def solution(mesh):
    in_specs = (
        P(("dp", "tensor"), None),
        P(("dp", "tensor"), None),
        P(("dp", "tensor"), None),
        P("dp"),
        P("dp"),
        P("dp", None),
        P(),
        P(None, "dp", "tensor"),
        P("tensor", "dp"),
        P(),
        P(),
        P(),
        P(),
        P(),
        P(None, None, "dp", "tensor"),
        P(None, "tensor", "dp"),
    )
    out_specs = (
        P(("dp", "tensor"), None),
        P(("dp", "tensor"), None),
        P(("dp", "tensor"), None),
        P(),
        P(None, "dp", "tensor"),
        P("tensor", "dp"),
        P(),
        P(),
        P(),
        P(),
        P(),
        P(None, None, "dp", "tensor"),
        P(None, "tensor", "dp"),
    )
    return jax.shard_map(
        per_device, mesh=mesh, in_specs=in_specs, out_specs=out_specs, check_vma=False
    )
```

```python
import functools

import jax
import jax.numpy as jnp
from jax import lax
from jax.experimental import pallas as pl
from jax.experimental.pallas import tpu as pltpu
from jax.sharding import PartitionSpec as P

HEAD = 64
NF = 8
NSEG = 13
NE = 12
PAD = 256
BLOCK = 512
SLICES = 4
MIX = 12
WINDOW = 1280
TILE = 256
GROUPS = 2

epsilon = 1e-06
HIGHEST = lax.Precision.HIGHEST
F32 = jnp.float32
BF16 = jnp.bfloat16
MESH = pl.DeviceIdType.MESH


def dot_nn(a, b):
    return lax.dot_general(a, b, (((1,), (0,)), ((), ())), preferred_element_type=F32)


def dot_nt(a, b):
    return lax.dot_general(a, b, (((1,), (1,)), ((), ())), preferred_element_type=F32)


def dot_tn(a, b):
    return lax.dot_general(a, b, (((0,), (0,)), ((), ())), preferred_element_type=F32)


def normed(values, gain_vector):
    return (
        values
        * lax.rsqrt(jnp.mean(values * values, axis=-1, keepdims=True) + epsilon)
        * gain_vector
    )


def tree_positions(segment, parent):
    token_count = segment.shape[0]
    labels = jnp.arange(NSEG, dtype=jnp.int32)
    own_hot = (segment[:, None] == labels[None, :]).astype(jnp.int32)
    parent_hot = (parent[:, None] == labels[None, :]).astype(jnp.int32)
    lengths = jnp.sum(own_hot, axis=0)
    starts = jnp.cumsum(lengths) - lengths
    own_start = jnp.sum(own_hot * starts[None, :], axis=1)
    parent_length = jnp.sum(parent_hot * lengths[None, :], axis=1)
    position_index = jnp.arange(token_count, dtype=jnp.int32)
    return (
        position_index
        - own_start
        + jnp.where(segment > 0, lengths[0], 0)
        + jnp.where(parent > 0, parent_length, 0)
    )


def rotary_angles(segment, parent):
    angle_rate = 10000.0 ** (-2.0 * jnp.arange(HEAD // 2, dtype=F32) / HEAD)
    angles = tree_positions(segment, parent).astype(F32)[:, None] * angle_rate[None, :]
    return jnp.concatenate([jnp.cos(angles), jnp.sin(angles)], axis=1)


def swap(values, axis, bits):
    size = lax.axis_size(axis)
    return lax.ppermute(values, axis, [(i, i ^ bits) for i in range(size)])


def together(*values):
    return lax.optimization_barrier(values)


def column_groups():
    size = lax.axis_size("dp")
    return [list(range(first, size, 2)) for first in range(2)]


def gather_column(own):
    return lax.all_gather(own, "dp", axis=0, tiled=False, axis_index_groups=column_groups())


def scatter_column(parts):
    return lax.psum_scatter(
        parts, "dp", scatter_dimension=0, tiled=False, axis_index_groups=column_groups()
    )


def by_parity(mine, other):
    even = lax.axis_index("dp") % 2 == 0
    return jnp.stack([jnp.where(even, mine, other), jnp.where(even, other, mine)])


def swap_halves(values):
    lane = lax.broadcasted_iota(jnp.int32, values.shape, 1)
    half = HEAD // 2
    return jnp.where(
        lane % HEAD < half, pltpu.roll(values, PAD - half, 1), pltpu.roll(values, half, 1)
    )


def rotation(angles):
    half = HEAD // 2
    source = lax.broadcasted_iota(jnp.int32, (2 * half, PAD), 0)
    lane = lax.broadcasted_iota(jnp.int32, (2 * half, PAD), 1)
    to_cos = (source == lane % half).astype(F32)
    to_sin = jnp.where(
        source == half + lane % half, jnp.where(lane % HEAD < half, -1.0, 1.0), 0.0
    )
    return [
        lax.dot_general(
            angles, where, (((1,), (0,)), ((), ())), precision=HIGHEST, preferred_element_type=F32
        )
        for where in (to_cos, to_sin)
    ]


def project_kernel(columns, tok_ref, gain_ref, angle_ref, pack_ref, *refs):
    if columns:
        given_ref, refs = refs[0], refs[1:]
    q_ref, k_ref, v_ref, kt_ref, vt_ref, one_ref = refs[:6]
    if columns:
        head_ref, received_ref, gathered, shards, send_sems, recv_sems = refs[6:]
    else:
        head_ref, (gathered, send_sems, recv_sems) = pack_ref, refs[6:]
    near, far, across, *column = enter(columns)
    copies = Copies(send_sems, recv_sems)
    dp, tensor = lax.axis_index("dp"), lax.axis_index("tensor")
    rows, width = tok_ref.shape
    share = pack_ref.shape[0]
    heads, last = [], []
    if columns:
        heads = [copies.start(pack_ref, shards.at[dp], device) for device in column]
        last.append(copies.start(pack_ref, shards.at[dp], across))
        shards[dp] = pack_ref[...]
    size = rows // SLICES
    slices = [pl.ds(c * size, size) for c in range(SLICES)]
    far_moves, near_moves = [], []
    for at in slices:
        values = tok_ref[at, :].astype(F32)
        scale = lax.rsqrt(jnp.mean(values * values, axis=1, keepdims=True) + epsilon)
        gathered[0, at, :] = (values * scale * gain_ref[...]).astype(BF16)
        far_moves.append(copies.start(gathered.at[0, at], gathered.at[2, at], far))
        near_moves.append(copies.start(gathered.at[0, at], gathered.at[1, at], near))
    corner_moves = []
    for c, at in enumerate(slices):
        far_moves[c].wait_recv()
        corner_moves.append(copies.start(gathered.at[2, at], gathered.at[3, at], near))
        if c < len(heads):
            heads[c].wait_recv()
            origin = lax.rem(dp + 8 - 2 * (c + 1), 8)
            last.append(copies.start(shards.at[origin], shards.at[origin], across))
    for move in last:
        move.wait_recv()
    beside = [copies.start(given_ref, received_ref, across)] if columns else []
    for move in near_moves + corner_moves:
        move.wait_recv()
    if columns:
        for d in range(8):
            at = pl.ds(d * share, share)
            piece = shards[d]
            for section in range(4):
                head_ref[at, section * PAD : section * PAD + 128] = piece[
                    :, section * 128 : (section + 1) * 128
                ]
                start = 512 + 128 * (section // 2)
                rest = piece[:, start : start + 128].astype(F32)
                if section % 2:
                    rest = pltpu.roll(rest, 64, 1)
                lane = lax.broadcasted_iota(jnp.int32, rest.shape, 1)
                head_ref[at, section * PAD + 128 : (section + 1) * PAD] = jnp.where(
                    lane < 64, rest, 0.0
                ).astype(BF16)
    for bits in range(4):
        start = pl.multiple_of(other(tensor, bits) * rows, rows)
        at = pl.ds(start, rows)
        values = gathered[bits]
        one_ref[at, :] = values
        cosine, sine = rotation(angle_ref[at, :])
        part = dot_nn(values, head_ref[:, :PAD])
        q_ref[at, :] = ((part * cosine + swap_halves(part) * sine) * HEAD**-0.5).astype(BF16)
        part = dot_nn(values, head_ref[:, PAD : 2 * PAD])
        part = part * cosine + swap_halves(part) * sine
        k_ref[at, :] = part.astype(BF16)
        kt_ref[:, at] = part.T.astype(BF16)
        part = dot_nn(values, head_ref[:, 2 * PAD : 3 * PAD])
        v_ref[at, :] = part.astype(BF16)
        vt_ref[:, at] = part.T.astype(BF16)
    for move in beside:
        move.wait_recv()
    copies.finish()


def project(columns, tokens, gain, angles, pack, given):
    rows, width = tokens.shape
    total = angles.shape[0]
    vmem = pl.BlockSpec(memory_space=pltpu.VMEM)
    copies = 3 * SLICES + 8
    anywhere = pl.BlockSpec(memory_space=pl.ANY)
    wide = jax.ShapeDtypeStruct((total, PAD), BF16)
    tall = jax.ShapeDtypeStruct((PAD, total), BF16)
    shapes = [wide, wide, wide, tall, tall, jax.ShapeDtypeStruct((total, width), BF16)]
    scratch = [pltpu.VMEM((4, rows, width), BF16)]
    arguments, extra = [tokens, gain[None], angles, pack], []
    if columns:
        shapes.append(jax.ShapeDtypeStruct((width, 4 * PAD), BF16))
        scratch.append(pltpu.VMEM((8, *pack.shape), BF16))
        arguments.append(given)
        extra.append(jax.ShapeDtypeStruct(given.shape, BF16))
    out = pl.pallas_call(
        functools.partial(project_kernel, columns),
        in_specs=[vmem] * 4 + [anywhere] * len(extra),
        out_specs=[vmem] * len(shapes) + [anywhere] * len(extra),
        out_shape=shapes + extra,
        scratch_shapes=scratch
        + [pltpu.SemaphoreType.DMA((copies,)), pltpu.SemaphoreType.DMA((copies,))],
        compiler_params=pltpu.CompilerParams(
            collective_id=3, has_side_effects=True, vmem_limit_bytes=56 << 20
        ),
        cost_estimate=pl.CostEstimate(
            flops=6 * total * width * PAD, bytes_accessed=16 * total * width, transcendentals=0
        ),
    )(*arguments)
    return out if columns else [*out, pack, swap(given, "dp", 1)]


def head_mask(values, head):
    lane = lax.broadcasted_iota(jnp.int32, values.shape, 1)
    return jnp.where(lane // HEAD == head, values, jnp.zeros_like(values))


def seen(i, j, seg_row, par_row, seg_col):
    key_at = j * BLOCK + lax.broadcasted_iota(jnp.int32, (BLOCK, 1), 0)
    query_at = i * BLOCK + lax.broadcasted_iota(jnp.int32, (1, BLOCK), 1)
    related = (seg_col == seg_row) | (seg_col == par_row) | (seg_col == 0)
    return related & (key_at <= query_at)


def attend_block(heads, i, q_ref, k_ref, vt_ref, rowinfo_ref, colinfo_ref, o_ref, total_ref):
    here = pl.ds(pl.multiple_of(i * BLOCK, BLOCK), BLOCK)
    queries = q_ref[here, :]
    by_head = [head_mask(queries, h) for h in range(heads)]
    seg_row, par_row = rowinfo_ref[0:1, here], rowinfo_ref[1:2, here]

    def step(j, carry):
        at = pl.ds(pl.multiple_of(j * BLOCK, BLOCK), BLOCK)
        keys = k_ref[at, :]
        visible = seen(i, j, seg_row, par_row, colinfo_ref[at, 0:1])
        out = []
        for h in range(heads):
            top, total, mixed = carry[h]
            scores = jnp.where(visible, dot_nt(keys, by_head[h]), -1e30)
            new_top = jnp.maximum(top, jnp.max(scores, axis=0, keepdims=True))
            shrink = jnp.exp(top - new_top)
            probs = jnp.exp(scores - new_top)
            total = total * shrink + jnp.sum(probs, axis=0, keepdims=True)
            mixed = mixed * shrink + dot_nn(
                vt_ref[h * HEAD : (h + 1) * HEAD, at], probs.astype(BF16)
            )
            out.append((new_top, total, mixed))
        return tuple(out)

    start = tuple(
        (
            jnp.full((1, BLOCK), -1e30, F32),
            jnp.zeros((1, BLOCK), F32),
            jnp.zeros((HEAD, BLOCK), F32),
        )
        for _ in range(heads)
    )
    done = lax.fori_loop(0, i + 1, step, start)
    mixed = [m / t for _, t, m in done] + [jnp.zeros((PAD - heads * HEAD, BLOCK), F32)]
    o_ref[here, :] = jnp.concatenate(mixed, axis=0).T.astype(BF16)
    total_ref[:, here] = jnp.concatenate(
        [m + jnp.log(t) for m, t, _ in done] + [jnp.zeros((8 - heads, BLOCK), F32)], axis=0
    )


def other(place, bits):
    if bits & 2:
        place = place + 2 - 4 * lax.rem(lax.div(place, 2), 2)
    if bits & 1:
        place = place + 1 - 2 * lax.rem(place, 2)
    return place


def enter(columns=False):
    dp, tensor = lax.axis_index("dp"), lax.axis_index("tensor")
    others = [(dp, other(tensor, 1)), (dp, other(tensor, 2)), (other(dp, 1), tensor)]
    if columns:
        others += [(lax.rem(dp + 2 * j, 8), tensor) for j in (1, 2, 3)]
    barrier = pltpu.get_barrier_semaphore()
    for device in others:
        pl.semaphore_signal(barrier, inc=1, device_id=device, device_id_type=MESH)
    pl.semaphore_wait(barrier, len(others))
    return others


class Copies:
    def __init__(self, send_sems, recv_sems):
        self.send_sems, self.recv_sems, self.made = send_sems, recv_sems, []

    def start(self, source, target, device):
        k = len(self.made)
        copy = pltpu.make_async_remote_copy(
            src_ref=source,
            dst_ref=target,
            send_sem=self.send_sems.at[k],
            recv_sem=self.recv_sems.at[k],
            device_id=device,
            device_id_type=MESH,
        )
        copy.start()
        self.made.append(copy)
        return copy

    def finish(self):
        for copy in self.made:
            copy.wait_send()


def quarter(ref, bits, rows):
    place = other(lax.axis_index("tensor"), bits)
    return ref.at[pl.ds(pl.multiple_of(place * rows, rows), rows)]


def sum_of_quarters(part, copies, near, far, near_send, near_recv, far_send, far_recv):
    rows = far_send.shape[0]
    near_send[0] = part(3).astype(BF16)
    first = copies.start(near_send.at[0], near_recv.at[0], near)
    near_send[1] = part(1).astype(BF16)
    second = copies.start(near_send.at[1], near_recv.at[1], near)
    mine = part(2)
    first.wait_recv()
    far_send[...] = (mine + near_recv[0].astype(F32)).astype(BF16)
    moves = []
    for c in range(SLICES):
        at = pl.ds(c * rows // SLICES, rows // SLICES)
        moves.append(copies.start(far_send.at[at], far_recv.at[at], far))
    mine = part(0)
    second.wait_recv()
    return mine + near_recv[1].astype(F32), moves


class Spread:
    def __init__(self, copies, devices, target, rows):
        self.copies, (self.near, self.far, self.across) = copies, devices
        self.rows, self.own, self.beside = rows, quarter(target.at[0], 0, rows), quarter(target.at[1], 0, rows)
        self.over, self.corner = quarter(target.at[0], 2, rows), quarter(target.at[1], 2, rows)
        self.from_far, self.from_across, self.from_corner, self.ends = {}, {}, {}, []

    def send(self, source, at, c):
        copies = self.copies
        self.from_far[c] = copies.start(source.at[at], self.own.at[at], self.far)
        self.from_across[c] = copies.start(source.at[at], self.beside.at[at], self.across)
        self.ends.append(copies.start(source.at[at], self.own.at[at], self.near))

    def pass_on(self, c, at):
        copies = self.copies
        self.from_far[c].wait_recv()
        if c >= SLICES // 2:
            self.from_corner[c] = copies.start(self.over.at[at], self.corner.at[at], self.across)
        self.ends.append(copies.start(self.over.at[at], self.over.at[at], self.near))
        self.from_across[c].wait_recv()
        if c < SLICES // 2:
            self.from_corner[c] = copies.start(self.beside.at[at], self.beside.at[at], self.far)
        self.ends.append(copies.start(self.beside.at[at], self.beside.at[at], self.near))

    def pass_corner(self, c, at):
        self.from_corner[c].wait_recv()
        self.ends.append(self.copies.start(self.corner.at[at], self.corner.at[at], self.near))

    def finish(self):
        for copy in self.ends:
            copy.wait_recv()


def branch_kernel(
    heads, q_ref, k_ref, vt_ref, rowinfo_ref, colinfo_ref, cot_ref,
    out_ref, tok_ref, gain_ref, carried_ref, mix_ref, picked_ref,
    att_ref, total_ref, hidden_ref, aux_ref, rows_ref, cots_ref,
    near_send, near_recv, far_send, far_recv, own, send_sems, recv_sems, local_sems,
):
    devices = enter()
    near, far, _ = devices
    copies = Copies(send_sems, recv_sems)
    rows, width = tok_ref.shape
    weights = out_ref[:, 3 * PAD :]
    size = rows // SLICES
    slices = [pl.ds(c * size, size) for c in range(SLICES)]
    locals_ = [pltpu.make_async_copy(cot_ref, quarter(cots_ref.at[0], 0, rows), local_sems.at[0])]
    locals_[0].start()
    cots = Spread(copies, devices, cots_ref, rows)
    for c, at in enumerate(slices):
        cots.send(cot_ref, at, c)

    def part(bits):
        if bits == 0:
            for c, at in enumerate(slices):
                cots.pass_on(c, at)
        place = other(lax.axis_index("tensor"), bits)
        for block in range(rows // BLOCK):
            attend_block(
                heads, place * (rows // BLOCK) + block,
                q_ref, k_ref, vt_ref, rowinfo_ref, colinfo_ref, att_ref, total_ref,
            )
        return dot_nt(quarter(att_ref, bits, rows)[...], weights)

    mine, moves = sum_of_quarters(
        part, copies, near, far, near_send, near_recv, far_send, far_recv
    )
    hidden_ref[...] = tok_ref[...].astype(F32) + mine
    spread = Spread(copies, devices, rows_ref, rows)
    for c, at in enumerate(slices):
        moves[c].wait_recv()
        hidden = hidden_ref[at, :] + far_recv[at, :].astype(F32)
        hidden_ref[at, :] = hidden
        scale = lax.rsqrt(jnp.mean(hidden * hidden, axis=1, keepdims=True) + epsilon)
        normed_two = hidden * scale * gain_ref[...]
        logits = carried_ref[at, :] + lax.dot_general(
            normed_two,
            mix_ref[...],
            (((1,), (0,)), ((), ())),
            precision=HIGHEST,
            preferred_element_type=F32,
        )
        picked = picked_ref[at, :] > 0
        top = jnp.max(jnp.where(picked, logits, -1e30), axis=1, keepdims=True)
        weight = jnp.where(picked, jnp.exp(jnp.where(picked, logits - top, 0.0)), 0.0)
        gate = weight / jnp.sum(weight, axis=1, keepdims=True)
        lane = lax.broadcasted_iota(jnp.int32, logits.shape, 1)
        turned = jnp.where(
            lane % 2 == 0, pltpu.roll(logits, 127, 1), pltpu.roll(logits, 1, 1)
        )
        top = jnp.maximum(logits, turned)
        mixture = jnp.exp(logits - top) / (jnp.exp(logits - top) + jnp.exp(turned - top))
        aux_ref[at, :] = jnp.where(lane < MIX, gate, jnp.where(lane < MIX + 4, mixture, 0.0))
        own[at, :width] = normed_two.astype(BF16)
        own[at, width:] = jnp.where(lane < NF, gate, 0.0).astype(BF16)
        spread.send(own, at, c)
        local = pltpu.make_async_copy(
            own.at[at], quarter(rows_ref.at[0], 0, rows).at[at], local_sems.at[1 + c]
        )
        local.start()
        locals_.append(local)
    for c, at in enumerate(slices):
        cots.pass_corner(c, at)
    for c, at in enumerate(slices):
        spread.pass_on(c, at)
    for c, at in enumerate(slices):
        spread.pass_corner(c, at)
    cots.finish()
    spread.finish()
    for local in locals_:
        local.wait()
    copies.finish()


def branch(
    heads, queries, keys, values_t, rowinfo, colinfo, cotangent, head_full, tokens, gain, carried, mix,
    picked,
):
    rows, width = tokens.shape
    total = queries.shape[0]
    vmem, anywhere = pl.BlockSpec(memory_space=pltpu.VMEM), pl.BlockSpec(memory_space=pl.ANY)
    copies = 2 + 15 * SLICES
    return pl.pallas_call(
        functools.partial(branch_kernel, heads),
        in_specs=[vmem] * 12,
        out_specs=[vmem] * 4 + [anywhere] * 2,
        out_shape=[
            jax.ShapeDtypeStruct((total, PAD), BF16),
            jax.ShapeDtypeStruct((8, total), F32),
            jax.ShapeDtypeStruct((rows, width), F32),
            jax.ShapeDtypeStruct((rows, 128), F32),
            jax.ShapeDtypeStruct((2, total, width + 128), BF16),
            jax.ShapeDtypeStruct((2, total, width), BF16),
        ],
        scratch_shapes=[
            pltpu.VMEM((2, rows, width), BF16),
            pltpu.VMEM((2, rows, width), BF16),
            pltpu.VMEM((rows, width), BF16),
            pltpu.VMEM((rows, width), BF16),
            pltpu.VMEM((rows, width + 128), BF16),
            pltpu.SemaphoreType.DMA((copies,)),
            pltpu.SemaphoreType.DMA((copies,)),
            pltpu.SemaphoreType.DMA((1 + SLICES,)),
        ],
        compiler_params=pltpu.CompilerParams(
            collective_id=1, has_side_effects=True, vmem_limit_bytes=48 << 20
        ),
        cost_estimate=pl.CostEstimate(
            flops=64 * rows * width * PAD, bytes_accessed=64 * rows * width, transcendentals=0
        ),
    )(
        queries, keys, values_t, rowinfo, colinfo, cotangent, head_full, tokens, gain[None],
        carried, mix, picked,
    )


class PairSum:
    def __init__(self, copies, devices, source, refs, local_sems):
        self.copies, (self.near, self.far, self.across) = copies, devices
        self.source, self.local_sems = source, local_sems
        self.kept, self.near_recv, self.corner_send, self.corner_recv = refs[:4]
        self.far_send, self.far_recv, self.across_send, self.across_recv = refs[4:]
        self.rows = self.far_send.shape[0]
        half = self.rows // 2
        self.halves = [pl.ds(0, half), pl.ds(half, half)]
        self.arrivals, self.locals_, self.from_far, self.from_across = {}, {}, {}, {}

    @staticmethod
    def shapes(rows, wide):
        one, two = (rows, wide), (2, rows // 2, wide)
        return [
            pltpu.VMEM(shape, BF16)
            for shape in ((4, *one), (4, *one), one, two, one, one, one, one)
        ]

    def start(self):
        for b in (3, 1, 2, 0):
            tree, bits = self.source.at[b // 2], 2 * (b % 2)
            self.arrivals[b] = self.copies.start(
                quarter(tree, bits + 1, self.rows), self.near_recv.at[b], self.near
            )
            self.locals_[b] = pltpu.make_async_copy(
                quarter(tree, bits, self.rows), self.kept.at[b], self.local_sems.at[b]
            )
            self.locals_[b].start()

    def joined(self, b, at):
        return self.kept[b, at, :].astype(F32) + self.near_recv[b, at, :].astype(F32)

    def arrived(self, b):
        self.arrivals[b].wait_recv()
        self.locals_[b].wait()

    def first_round(self):
        low, high = self.halves
        self.arrived(3)
        self.corner_send[...] = self.joined(3, pl.ds(0, self.rows)).astype(BF16)
        start = self.copies.start
        self.corner_far = start(self.corner_send.at[low], self.corner_recv.at[0], self.far)
        self.corner_across = start(self.corner_send.at[high], self.corner_recv.at[1], self.across)
        self.arrived(1)
        self.far_send[low, :] = self.joined(1, low).astype(BF16)
        self.from_far[0] = start(self.far_send.at[low], self.far_recv.at[low], self.far)
        self.arrived(2)
        self.across_send[high, :] = self.joined(2, high).astype(BF16)
        self.from_across[1] = start(self.across_send.at[high], self.across_recv.at[high], self.across)

    def second_round(self):
        low, high = self.halves
        start = self.copies.start
        self.corner_far.wait_recv()
        self.across_send[low, :] = (
            self.joined(2, low) + self.corner_recv[0].astype(F32)
        ).astype(BF16)
        self.from_across[0] = start(self.across_send.at[low], self.across_recv.at[low], self.across)
        self.corner_across.wait_recv()
        self.far_send[high, :] = (
            self.joined(1, high) + self.corner_recv[1].astype(F32)
        ).astype(BF16)
        self.from_far[1] = start(self.far_send.at[high], self.far_recv.at[high], self.far)
        self.arrived(0)

    def total(self, h):
        self.from_far[h].wait_recv()
        self.from_across[h].wait_recv()
        at = self.halves[h]
        return (
            self.joined(0, at)
            + self.far_recv[at, :].astype(F32)
            + self.across_recv[at, :].astype(F32)
        )


def attend_back_block(
    heads, i, q_ref, g_ref, o_ref, k_ref, v_ref, kt_ref, rowinfo_ref, colinfo_ref, total_ref, angle_ref,
    grad_ref, key_sum, value_sum, query_sum,
):
    here = pl.ds(pl.multiple_of(i * BLOCK, BLOCK), BLOCK)
    query_sum[...] = jnp.zeros_like(query_sum)
    queries, grads = q_ref[here, :], g_ref[here, :]
    q_heads = [head_mask(queries, h) for h in range(heads)]
    g_heads = [head_mask(grads, h) for h in range(heads)]
    seg_row, par_row = rowinfo_ref[0:1, here], rowinfo_ref[1:2, here]
    product = grads.astype(F32) * o_ref[here, :].astype(F32)
    lane = lax.broadcasted_iota(jnp.int32, (8, PAD), 1)
    which = lax.broadcasted_iota(jnp.int32, (8, PAD), 0)
    delta = lax.dot_general(
        (lane // HEAD == which).astype(F32),
        product,
        (((1,), (1,)), ((), ())),
        precision=HIGHEST,
        preferred_element_type=F32,
    )
    totals = total_ref[:, here]

    def step(j, carry):
        at = pl.ds(pl.multiple_of(j * BLOCK, BLOCK), BLOCK)
        keys, values = k_ref[at, :], v_ref[at, :]
        visible = seen(i, j, seg_row, par_row, colinfo_ref[at, 0:1])
        key_part, value_part = key_sum[at, :], value_sum[at, :]
        for h in range(heads):
            scores = jnp.where(visible, dot_nt(keys, q_heads[h]), -1e30)
            probs = jnp.exp(scores - totals[h : h + 1, :])
            value_part = value_part + dot_nn(probs.astype(BF16), g_heads[h])
            grad_probs = dot_nt(values, g_heads[h])
            grad_scores = (probs * (grad_probs - delta[h : h + 1, :])).astype(BF16)
            key_part = key_part + dot_nn(grad_scores, q_heads[h])
            lanes = slice(h * HEAD, (h + 1) * HEAD)
            query_sum[lanes, :] += dot_nn(kt_ref[lanes, at], grad_scores)
        key_sum[at, :] = key_part
        value_sum[at, :] = value_part
        return carry

    lax.fori_loop(0, i + 1, step, 0)
    grad_ref[here, :PAD] = turned_back(query_sum[...].T * HEAD**-0.5, angle_ref[here, :])


def turned_back(values, angles):
    cosine, sine = rotation(angles)
    return (values * cosine - swap_halves(values) * sine).astype(BF16)


def branch_back_kernel(
    heads, hidden_ref, aux_ref, cot_ref, gain_ref, mix_ref, vector_ref, carried_ref, att_ref, out_ref,
    q_ref, k_ref, v_ref, kt_ref, rowinfo_ref, colinfo_ref, total_ref, angle_ref, sums_ref, grad_ins_ref,
    grad_hidden_ref, grad_logits_ref, grad_out_ref, small_ref, grad_ref, result_ref,
    normed_two, base, gathered, grad_att, key_sum, value_sum, query_sum,
    send_sems, recv_sems, local_sems, *buffers,
):
    devices = enter()
    near, far, _ = devices
    copies = Copies(send_sems, recv_sems)
    rows, width = hidden_ref.shape
    half = rows // 2
    halves = [pl.ds(0, half), pl.ds(half, half)]
    incoming = PairSum(copies, devices, grad_ins_ref, buffers[:8], local_sems.at[0])
    results = PairSum(copies, devices, sums_ref, buffers[8:], local_sems.at[1])
    incoming.start()
    key_sum[...] = jnp.zeros_like(key_sum)
    value_sum[...] = jnp.zeros_like(value_sum)

    gain = gain_ref[...]
    lane = lax.broadcasted_iota(jnp.int32, (half, 128), 1)

    def column(values, at):
        return jnp.sum(jnp.where(lane == at, values, 0.0), axis=1, keepdims=True)

    known = []
    for at in halves:
        hidden, aux, grads = hidden_ref[at, :], aux_ref[at, :], cot_ref[at, :].astype(F32)
        scale = lax.rsqrt(jnp.mean(hidden * hidden, axis=1, keepdims=True) + epsilon)
        normed = hidden * scale * gain
        normed_two[at, :] = normed
        gates = [column(aux, NF + 1 + k) for k in range(3)]
        mixes = [column(aux, MIX + k) for k in range(4)]
        along = jnp.sum(grads * normed, axis=1, keepdims=True)
        vectors = [
            jnp.sum(grads * vector_ref[c : c + 1, :], axis=1, keepdims=True) for c in range(2)
        ]
        kept = gates[0] + gates[1] * mixes[0] + gates[2] * mixes[2]
        base[at, :] = grads * kept
        sums = []
        for c in range(2):
            sums.append(
                jnp.sum(grads * (gates[1 + c] * mixes[2 * c + 1]), axis=0, keepdims=True)
            )
        by_gate = jnp.where(lane == NF + 1, along, 0.0)
        by_mix = jnp.zeros((half, 128), F32)
        for c in range(2):
            first, second = mixes[2 * c], mixes[2 * c + 1]
            by_gate = by_gate + jnp.where(
                lane == NF + 2 + c, first * along + second * vectors[c], 0.0
            )
            d_first, d_second = gates[1 + c] * along, gates[1 + c] * vectors[c]
            inner = first * d_first + second * d_second
            by_mix = by_mix + jnp.where(lane == MIX + 2 * c, first * (d_first - inner), 0.0)
            by_mix = by_mix + jnp.where(lane == MIX + 2 * c + 1, second * (d_second - inner), 0.0)
        known.append((scale, by_gate, by_mix, sums))
    incoming.first_round()
    incoming.second_round()

    gain_sum = jnp.zeros((1, width), F32)
    far_moves, near_moves = [], []
    for h, at in enumerate(halves):
        scale, by_gate, by_mix, _ = known[h]
        arriving = incoming.total(h)
        by_gate = by_gate + jnp.where(lane < NF, arriving[:, width:], 0.0)
        gates = jnp.where(lane < MIX, aux_ref[at, :], 0.0)
        grad_logits = by_mix + gates * (
            by_gate - jnp.sum(gates * by_gate, axis=1, keepdims=True)
        )
        grad_logits_ref[at, :] = grad_logits
        grad_normed = arriving[:, :width] + base[at, :] + lax.dot_general(
            grad_logits,
            mix_ref[...],
            (((1,), (1,)), ((), ())),
            precision=HIGHEST,
            preferred_element_type=F32,
        )
        hidden = hidden_ref[at, :]
        gain_sum = gain_sum + jnp.sum(hidden * scale * grad_normed, axis=0, keepdims=True)
        weighted = gain * grad_normed
        inner = jnp.mean(hidden * weighted, axis=1, keepdims=True)
        grad_hidden = (
            cot_ref[at, :].astype(F32) + scale * weighted - hidden * (scale * scale * scale * inner)
        )
        grad_hidden_ref[at, :] = grad_hidden
        gathered[0, at, :] = grad_hidden.astype(BF16)
        far_moves.append(copies.start(gathered.at[0, at], gathered.at[2, at], far))
        near_moves.append(copies.start(gathered.at[0, at], gathered.at[1, at], near))
    results.start()

    def over_tokens(a, b):
        return lax.dot_general(
            a, b, (((0,), (0,)), ((), ())), precision=HIGHEST, preferred_element_type=F32
        )

    small_ref[...] = jnp.zeros_like(small_ref)
    small_ref[:16, :width] = over_tokens(grad_logits_ref[...], normed_two[...])[:16]
    small_ref[16:, :width] = jnp.concatenate(
        [gain_sum] + [known[0][3][c] + known[1][3][c] for c in range(2)]
        + [jnp.zeros((5, width), F32)],
        axis=0,
    )
    small_ref[:16, width:] = over_tokens(carried_ref[...], grad_logits_ref[...])[:16]

    def attention_back(bits):
        values = gathered[bits]
        quarter(grad_att, bits, rows)[...] = dot_nn(values, out_ref[:, 3 * PAD :]).astype(BF16)
        product = dot_tn(values, quarter(att_ref, bits, rows)[...])
        grad_out_ref[...] = grad_out_ref[...] + product if bits else product
        place = other(lax.axis_index("tensor"), bits)
        for block in range(rows // BLOCK):
            attend_back_block(
                heads, place * (rows // BLOCK) + block, q_ref, grad_att, att_ref, k_ref, v_ref, kt_ref,
                rowinfo_ref, colinfo_ref, total_ref, angle_ref, grad_ref, key_sum, value_sum, query_sum,
            )

    attention_back(0)
    results.first_round()
    for move in near_moves:
        move.wait_recv()
    last = []
    for h, at in enumerate(halves):
        far_moves[h].wait_recv()
        last.append(copies.start(gathered.at[2, at], gathered.at[3, at], near))
    attention_back(1)
    results.second_round()
    attention_back(2)
    for move in last:
        move.wait_recv()
    attention_back(3)
    for h, at in enumerate(halves):
        aux = aux_ref[at, :]
        gates = [column(aux, NF + 1 + k) for k in range(3)]
        mixes = [column(aux, MIX + k) for k in range(4)]
        kept = gates[0] + gates[1] * mixes[0] + gates[2] * mixes[2]
        result = hidden_ref[at, :] + kept * normed_two[at, :] + results.total(h)
        for c in range(2):
            result = result + (gates[1 + c] * mixes[2 * c + 1]) * vector_ref[c : c + 1, :]
        result_ref[at, :] = result.astype(BF16)

    def finish_keys(j, carry):
        at = pl.ds(pl.multiple_of(j * BLOCK, BLOCK), BLOCK)
        grad_ref[at, PAD : 2 * PAD] = turned_back(key_sum[at, :], angle_ref[at, :])
        grad_ref[at, 2 * PAD :] = value_sum[at, :].astype(BF16)
        return carry

    lax.fori_loop(0, grad_ref.shape[0] // BLOCK, finish_keys, 0)
    copies.finish()


def branch_back(
    heads, hidden, aux, cotangent, gain, mix, vectors, carried, attended, head_full, queries, keys, values,
    keys_t, rowinfo, colinfo, totals, angles, sums, grad_ins,
):
    rows, width = hidden.shape
    total = queries.shape[0]
    vmem, anywhere = pl.BlockSpec(memory_space=pltpu.VMEM), pl.BlockSpec(memory_space=pl.ANY)
    copies = 2 * 10 + 6
    return pl.pallas_call(
        functools.partial(branch_back_kernel, heads),
        in_specs=[vmem] * 17 + [anywhere] * 2,
        out_specs=[vmem] * 6,
        out_shape=[
            jax.ShapeDtypeStruct((rows, width), F32),
            jax.ShapeDtypeStruct((rows, 128), F32),
            jax.ShapeDtypeStruct((width, PAD), F32),
            jax.ShapeDtypeStruct((24, width + 128), F32),
            jax.ShapeDtypeStruct((total, 3 * PAD), BF16),
            jax.ShapeDtypeStruct((rows, width), BF16),
        ],
        scratch_shapes=[
            pltpu.VMEM((rows, width), F32),
            pltpu.VMEM((rows, width), F32),
            pltpu.VMEM((4, rows, width), BF16),
            pltpu.VMEM((total, PAD), BF16),
            pltpu.VMEM((total, PAD), F32),
            pltpu.VMEM((total, PAD), F32),
            pltpu.VMEM((PAD, BLOCK), F32),
            pltpu.SemaphoreType.DMA((copies,)),
            pltpu.SemaphoreType.DMA((copies,)),
            pltpu.SemaphoreType.DMA((2, 4)),
        ]
        + PairSum.shapes(rows, grad_ins.shape[2])
        + PairSum.shapes(rows, width),
        compiler_params=pltpu.CompilerParams(
            collective_id=2, has_side_effects=True, vmem_limit_bytes=61 << 20
        ),
        cost_estimate=pl.CostEstimate(
            flops=256 * rows * width * PAD, bytes_accessed=64 * rows * width, transcendentals=0
        ),
    )(
        hidden, aux, cotangent, gain[None], mix, vectors, carried, attended, head_full,
        queries, keys, values, keys_t, rowinfo, colinfo, totals, angles, sums, grad_ins,
    )


def finish_kernel(
    columns, grad_ref, one_ref, head_ref, grad_out_ref, small_ref, grad_hidden_ref, tok_ref, gain_ref,
    *refs
):
    if columns:
        given_ref, received_ref, refs = refs[0], refs[4], refs[1:4] + refs[5:]
    grad_tok_ref, pack_ref, sum_ref, refs = refs[0], refs[1], refs[2], refs[3:]
    near_send, near_recv, far_send, far_recv, send_sems, recv_sems = refs[:6]
    near, far, across, *column = enter(columns)
    copies = Copies(send_sems, recv_sems)
    dp = lax.axis_index("dp")
    rows, width = tok_ref.shape
    share = width // 8

    def part(bits):
        return dot_nt(quarter(grad_ref, bits, rows)[...], head_ref[:, : 3 * PAD])

    mine, moves = sum_of_quarters(
        part, copies, near, far, near_send, near_recv, far_send, far_recv
    )
    grad_tok_ref[...] = mine

    packed = refs[6] if columns else pack_ref
    products = refs[-1]
    products[...] = dot_tn(one_ref[...], grad_ref[...])
    along = jnp.zeros((8, width), F32)
    rest = None
    for section in range(4):
        at = slice(section * PAD, (section + 1) * PAD)
        if section < 3:
            grad = products[:, at]
            along = along + lax.dot_general(
                jnp.ones((8, PAD), F32),
                grad * head_ref[:, at].astype(F32),
                (((1,), (1,)), ((), ())),
                precision=HIGHEST,
                preferred_element_type=F32,
            )
        else:
            grad = grad_out_ref[...]
        if not columns:
            packed[:, at] = grad.astype(BF16)
            continue
        low, high = grad[:, :128].astype(BF16), grad[:, 128:]
        if section % 2 == 0:
            rest = high
        else:
            lane = lax.broadcasted_iota(jnp.int32, high.shape, 1)
            rest = jnp.where(lane < 64, rest, pltpu.roll(high, 64, 1)).astype(BF16)
        for d in range(8):
            cut = slice(d * share, (d + 1) * share)
            packed[d, :, section * 128 : (section + 1) * 128] = low[cut]
            if section % 2:
                start = 512 + 128 * (section // 2)
                packed[d, :, start : start + 128] = rest[cut]
    small = small_ref[...]
    row = lax.broadcasted_iota(jnp.int32, (24, width), 0)
    small = jnp.concatenate(
        [
            jnp.where(row == 19, along[:1] / gain_ref[...], small[:, :width]),
            small[:, width:],
        ],
        axis=1,
    )
    if columns:
        _, pair_recv, column_send, column_recv, sums, sum_recv = refs[6:-1]
        pair_moves = []
        for j in range(4):
            there = lax.rem(other(dp, 1) + 2 * j, 8)
            pair_moves.append(copies.start(packed.at[there], pair_recv.at[j], across))
        sums[0] = small
        steps = [near, far, across, (other(dp, 2), lax.axis_index("tensor")), column[1]]
        sum_moves = [copies.start(sums.at[0], sum_recv.at[0], steps[0])]

        def add_up():
            k = len(sum_moves)
            sum_moves[-1].wait_recv()
            if k < 5:
                sums[k] = sums[k - 1] + sum_recv[k - 1]
                sum_moves.append(copies.start(sums.at[k], sum_recv.at[k], steps[k]))
            else:
                sum_ref[...] = sums[4] + sum_recv[4]

        add_up()
        add_up()
        column_moves = []
        for j in (1, 2, 3, 0):
            pair_moves[j].wait_recv()
            paired = packed[lax.rem(dp + 2 * j, 8)].astype(F32) + pair_recv[j].astype(F32)
            if j:
                column_send[j - 1] = paired.astype(BF16)
                column_moves.append(
                    copies.start(column_send.at[j - 1], column_recv.at[j - 1], column[j - 1])
                )
            else:
                pack_ref[...] = paired
        beside = copies.start(given_ref.at[1 - lax.rem(dp, 2)], received_ref, across)
        add_up()
    else:
        sum_ref[...] = small

    size = rows // SLICES
    for c in range(SLICES):
        at = pl.ds(c * size, size)
        moves[c].wait_recv()
        grad_normed = grad_tok_ref[at, :] + far_recv[at, :].astype(F32)
        values = tok_ref[at, :].astype(F32)
        scale = lax.rsqrt(jnp.mean(values * values, axis=1, keepdims=True) + epsilon)
        weighted = gain_ref[...] * grad_normed
        inner = jnp.mean(values * weighted, axis=1, keepdims=True)
        grad_tok_ref[at, :] = (
            grad_hidden_ref[at, :] + scale * weighted - values * (scale * scale * scale * inner)
        )
    if columns:
        add_up()
        for j in range(3):
            column_moves[j].wait_recv()
            pack_ref[...] = pack_ref[...] + column_recv[j].astype(F32)
        add_up()
        beside.wait_recv()
    copies.finish()


def finish(columns, grads, ones, head_full, grad_out, small, grad_hidden, tokens, gain, given):
    rows, width = tokens.shape
    share = width // 8
    vmem = pl.BlockSpec(memory_space=pltpu.VMEM)
    copies = 2 + SLICES + 13
    anywhere = pl.BlockSpec(memory_space=pl.ANY)
    pack = (
        jax.ShapeDtypeStruct((share, width), F32)
        if columns
        else jax.ShapeDtypeStruct(head_full.shape, BF16)
    )
    scratch = [
        pltpu.VMEM((2, rows, width), BF16),
        pltpu.VMEM((2, rows, width), BF16),
        pltpu.VMEM((rows, width), BF16),
        pltpu.VMEM((rows, width), BF16),
        pltpu.SemaphoreType.DMA((copies,)),
        pltpu.SemaphoreType.DMA((copies,)),
    ]
    if columns:
        scratch += [
            pltpu.VMEM((8, share, width), BF16),
            pltpu.VMEM((4, share, width), BF16),
            pltpu.VMEM((3, share, width), BF16),
            pltpu.VMEM((3, share, width), BF16),
            pltpu.VMEM((5, *small.shape), F32),
            pltpu.VMEM((5, *small.shape), F32),
        ]
    scratch.append(pltpu.VMEM((width, 3 * PAD), F32))
    extra = [given] if columns else []
    out = pl.pallas_call(
        functools.partial(finish_kernel, columns),
        in_specs=[vmem] * 8 + [anywhere] * len(extra),
        out_specs=[vmem] * 3 + [anywhere] * len(extra),
        out_shape=[
            jax.ShapeDtypeStruct((rows, width), F32),
            pack,
            jax.ShapeDtypeStruct(small.shape, F32),
        ]
        + [jax.ShapeDtypeStruct(a.shape[1:], a.dtype) for a in extra],
        scratch_shapes=scratch,
        compiler_params=pltpu.CompilerParams(
            collective_id=4, has_side_effects=True, vmem_limit_bytes=56 << 20
        ),
        cost_estimate=pl.CostEstimate(
            flops=32 * rows * width * PAD, bytes_accessed=64 * rows * width, transcendentals=0
        ),
    )(grads, ones, head_full, grad_out, small, grad_hidden, tokens, gain[None], *extra)
    if columns:
        return out
    there = 1 - lax.axis_index("dp") % 2
    return [*out, swap(lax.dynamic_index_in_dim(given, there, 0, keepdims=False), "dp", 1)]


def route_kernel(routes_ref, rows_ref, cols_ref, info_ref):
    tokens = routes_ref.shape[2]
    expert = lax.broadcasted_iota(jnp.int32, (NF, tokens), 0)
    step = 256
    down = lax.broadcasted_iota(jnp.int32, (step, step), 0)
    across = lax.broadcasted_iota(jnp.int32, (step, step), 1)
    before = jnp.where(down < across, 1.0, 0.0).astype(BF16)
    for a in range(2):
        hot = (expert == routes_ref[a, 0:1, :]) | (expert == routes_ref[a, 1:2, :])
        ones = jnp.where(hot, 1.0, 0.0)
        ranks, so_far = [], jnp.zeros((NF, 1), F32)
        for b in range(tokens // step):
            part = ones[:, b * step : (b + 1) * step]
            ranks.append(dot_nn(part.astype(BF16), before) + so_far)
            so_far = so_far + jnp.sum(part, axis=1, keepdims=True)
        rank = jnp.concatenate(ranks, axis=1)
        slots = jnp.where(hot, rank, -1.0)
        rows_ref[a] = slots.astype(jnp.int32)
        spread = jnp.concatenate([slots, jnp.zeros((128 - NF, tokens), F32)], axis=0)
        cols_ref[a] = spread.T.astype(jnp.int32)
        lane = lax.broadcasted_iota(jnp.int32, (NF, 128), 1)
        info = jnp.where(lane == 0, so_far, 0.0)
        for c in range(2):
            first = jnp.sum(jnp.where(rank + ones <= c * TILE, 1.0, 0.0), axis=1, keepdims=True)
            after = jnp.sum(jnp.where(rank < (c + 1) * TILE, 1.0, 0.0), axis=1, keepdims=True)
            info = jnp.where(lane == 1 + 2 * c, first, jnp.where(lane == 2 + 2 * c, after, info))
        info_ref[a] = info.astype(jnp.int32)


def route(routes):
    tokens = routes.shape[2]
    return pl.pallas_call(
        route_kernel,
        out_shape=[
            jax.ShapeDtypeStruct((2, NF, tokens), jnp.int32),
            jax.ShapeDtypeStruct((2, tokens, 128), jnp.int32),
            jax.ShapeDtypeStruct((2, NF, 128), jnp.int32),
        ],
        cost_estimate=pl.CostEstimate(flops=10**7, bytes_accessed=10**6, transcendentals=0),
    )(routes)


def experts_kernel(
    whole_weights, n_before, base_ref, info_ref, slot_rows_ref, slot_cols_ref, weights_ref, *refs
):
    (rows_in, grads_in), before, refs = refs[:2], refs[2 : 2 + n_before], refs[2 + n_before :]
    sums_out, grad_ins_out, out_ref, rows, grads, sums, grad_ins = refs[:7]
    weight, row_acc, grad_acc, slot_col, inputs, grad_outs, acts, gates, ups, in_sems, out_sems = refs[7:]
    step = pl.program_id(0)
    expert = base_ref[0] + step
    tokens, width = grads.shape[1:]
    wide = rows.shape[2]
    arrivals = [
        [pltpu.make_async_copy(rows_in.at[a], rows.at[a], in_sems.at[a, 0]),
         pltpu.make_async_copy(grads_in.at[a], grads.at[a], in_sems.at[a, 1])]
        + [pltpu.make_async_copy(source.at[a], target.at[a], in_sems.at[a, 2 + k])
           for k, (source, target) in enumerate(zip(before, (sums, grad_ins)))]
        for a in range(2)
    ]
    leaving = [
        [pltpu.make_async_copy(source.at[a], target.at[a], out_sems.at[a, k])
         for k, (source, target) in enumerate(((sums, sums_out), (grad_ins, grad_ins_out)))]
        for a in range(2)
    ]

    @pl.when(step == 0)
    def _():
        for copy in arrivals[0] + arrivals[1]:
            copy.start()
        if not n_before:
            sums[...] = jnp.zeros_like(sums)
            grad_ins[...] = jnp.zeros_like(grad_ins)

    if whole_weights:
        weight[...] = weights_ref[0]
    else:
        depth, _, _, _, share, _ = weights_ref.shape
        for z in range(depth):
            for y in range(2):
                weight[:, pl.ds((2 * z + y) * share, share), :] = weights_ref[z, y, 0]

    def tree(a):
        def dispatch(c, start, count):
            down = c * TILE + lax.broadcasted_iota(jnp.int32, (TILE, 1), 0)
            at = pl.ds(start, count)
            picked = slot_rows_ref[a, pl.ds(expert, 1), at] == down
            picked = jnp.where(picked, 1.0, 0.0).astype(BF16)
            row_acc[...] = dot_nn(picked, rows[a, at, :])
            grad_acc[...] = dot_nn(picked, grads[a, at, :])

        slot_col[...] = pltpu.roll(slot_cols_ref[a], 128 - expert, 1)

        def combine(c, start, count, back):
            across = c * TILE + lax.broadcasted_iota(jnp.int32, (1, TILE), 1)
            size = 256
            for b in range(count // size):
                at = pl.ds(pl.multiple_of(start + b * size, 128), size)
                here = jnp.where(slot_col[at, 0:1] == across, 1.0, 0.0).astype(BF16)
                part = dot_nn(here, back)
                sums[a, at, :] = (sums[a, at, :].astype(F32) + part[:, :width]).astype(BF16)
                grad_ins[a, at, :] = (
                    grad_ins[a, at, :].astype(F32) + part[:, width:]
                ).astype(BF16)

        def tile(c, carry):
            k = 8 * a + expert
            first, after = info_ref[k, 1 + 2 * c], info_ref[k, 2 + 2 * c]
            start = pl.multiple_of(jnp.minimum(first // 128 * 128, tokens - WINDOW), 128)
            narrow = after <= start + WINDOW

            @pl.when(narrow)
            def _():
                dispatch(c, start, WINDOW)

            @pl.when(jnp.logical_not(narrow))
            def _():
                dispatch(c, 0, tokens)

            at = pl.ds(pl.multiple_of((2 * a + c) * TILE, TILE), TILE)
            inputs[at, :] = row_acc[:, :width].astype(BF16)
            lane = lax.broadcasted_iota(jnp.int32, (TILE, wide - width), 1)
            gate = jnp.sum(
                jnp.where(lane == expert, row_acc[:, width:], 0.0), axis=1, keepdims=True
            )
            grad_out = (gate * grad_acc[...]).astype(BF16)
            grad_outs[at, :] = grad_out
            gate_part = dot_nn(inputs[at, :], weight[0])
            up_part = dot_nn(inputs[at, :], weight[1])
            sigmoid = 1.0 / (1.0 + jnp.exp(-gate_part))
            swish = gate_part * sigmoid
            act = (swish * up_part).astype(BF16)
            acts[at, :] = act
            expert_out = dot_nt(act, weight[2])
            along = jnp.sum(expert_out * grad_acc[...], axis=1, keepdims=True)
            grad_act = dot_nn(grad_out, weight[2])
            grad_gate = (
                grad_act * up_part * sigmoid * (1.0 + gate_part * (1.0 - sigmoid))
            ).astype(BF16)
            grad_up = (grad_act * swish).astype(BF16)
            gates[at, :] = grad_gate
            ups[at, :] = grad_up
            grad_in = dot_nt(grad_gate, weight[0]) + dot_nt(grad_up, weight[1])
            back = jnp.concatenate(
                [
                    (gate * expert_out).astype(BF16),
                    grad_in.astype(BF16),
                    jnp.where(lane == expert, along, 0.0).astype(BF16),
                ],
                axis=1,
            )

            @pl.when(narrow)
            def _():
                combine(c, start, WINDOW, back)

            @pl.when(jnp.logical_not(narrow))
            def _():
                combine(c, 0, tokens, back)

            return carry

        tiles = (info_ref[8 * a + expert, 0] + TILE - 1) // TILE

        def empty(c, carry):
            at = pl.ds(pl.multiple_of((2 * a + c) * TILE, TILE), TILE)
            for ref in (inputs, grad_outs, acts, gates, ups):
                ref[at, :] = jnp.zeros((TILE, ref.shape[1]), BF16)
            return carry

        lax.fori_loop(0, tiles, tile, 0)
        lax.fori_loop(tiles, 2, empty, 0)

    def one_tree(a, carry):
        for k in range(2):

            @pl.when(jnp.logical_and(step == 0, a == k))
            def _(k=k):
                for copy in arrivals[k]:
                    copy.wait()

        tree(a)
        for k in range(2):

            @pl.when(jnp.logical_and(step == pl.num_programs(0) - 1, a == k))
            def _(k=k):
                for copy in leaving[k]:
                    copy.start()

        return carry

    lax.fori_loop(0, 2, one_tree, 0)

    for k, (left, right) in enumerate(((inputs, gates), (inputs, ups), (grad_outs, acts))):
        size = 256
        for b in range(width // size):
            at = slice(b * size, (b + 1) * size)
            if whole_weights:
                out_ref[0, k, at, :] = dot_tn(left[:, at], right[...]).astype(BF16)
            else:
                weight[k, at, :] = dot_tn(left[:, at], right[...]).astype(BF16)
    if not whole_weights:
        for z in range(depth):
            for y in range(2):
                out_ref[z, y, 0] = weight[:, pl.ds((2 * z + y) * share, share), :]

    @pl.when(step == pl.num_programs(0) - 1)
    def _():
        for copy in leaving[0] + leaving[1]:
            copy.wait()


def experts(base, weights, info, rows, grads, slot_rows, slot_cols, before):
    _, tokens, width = grads.shape
    wide = rows.shape[2]
    whole_weights = weights.ndim == 4
    kinds, share, hidden = weights.shape[-3:]
    group = weights.shape[0] if whole_weights else weights.shape[2]
    depth = width if whole_weights else 2 * weights.shape[0] * share
    whole = lambda a: pl.BlockSpec(a.shape, lambda e, *_: (0,) * a.ndim, pipeline_mode=pl.Buffered(1))
    anywhere = pl.BlockSpec(memory_space=pl.ANY)
    if whole_weights:
        weight_spec = pl.BlockSpec((1, kinds, share, hidden), lambda e, *_: (e, 0, 0, 0))
    else:
        weight_spec = pl.BlockSpec(
            (weights.shape[0], 2, 1, kinds, share, hidden), lambda e, *_: (0, 0, e, 0, 0, 0)
        )
    sums = jax.ShapeDtypeStruct((2, tokens, width), BF16)
    grad_ins = jax.ShapeDtypeStruct((2, tokens, wide), BF16)
    return pl.pallas_call(
        functools.partial(experts_kernel, whole_weights, len(before)),
        grid_spec=pltpu.PrefetchScalarGridSpec(
            num_scalar_prefetch=2,
            grid=(group,),
            in_specs=[whole(slot_rows), whole(slot_cols), weight_spec]
            + [anywhere] * (2 + len(before)),
            out_specs=[anywhere, anywhere, weight_spec],
            scratch_shapes=[
                pltpu.VMEM((2, tokens, wide), BF16),
                pltpu.VMEM((2, tokens, width), BF16),
                pltpu.VMEM((2, tokens, width), BF16),
                pltpu.VMEM((2, tokens, wide), BF16),
                pltpu.VMEM((kinds, depth, hidden), BF16),
                pltpu.VMEM((TILE, wide), F32),
                pltpu.VMEM((TILE, width), F32),
                pltpu.VMEM((tokens, 128), jnp.int32),
                pltpu.VMEM((4 * TILE, width), BF16),
                pltpu.VMEM((4 * TILE, width), BF16),
                pltpu.VMEM((4 * TILE, hidden), BF16),
                pltpu.VMEM((4 * TILE, hidden), BF16),
                pltpu.VMEM((4 * TILE, hidden), BF16),
                pltpu.SemaphoreType.DMA((2, 4)),
                pltpu.SemaphoreType.DMA((2, 2)),
            ],
        ),
        out_shape=[sums, grad_ins, jax.ShapeDtypeStruct(weights.shape, BF16)],
        compiler_params=pltpu.CompilerParams(vmem_limit_bytes=60 << 20),
        cost_estimate=pl.CostEstimate(
            flops=group * tokens * width * (9 * hidden + 4 * tokens),
            bytes_accessed=16 * tokens * width,
            transcendentals=0,
        ),
    )(base, info, slot_rows, slot_cols, weights, rows, grads, *before)


def per_device(
    tokens_in,
    carried_logits,
    cotangent,
    segment_ids,
    parent_ids,
    routes,
    attention_gain,
    head_weight,
    output_weight,
    expert_gain,
    router_weight,
    carry_weight,
    constant_gate,
    constant_vector,
    expert_first,
    expert_second,
):
    row_count, width = tokens_in.shape
    tree_len = segment_ids.shape[0]
    head_width = head_weight.shape[2]
    heads = head_width // HEAD
    share = head_weight.shape[1]
    parity = lax.axis_index("dp") % 2
    index = lax.axis_index("tensor")
    own_experts = NF // 2
    group = own_experts // GROUPS
    layered = share % 16 == 0

    columns = lax.axis_size("dp") == 8

    def gather_experts(shards):
        gathered = gather_column(shards)
        if layered:
            return gathered
        return gathered.transpose(2, 3, 0, 1, 4, 5).reshape(group, 3, width, -1)

    sections = jnp.concatenate([head_weight, output_weight.T[None]], axis=0).astype(BF16)
    spread = lambda a, to: jnp.pad(a, ((0, 0), (0, to - a.shape[1])))
    if columns:
        pack = jnp.concatenate(
            [sections[k, :, :128] for k in range(4)] + [sections[k, :, 128:] for k in range(4)], axis=1
        )
    else:
        pack = jnp.concatenate([spread(sections[k], PAD) for k in range(4)], axis=1)
        pack = gather_column(pack)
        pack = jnp.moveaxis(by_parity(pack, swap(pack, "dp", 1)), 0, 1).reshape(width, 4 * PAD)
    expert_pack = jnp.concatenate(
        [expert_first.astype(BF16), expert_second.astype(BF16).transpose(0, 2, 1)[:, None]], axis=1
    )
    kept = lax.dynamic_slice_in_dim(expert_pack, parity * own_experts, own_experts, 0)
    given = lax.dynamic_slice_in_dim(expert_pack, (1 - parity) * own_experts, own_experts, 0)
    cut = lambda a, g: a[g * group : (g + 1) * group]
    shards = by_parity(cut(kept, 0), swap(cut(given, 0), "dp", 1))

    angles, routes_there = together(
        rotary_angles(segment_ids, parent_ids), swap(routes.T, "dp", 1)
    )
    slot_rows, slot_cols, info = route(jnp.stack([routes.T, routes_there]))
    info = info.reshape(2 * NF, -1)[:, :8]
    rowinfo = jnp.pad(jnp.stack([segment_ids, parent_ids]), ((0, 6), (0, 0)))
    colinfo = rowinfo.T
    local_routes = lax.dynamic_slice_in_dim(routes, index * row_count, row_count, 0)
    picked = jnp.sum(
        (local_routes[:, :, None] == jnp.arange(128, dtype=jnp.int32)).astype(F32), axis=1
    )
    carried_part = spread(jnp.dot(carried_logits, carry_weight, precision=HIGHEST), 128)
    mix_weight = spread(jnp.concatenate([spread(router_weight, MIX), constant_gate], axis=1), 128)
    vectors = jnp.pad(constant_vector, ((0, 6), (0, 0)))
    (
        pack, shards, slot_rows, slot_cols, info, rowinfo, colinfo, picked, carried_part, mix_weight,
        vectors,
    ) = together(
        pack, shards, slot_rows, slot_cols, info, rowinfo, colinfo, picked, carried_part, mix_weight,
        vectors,
    )
    expert_weights = [gather_experts(shards)]

    queries, keys, values, keys_t, values_t, gathered_one, head_full, received = project(
        columns, tokens_in, attention_gain, angles, pack, given[group:]
    )
    for g in range(1, GROUPS):
        shards = by_parity(cut(kept, g), cut(received, g - 1))
        queries, shards = together(queries, shards)
        expert_weights.append(gather_experts(shards))
    attended, totals, hidden, aux, expert_rows, grad_rows = branch(
        heads, queries, keys, values_t, rowinfo, colinfo, cotangent, head_full, tokens_in, expert_gain,
        carried_part, mix_weight, picked,
    )

    parts, own_grads = [], []
    for g in range(GROUPS):
        base = (parity * own_experts + g * group).astype(jnp.int32).reshape(1)
        *parts, weight_grads = experts(
            base, expert_weights[g], info, expert_rows, grad_rows, slot_rows, slot_cols, parts
        )
        if not layered:
            weight_grads = weight_grads.reshape(group, 3, -1, 2, share, weight_grads.shape[-1])
            weight_grads = weight_grads.transpose(2, 3, 0, 1, 4, 5)
        own_grads.append(scatter_column(weight_grads))
    sums, grad_ins = parts

    grad_hidden, grad_logits, grad_output_t, small, grad_projected, output = branch_back(
        heads, hidden, aux, cotangent, expert_gain, mix_weight, vectors, spread(carried_logits, 128),
        attended, head_full, queries, keys, values, keys_t, rowinfo, colinfo, totals, angles, sums,
        grad_ins,
    )
    mine = lambda a: lax.dynamic_index_in_dim(a, parity, 0, keepdims=False)
    theirs = lambda a: lax.dynamic_index_in_dim(a, 1 - parity, 0, keepdims=False)
    grad_projected, own_grads[0] = together(grad_projected, own_grads[0])
    grad_tokens, own_pack, small, received = finish(
        columns, grad_projected, gathered_one, head_full, grad_output_t, small, grad_hidden, tokens_in,
        attention_gain, own_grads[0],
    )
    grad_logits, own_pack = together(grad_logits, own_pack)
    grad_carried = lax.dot_general(
        grad_logits[:, :NE], carry_weight, (((1,), (1,)), ((), ())), precision=HIGHEST
    )
    if columns:
        own_sections = [
            jnp.concatenate(
                [own_pack[:, 128 * k : 128 * (k + 1)], own_pack[:, 512 + 64 * k : 576 + 64 * k]], axis=1
            )
            for k in range(4)
        ]
    else:
        blocks = own_pack.reshape(-1, 2, share, 4 * PAD)
        kept = lax.dynamic_index_in_dim(blocks, parity, 1, keepdims=False)
        given = lax.dynamic_index_in_dim(blocks, 1 - parity, 1, keepdims=False)
        paired = kept.astype(F32) + swap(given, "dp", 1).astype(F32)
        own_pack = scatter_column(paired.astype(BF16)).astype(F32)
        own_sections = [own_pack[:, k * PAD : k * PAD + head_width] for k in range(4)]
        small = lax.psum(small, ("dp", "tensor"))
    kept = jnp.concatenate([mine(a) for a in own_grads], axis=0)
    received = jnp.concatenate([received] + [swap(theirs(a), "dp", 1) for a in own_grads[1:]], axis=0)
    own_grads = by_parity(kept, received).reshape(NF, 3, share, -1).astype(F32)
    grad_first = own_grads[:, :2]
    grad_second = own_grads[:, 2].transpose(0, 2, 1)
    return (
        output,
        grad_tokens,
        grad_carried,
        small[19, :width],
        jnp.stack(own_sections[:3]),
        own_sections[3].T,
        small[16, :width],
        small[:NE, :width].T,
        small[:NE, width : width + NE],
        small[MIX : MIX + 4, :width].T,
        small[17:19, :width],
        grad_first,
        grad_second,
    )


def solution(mesh):
    in_specs = (
        P(("dp", "tensor"), None),
        P(("dp", "tensor"), None),
        P(("dp", "tensor"), None),
        P("dp"),
        P("dp"),
        P("dp", None),
        P(),
        P(None, "dp", "tensor"),
        P("tensor", "dp"),
        P(),
        P(),
        P(),
        P(),
        P(),
        P(None, None, "dp", "tensor"),
        P(None, "tensor", "dp"),
    )
    out_specs = (
        P(("dp", "tensor"), None),
        P(("dp", "tensor"), None),
        P(("dp", "tensor"), None),
        P(),
        P(None, "dp", "tensor"),
        P("tensor", "dp"),
        P(),
        P(),
        P(),
        P(),
        P(),
        P(None, None, "dp", "tensor"),
        P(None, "tensor", "dp"),
    )
    return jax.shard_map(
        per_device, mesh=mesh, in_specs=in_specs, out_specs=out_specs, check_vma=False
    )
```
